32 devices in a mesh: sp: 8 (over z, x), wa: 4 (over y, core).
Axes of the slice: x: 2, y: 2, z: 4, core: 2. Of those that a mesh axis runs over, the one named last changes fastest.
Arguments:
- fields_in: bfloat16 [2, 24, 180, 768], P(None, 'sp'), may hold values from -6 to 6
- norm1_gain: float32 [768], replicated, may hold values from 0.1 to 1.9
- norm1_shift: float32 [768], replicated, may hold values from -1.75 to 1.75
- spec_w1: bfloat16 [8, 2, 96, 96], P('wa'), may hold values from -0.4375 to 0.4375
- spec_b1: bfloat16 [8, 2, 96], P('wa'), may hold values from -0.625 to 0.625
- spec_w2: bfloat16 [8, 2, 96, 96], P('wa'), may hold values from -0.4375 to 0.4375
- spec_b2: bfloat16 [8, 2, 96], P('wa'), may hold values from -0.625 to 0.625
- norm2_gain: float32 [768], replicated, may hold values from 0.1 to 1.9
- norm2_shift: float32 [768], replicated, may hold values from -1.75 to 1.75
- fc1_weight: bfloat16 [768, 3072], P(None, 'wa'), may hold values from -0.21875 to 0.21875
- fc1_bias: bfloat16 [3072], P('wa'), may hold values from -1.75 to 1.75
- fc2_weight: bfloat16 [3072, 768], P('wa'), may hold values from -0.109375 to 0.109375
- fc2_bias: bfloat16 [768], replicated, may hold values from -1.75 to 1.75
- out_grad: bfloat16 [2, 24, 180, 768], P(None, 'sp'), may hold values from -6 to 6
Outputs:
- output: float32 [2, 24, 180, 768], P(None, 'sp')
- fields_grad: float32 [2, 24, 180, 768], P(None, 'sp')
- norm1_gain_grad: float32 [768], replicated
- norm1_shift_grad: float32 [768], replicated
- spec_w1_grad: float32 [8, 2, 96, 96], P('wa')
- spec_b1_grad: float32 [8, 2, 96], P('wa')
- spec_w2_grad: float32 [8, 2, 96, 96], P('wa')
- spec_b2_grad: float32 [8, 2, 96], P('wa')
- norm2_gain_grad: float32 [768], replicated
- norm2_shift_grad: float32 [768], replicated
- fc1_weight_grad: float32 [768, 3072], P(None, 'wa')
- fc1_bias_grad: float32 [3072], P('wa')
- fc2_weight_grad: float32 [3072, 768], P('wa')
- fc2_bias_grad: float32 [768], replicated
The draws below stay inside these ranges and needn't reach their ends.
All inputs are finite; a program needn't handle non-finite values.
Results may differ from the reference program's by a relative error of at most 0.024.
The reference program's roundings to bfloat16 on the way count: a program that leaves them out, or rounds other values in their place, can miss the bound.
Values may be sent and summed in bfloat16 or wider, within the bound.
A program may use at most 128 MiB of HBM per device.

```python
import math
from functools import partial
import jax
import jax.numpy as jnp
from jax import lax

BLOCKS = 8
BS = 96
D = 768
FF = 3072
W = 180
FIELDS = 2
H = 24
KW = 91


def block_scale(own_key, dims, pieces, smallest, high):
    level = 1.0
    for dim, shards_of in pieces:
        steps = jax.random.uniform(jax.random.fold_in(jax.random.fold_in(own_key, 6), dim), (shards_of,), jnp.float32, smallest / len(pieces), high / len(pieces))
        level = level * jnp.repeat(jnp.exp(steps), dims[dim] // shards_of).reshape((-1,) + (1,) * (len(dims) - 1 - dim))
    return level


def normal_values(rng, shape, scale, most, split=(), held_as=jnp.bfloat16):
    level = block_scale(rng, shape, split, -0.22, 0.18) if split else 1.0
    result = jax.random.normal(rng, shape, jnp.float32) * scale * level
    return jnp.minimum(jnp.maximum(result, -most), most).astype(held_as)


def setup_inputs(seed: int = 0) -> dict:
    streams_of = jax.random.split(jax.random.key(seed), 15)
    return {
        "fields_in": normal_values(streams_of[0], (FIELDS, H, W, D), 1.0, 6.0, ((1, 8),)),
        "norm1_gain": jnp.clip(1.0 + 0.18 * jax.random.normal(streams_of[1], (D,), jnp.float32), 0.1, 1.9),
        "norm1_shift": normal_values(streams_of[2], (D,), 0.3, 1.75, (), jnp.float32),
        "spec_w1": normal_values(streams_of[3], (BLOCKS, 2, BS, BS), (2 * BS) ** -0.5, 0.4375, ((0, 4),)),
        "spec_b1": normal_values(streams_of[4], (BLOCKS, 2, BS), 0.1, 0.625, ((0, 4),)),
        "spec_w2": normal_values(streams_of[5], (BLOCKS, 2, BS, BS), (2 * BS) ** -0.5, 0.4375, ((0, 4),)),
        "spec_b2": normal_values(streams_of[6], (BLOCKS, 2, BS), 0.1, 0.625, ((0, 4),)),
        "norm2_gain": jnp.clip(1.0 + 0.18 * jax.random.normal(streams_of[7], (D,), jnp.float32), 0.1, 1.9),
        "norm2_shift": normal_values(streams_of[8], (D,), 0.3, 1.75, (), jnp.float32),
        "fc1_weight": normal_values(streams_of[9], (D, FF), D ** -0.5, 0.21875, ((1, 4),)),
        "fc1_bias": normal_values(streams_of[10], (FF,), 0.3, 1.75, ((0, 4),)),
        "fc2_weight": normal_values(streams_of[11], (FF, D), FF ** -0.5, 0.109375, ((0, 4),)),
        "fc2_bias": normal_values(streams_of[12], (D,), 0.3, 1.75),
        "out_grad": normal_values(streams_of[13], (FIELDS, H, W, D), 1.0, 6.0, ((1, 8),)),
    }


@jax.custom_vjp
def low(v):
    return lax.optimization_barrier(v.astype(jnp.bfloat16)).astype(jnp.float32)

@jax.custom_vjp
def low_back(v):
    return v

def low_keep(v):
    return (low(v), None)

def low_pass(kept, grad):
    return (grad,)

def back_keep(v):
    return (v, None)

def back_low(kept, grad):
    return (low(grad),)
low.defvjp(low_keep, low_pass)
low_back.defvjp(back_keep, back_low)
threshold = 0.01

def phase_angles(rows, columns, period):
    product = rows[:, None] * columns[None, :] % period
    return 2.0 * math.pi / period * product.astype(jnp.float32)

def width_tables(width, modes):
    positions = jnp.arange(width, dtype=jnp.int32)
    wavenums = jnp.arange(modes, dtype=jnp.int32)
    angles = phase_angles(positions, wavenums, width)
    scale = 1.0 / math.sqrt(width)
    cosine = jnp.cos(angles)
    sine = jnp.sin(angles)
    forward_cos = cosine * scale
    forward_sin = -sine * scale
    weights = jnp.where((wavenums == 0) | (2 * wavenums == width), 1.0, 2.0).astype(jnp.float32)
    inverse_cos = weights[:, None] * cosine.T * scale
    inverse_sin = -(weights[:, None] * sine.T) * scale
    return (forward_cos, forward_sin, inverse_cos, inverse_sin)

def height_tables(modes, rows, period):
    angles = phase_angles(modes, rows, period)
    scale = 1.0 / math.sqrt(period)
    return (jnp.cos(angles) * scale, jnp.sin(angles) * scale)

def layer_norm(values, gain, shift):
    centred = values - lax.optimization_barrier(jnp.mean(values, -1, keepdims=True))
    variance = lax.optimization_barrier(jnp.mean(centred * centred, -1, keepdims=True))
    return centred * lax.rsqrt(variance + 1e-05) * gain + shift

def shrink(values):
    return values - threshold * jnp.tanh(values / threshold)

def forward(inputs, gain_one, shift_one, weight_one, bias_one, weight_two, bias_two, gain_two, shift_two, fc_one, fc_bias_one, fc_two, fc_bias_two):
    highest = lax.Precision.HIGHEST
    esum = partial(jnp.einsum, precision=highest)
    tables = width_tables(W, KW)
    forward_cos, forward_sin, inverse_cos, inverse_sin = [low(table) for table in tables]
    row_index = jnp.arange(H, dtype=jnp.int32)
    row_cos, row_sin = [low(table) for table in height_tables(row_index, row_index, H)]
    normed_one = low_back(low(layer_norm(inputs, gain_one, shift_one)))
    col_real = low_back(low(esum('fhwd,wk->fhkd', normed_one, forward_cos)))
    col_imag = low_back(low(esum('fhwd,wk->fhkd', normed_one, forward_sin)))
    spec_real = esum('qh,fhkd->fqkd', row_cos, col_real) + esum('qh,fhkd->fqkd', row_sin, col_imag)
    spec_imag = esum('qh,fhkd->fqkd', row_cos, col_imag) - esum('qh,fhkd->fqkd', row_sin, col_real)
    spec_real = low_back(low(spec_real))
    spec_imag = low_back(low(spec_imag))
    block_shape = (FIELDS, H, KW, BLOCKS, BS)
    spec_real = spec_real.reshape(block_shape)
    spec_imag = spec_imag.reshape(block_shape)

    def complex_apply(real_part, imag_part, weight_real, weight_imag):
        real_out = esum('fqkbc,bcd->fqkbd', real_part, weight_real) - esum('fqkbc,bcd->fqkbd', imag_part, weight_imag)
        imag_out = esum('fqkbc,bcd->fqkbd', imag_part, weight_real) + esum('fqkbc,bcd->fqkbd', real_part, weight_imag)
        return (real_out, imag_out)
    pre_real, pre_imag = complex_apply(spec_real, spec_imag, weight_one[:, 0], weight_one[:, 1])
    pre_real = low_back(pre_real + bias_one[:, 0])
    pre_imag = low_back(pre_imag + bias_one[:, 1])
    hid_real = low(jax.nn.gelu(pre_real))
    hid_imag = low(jax.nn.gelu(pre_imag))
    two_real, two_imag = complex_apply(hid_real, hid_imag, weight_two[:, 0], weight_two[:, 1])
    two_real = low_back(two_real + bias_two[:, 0])
    two_imag = low_back(two_imag + bias_two[:, 1])
    filt_real = low(shrink(two_real)).reshape(FIELDS, H, KW, D)
    filt_imag = low(shrink(two_imag)).reshape(FIELDS, H, KW, D)
    back_real = esum('qh,fqkd->fhkd', row_cos, filt_real) - esum('qh,fqkd->fhkd', row_sin, filt_imag)
    back_imag = esum('qh,fqkd->fhkd', row_cos, filt_imag) + esum('qh,fqkd->fhkd', row_sin, filt_real)
    back_real = low_back(low(back_real))
    back_imag = low_back(low(back_imag))
    filter_out = esum('fhkd,kw->fhwd', back_real, inverse_cos) + esum('fhkd,kw->fhwd', back_imag, inverse_sin)
    filter_out = low_back(low(filter_out))
    mixed = inputs + filter_out
    normed_two = low(layer_norm(mixed, gain_two, shift_two))
    hidden_pre = low_back(esum('fhwd,de->fhwe', normed_two, fc_one) + fc_bias_one)
    activated = low(jax.nn.gelu(hidden_pre))
    return mixed + (esum('fhwe,ed->fhwd', activated, fc_two) + fc_bias_two)

def reference(fields_in, norm1_gain, norm1_shift, spec_w1, spec_b1, spec_w2, spec_b2, norm2_gain, norm2_shift, fc1_weight, fc1_bias, fc2_weight, fc2_bias, out_grad):
    values = [fields_in, norm1_gain, norm1_shift, spec_w1, spec_b1, spec_w2, spec_b2, norm2_gain, norm2_shift, fc1_weight, fc1_bias, fc2_weight, fc2_bias]
    values = [item.astype(jnp.float32) for item in values]
    output, pullback = jax.vjp(forward, *values)
    grads = pullback(out_grad.astype(jnp.float32))
    return (output, grads[0], grads[1], grads[2], grads[3], grads[4], grads[5], grads[6], grads[7], grads[8], grads[9], grads[10], grads[11], grads[12])
```

```python
import math

import jax
import jax.numpy as jnp
import numpy as np
from jax import lax
from jax.sharding import PartitionSpec as P

threshold = 0.01


def phase_angles(rows, columns, period):
    product = rows[:, None] * columns[None, :] % period
    return (np.float32(2.0 * math.pi / period) * product.astype(np.float32)).astype(np.float32)


def longitude_table(width, modes, padded):
    angles = phase_angles(np.arange(width), np.arange(modes), width)
    scale = np.float32(1.0 / math.sqrt(width))
    table = np.zeros((2, padded, width), np.float32)
    table[0, :modes] = (np.cos(angles) * scale).T
    table[1, :modes] = (-np.sin(angles) * scale).T
    return table.astype(jnp.bfloat16)


def latitude_table(period, own_rows, inner):
    angles = phase_angles(np.arange(period), np.arange(period), period)
    scale = np.float32(1.0 / math.sqrt(period))
    cosine = (np.cos(angles) * scale).reshape(period, -1, own_rows)
    sine = (np.sin(angles) * scale).reshape(period, -1, own_rows)
    owners = period // own_rows
    table = np.zeros((2, period, inner, owners, 2, own_rows, inner), np.float32)
    for index in range(inner):
        table[0, :, index, :, 0, :, index] = cosine
        table[0, :, index, :, 1, :, index] = sine
        table[1, :, index, :, 1, :, index] = cosine
        table[1, :, index, :, 0, :, index] = -sine
    return table.reshape(2 * period * inner, 2 * period * inner).astype(jnp.bfloat16)


def wide_dot(spec, left, right):
    return jnp.einsum(spec, left, right, preferred_element_type=jnp.float32)


def complex_apply(real_part, imag_part, weight):
    product = lambda left, right: wide_dot("mbc,bcd->mbd", left, right)
    real_out = product(real_part, weight[:, 0]) - product(imag_part, weight[:, 1])
    imag_out = product(imag_part, weight[:, 0]) + product(real_part, weight[:, 1])
    return real_out, imag_out


def complex_adjoint(grad_real, grad_imag, weight):
    product = lambda left, right: wide_dot("mbd,bcd->mbc", left, right)
    real_in = product(grad_real, weight[:, 0]) + product(grad_imag, weight[:, 1])
    imag_in = product(grad_imag, weight[:, 0]) - product(grad_real, weight[:, 1])
    return real_in, imag_in


def complex_weight_grads(real_part, imag_part, grad_real, grad_imag):
    outer = lambda left, right: wide_dot("mbc,mbd->bcd", left, right)
    weight_real = outer(real_part, grad_real) + outer(imag_part, grad_imag)
    weight_imag = outer(real_part, grad_imag) - outer(imag_part, grad_real)
    bias_real = jnp.sum(grad_real, 0, dtype=jnp.float32)
    bias_imag = jnp.sum(grad_imag, 0, dtype=jnp.float32)
    return jnp.stack([weight_real, weight_imag], 1), jnp.stack([bias_real, bias_imag], 1)


def layer_norm(values, gain, shift):
    centred = values - jnp.mean(values, -1, keepdims=True)
    variance = jnp.mean(centred * centred, -1, keepdims=True)
    inv_std = lax.rsqrt(variance + 1e-05)
    normal_hat = centred * inv_std
    return (normal_hat * gain + shift, normal_hat, inv_std)


def norm_backward(grad, normal_hat, inv_std, gain):
    scaled = grad * gain
    return inv_std * (
        scaled
        - jnp.mean(scaled, -1, keepdims=True)
        - normal_hat * jnp.mean(scaled * normal_hat, -1, keepdims=True)
    )


def shrink(values):
    return values - threshold * jnp.tanh(values / threshold)


def shrink_slope(values):
    bent = jnp.tanh(values / threshold)
    return bent * bent


def local(
    fields_in,
    norm1_gain,
    norm1_shift,
    spec_w1,
    spec_b1,
    spec_w2,
    spec_b2,
    norm2_gain,
    norm2_shift,
    fc1_weight,
    fc1_bias,
    fc2_weight,
    fc2_bias,
    out_grad,
):
    narrow = jnp.bfloat16
    fields, rows_here, width, channels = fields_in.shape
    sp_size, wa_size = lax.axis_size("sp"), lax.axis_size("wa")
    block = spec_w1.shape[2]
    blocks = channels // block
    modes = width // 2 + 1
    period = rows_here * sp_size
    each = -(-modes // (sp_size * wa_size))
    padded = each * sp_size * wa_size
    count = period * fields * each
    long_all = jnp.asarray(longitude_table(width, modes, padded))
    weights = np.where((np.arange(padded) == 0) | (2 * np.arange(padded) == width), 1.0, 2.0)
    long_back_all = jnp.asarray((longitude_table(width, modes, padded) * weights[None, :, None]).astype(narrow))
    lat = jnp.asarray(latitude_table(period, rows_here, fields * each))
    place = lax.axis_index("wa")
    pick = lambda table: lax.dynamic_slice_in_dim(
        table, place * (each * sp_size), each * sp_size, 1
    ).reshape(2, sp_size, each, width)
    long_own, long_back_own = pick(long_all), pick(long_back_all)
    long_all = long_all.reshape(2, wa_size, sp_size, each, width)
    long_back_all = long_back_all.reshape(2, wa_size, sp_size, each, width)
    w1 = lax.all_gather(spec_w1, "wa", axis=0, tiled=True)
    b1 = lax.all_gather(spec_b1, "wa", axis=0, tiled=True).astype(jnp.float32)
    w2 = lax.all_gather(spec_w2, "wa", axis=0, tiled=True)
    b2 = lax.all_gather(spec_b2, "wa", axis=0, tiled=True).astype(jnp.float32)

    def to_modes(rows_data, table):
        parts = wide_dot("xsjw,fhwc->sxhfjc", table, rows_data).astype(narrow)
        parts = parts.reshape(sp_size, -1, channels)
        return lax.all_to_all(parts, "sp", 0, 0, tiled=True).reshape(-1, channels)

    def to_rows(mode_data, table):
        parts = mode_data.astype(narrow).reshape(sp_size, -1, channels)
        parts = lax.all_to_all(parts, "sp", 0, 0, tiled=True)
        parts = lax.all_gather(parts, "wa", axis=0)
        parts = parts.reshape(wa_size, sp_size, 2, rows_here, fields, each, channels)
        return wide_dot("xasjw,asxhfjc->fhwc", table, parts)

    def halves(values):
        values = values.reshape(2, count, blocks, block)
        return values[0], values[1]

    def join(real_part, imag_part):
        return jnp.stack([real_part, imag_part]).reshape(2 * count, channels).astype(narrow)

    all_but_last = (0, 1, 2)
    input_wide = fields_in.astype(jnp.float32)
    normed_one, hat_one, inv_std_one = layer_norm(input_wide, norm1_gain, norm1_shift)
    columns = to_modes(normed_one.astype(narrow), long_own)
    spectrum = wide_dot("qh,hc->qc", lat, columns).astype(narrow)
    spec_real, spec_imag = halves(spectrum)
    one_real, one_imag = complex_apply(spec_real, spec_imag, w1)
    hid_real, real_pull = jax.vjp(jax.nn.gelu, one_real + b1[:, 0])
    hid_imag, imag_pull = jax.vjp(jax.nn.gelu, one_imag + b1[:, 1])
    hid_real = hid_real.astype(narrow)
    hid_imag = hid_imag.astype(narrow)
    two_real, two_imag = complex_apply(hid_real, hid_imag, w2)
    two_real = two_real + b2[:, 0]
    two_imag = two_imag + b2[:, 1]
    filtered = join(shrink(two_real), shrink(two_imag))
    filter_all = to_rows(wide_dot("qh,qc->hc", lat, filtered), long_back_all).astype(narrow)
    mixed = input_wide + filter_all.astype(jnp.float32)
    normed_two, hat_two, inv_std_two = layer_norm(mixed, norm2_gain, norm2_shift)
    normed_rows = normed_two.astype(narrow).reshape(-1, channels)
    hidden_pre = wide_dot("rd,de->re", normed_rows, fc1_weight) + fc1_bias.astype(jnp.float32)
    activated, gelu_pull = jax.vjp(jax.nn.gelu, hidden_pre)
    activated = activated.astype(narrow)
    grad_rows = out_grad.reshape(-1, channels)
    grad_act = wide_dot("rd,ed->re", grad_rows, fc2_weight)
    grad_hidden = gelu_pull(grad_act)[0].astype(narrow)
    grad_norm_part = wide_dot("re,de->rd", grad_hidden, fc1_weight)
    grad_norm_two = (
        lax.psum(grad_norm_part.astype(narrow), "wa").astype(jnp.float32).reshape(mixed.shape)
    )
    branch = lax.psum(wide_dot("re,ed->rd", activated, fc2_weight).astype(narrow), "wa")
    output = mixed + (branch.astype(jnp.float32) + fc2_bias.astype(jnp.float32)).reshape(mixed.shape)
    fc2_weight_grad = wide_dot("re,rd->ed", activated, grad_rows)
    fc2_bias_grad = jnp.sum(grad_rows, 0, dtype=jnp.float32)
    fc1_weight_grad = wide_dot("rd,re->de", normed_rows, grad_hidden)
    fc1_bias_grad = jnp.sum(grad_hidden, 0, dtype=jnp.float32)
    fc_sums = lax.psum((fc1_weight_grad.astype(narrow), fc2_weight_grad.astype(narrow)), "sp")
    norm2_gain_grad = jnp.sum(grad_norm_two * hat_two, all_but_last)
    norm2_shift_grad = jnp.sum(grad_norm_two, all_but_last)
    grad_mixed = out_grad.astype(jnp.float32) + norm_backward(
        grad_norm_two, hat_two, inv_std_two, norm2_gain
    )
    grad_columns = to_modes(grad_mixed.astype(narrow), long_back_own)
    grad_filtered = wide_dot("qh,hc->qc", lat, grad_columns)
    grad_out_real, grad_out_imag = halves(grad_filtered)
    grad_two_real = (grad_out_real * shrink_slope(two_real)).astype(narrow)
    grad_two_imag = (grad_out_imag * shrink_slope(two_imag)).astype(narrow)
    spec_w2_grad, spec_b2_grad = complex_weight_grads(
        hid_real, hid_imag, grad_two_real, grad_two_imag
    )
    grad_hid_real, grad_hid_imag = complex_adjoint(grad_two_real, grad_two_imag, w2)
    grad_one_real = real_pull(grad_hid_real)[0].astype(narrow)
    grad_one_imag = imag_pull(grad_hid_imag)[0].astype(narrow)
    spec_w1_grad, spec_b1_grad = complex_weight_grads(
        spec_real, spec_imag, grad_one_real, grad_one_imag
    )
    grad_spec_real, grad_spec_imag = complex_adjoint(grad_one_real, grad_one_imag, w1)
    grad_spectrum = join(grad_spec_real, grad_spec_imag)
    grad_norm_one = (
        to_rows(wide_dot("qh,qc->hc", lat, grad_spectrum), long_all)
        .astype(narrow)
        .astype(jnp.float32)
    )
    norm1_gain_grad = jnp.sum(grad_norm_one * hat_one, all_but_last)
    norm1_shift_grad = jnp.sum(grad_norm_one, all_but_last)
    fields_grad = grad_mixed + norm_backward(grad_norm_one, hat_one, inv_std_one, norm1_gain)
    own_blocks = blocks // wa_size
    spec_w1_grad, spec_w2_grad, spec_b1_grad, spec_b2_grad = [
        lax.dynamic_slice_in_dim(value, place * own_blocks, own_blocks, 0)
        for value in lax.psum(
            (spec_w1_grad, spec_w2_grad, spec_b1_grad, spec_b2_grad), ("sp", "wa")
        )
    ]
    sums = lax.psum(
        (
            fc1_bias_grad,
            fc2_bias_grad,
            norm1_gain_grad,
            norm1_shift_grad,
            norm2_gain_grad,
            norm2_shift_grad,
        ),
        "sp",
    )
    return (
        output,
        fields_grad,
        sums[2],
        sums[3],
        spec_w1_grad,
        spec_b1_grad,
        spec_w2_grad,
        spec_b2_grad,
        sums[4],
        sums[5],
        fc_sums[0].astype(jnp.float32),
        sums[0],
        fc_sums[1].astype(jnp.float32),
        sums[1],
    )


def solution(mesh):
    return jax.shard_map(
        local,
        mesh=mesh,
        in_specs=(
            P(None, "sp", None, None),
            P(),
            P(),
            P("wa", None, None, None),
            P("wa", None, None),
            P("wa", None, None, None),
            P("wa", None, None),
            P(),
            P(),
            P(None, "wa"),
            P("wa"),
            P("wa", None),
            P(),
            P(None, "sp", None, None),
        ),
        out_specs=(
            P(None, "sp", None, None),
            P(None, "sp", None, None),
            P(),
            P(),
            P("wa", None, None, None),
            P("wa", None, None),
            P("wa", None, None, None),
            P("wa", None, None),
            P(),
            P(),
            P(None, "wa"),
            P("wa"),
            P("wa", None),
            P(),
        ),
        check_vma=False,
    )
```

```python
import functools
import math
import types

import jax
import jax.numpy as jnp
import numpy as np
from jax import lax
from jax.experimental import pallas as pl
from jax.experimental.pallas import tpu as pltpu
from jax.sharding import PartitionSpec as P

threshold = 0.01
narrow = jnp.bfloat16
wide = jnp.float32
MESH = pl.DeviceIdType.MESH
halves = 2


def round_up(value, step):
    return -(-value // step) * step


def phase_angles(rows, columns, period):
    product = rows[:, None] * columns[None, :] % period
    return (np.float32(2.0 * math.pi / period) * product.astype(np.float32)).astype(np.float32)


def plan(n_sp, n_wa, fields, rows_here, width, channels, blocks, block, hidden):
    z = types.SimpleNamespace(
        n_sp=n_sp, n_wa=n_wa, n_y=n_wa // 2, width=width, channels=channels, hidden=hidden,
        blocks=blocks, block=block, rows=fields * rows_here, fields=fields, rows_here=rows_here,
    )
    z.period = rows_here * n_sp
    z.modes = width // 2 + 1
    z.each = -(-z.modes // (n_sp * n_wa))
    z.pitch = round_up(width, 32)
    z.lanes = channels // halves
    z.slot = round_up(2 * rows_here * fields * z.each, 8)
    z.group = round_up(2 * n_sp * z.each, 16)
    z.count = z.period * fields * z.each
    z.half_blocks = blocks // halves
    z.own_blocks = blocks // n_wa
    z.pack = round_up(4 * block + 16, 16 * n_sp // math.gcd(16 * n_sp, z.own_blocks))
    return z


def longitude_tables(z):
    angles = phase_angles(np.arange(z.width), np.arange(z.modes), z.width)
    scale = np.float32(1.0 / math.sqrt(z.width))
    padded = z.each * z.n_sp * z.n_wa
    table = np.zeros((2, padded, z.width), np.float32)
    table[0, : z.modes] = (np.cos(angles) * scale).T
    table[1, : z.modes] = (-np.sin(angles) * scale).T
    k = np.arange(padded)
    weights = np.where((k == 0) | (2 * k == z.width), 1.0, 2.0).astype(np.float32)
    both = np.stack([table, table * weights[None, :, None]])
    both = both.reshape(2, 2, z.n_wa, z.n_sp * z.each, z.width)
    rows = np.zeros((2, z.n_wa, z.group, z.pitch), np.float32)
    rows[:, :, : 2 * z.n_sp * z.each, : z.width] = both.transpose(0, 2, 1, 3, 4).reshape(
        2, z.n_wa, -1, z.width
    )
    out = rows.reshape(2, z.n_wa * z.group, z.pitch).transpose(0, 2, 1)
    return rows.astype(narrow), out.astype(narrow)


def slot_index(z):
    table = np.zeros((z.n_sp, z.slot, z.rows, z.group), np.float32)
    for d in range(z.n_sp):
        for c in range(2):
            for h in range(z.rows_here):
                for f in range(z.fields):
                    for j in range(z.each):
                        r = ((c * z.rows_here + h) * z.fields + f) * z.each + j
                        table[d, r, f * z.rows_here + h, (c * z.n_sp + d) * z.each + j] = 1.0
    return table.reshape(z.n_sp * z.slot, z.rows * z.group).astype(narrow)


def latitude_table(z):
    angles = phase_angles(np.arange(z.period), np.arange(z.period), z.period)
    scale = np.float32(1.0 / math.sqrt(z.period))
    inner = z.fields * z.each
    cosine = (np.cos(angles) * scale).reshape(z.period, z.n_sp, z.rows_here)
    sine = (np.sin(angles) * scale).reshape(z.period, z.n_sp, z.rows_here)
    table = np.zeros((2, z.period, inner, z.n_sp, 2, z.rows_here, inner), np.float32)
    for i in range(inner):
        table[0, :, i, :, 0, :, i] = cosine
        table[0, :, i, :, 1, :, i] = sine
        table[1, :, i, :, 1, :, i] = cosine
        table[1, :, i, :, 0, :, i] = -sine
    padded = np.zeros((2 * z.count, z.n_sp, z.slot), np.float32)
    padded[:, :, : 2 * z.rows_here * inner] = table.reshape(2 * z.count, z.n_sp, -1)
    return padded.reshape(2 * z.count, z.n_sp * z.slot).astype(narrow)


def dot(left, right):
    return jnp.dot(left, right, preferred_element_type=wide)


def dot_right_transposed(left, right):
    return lax.dot_general(left, right, (((1,), (1,)), ((), ())), preferred_element_type=wide)


def dot_left_transposed(left, right):
    return lax.dot_general(left, right, (((0,), (0,)), ((), ())), preferred_element_type=wide)


def gelu_with_slope(v):
    scale = np.float32(math.sqrt(2.0 / math.pi))
    square = v * v
    bent = jnp.tanh(scale * v * (1.0 + 0.044715 * square))
    above = 0.5 + 0.5 * bent
    slope = above + 0.5 * v * (1.0 - bent * bent) * (scale * (1.0 + (3 * 0.044715) * square))
    return v * above, slope


def row_parts(z, step=48):
    return [(start, min(step, z.width - start)) for start in range(0, z.width, step)]


def place(e):
    sp, wa = lax.axis_index("sp"), lax.axis_index("wa")
    e.sp, e.wa = sp, wa
    core = lax.rem(wa, 2)
    e.core = core
    e.sibling = (sp, wa + 1 - 2 * core)
    e.sp_peers = [(lax.rem(sp + i, e.z.n_sp), wa) for i in range(1, e.z.n_sp)]
    e.y_peers = [(sp, lax.rem(wa + 2 * j, e.z.n_wa)) for j in range(1, e.z.n_y)]
    e.wa_peers = [(sp, lax.rem(wa + j, e.z.n_wa)) for j in range(1, e.z.n_wa)]


def greet(e):
    barrier = pltpu.get_barrier_semaphore()
    for peer in e.sp_peers + e.wa_peers:
        pl.semaphore_signal(barrier, inc=1, device_id=peer, device_id_type=MESH)


def greeted(e):
    barrier = pltpu.get_barrier_semaphore()
    pl.semaphore_wait(barrier, len(e.sp_peers) + len(e.wa_peers))


def remote(source, target, send, recv, peer):
    copy = pltpu.make_async_remote_copy(
        src_ref=source, dst_ref=target, send_sem=send, recv_sem=recv,
        device_id=peer, device_id_type=MESH,
    )
    copy.start()
    return copy


def norm_parts(values):
    mean = jnp.mean(values, -1, keepdims=True)
    centred = values - mean
    variance = jnp.mean(centred * centred, -1, keepdims=True)
    return centred, lax.rsqrt(variance + 1e-05)


def clear_padding(e, buffer):
    start = e.z.width // 16 * 16
    if start < e.z.pitch:
        buffer[:, start:, :] = jnp.zeros_like(buffer[:, start:, :])


def lane_slice(e, half):
    return pl.ds(half * e.z.lanes, e.z.lanes)


def to_slots(e, source, table, columns, slots, half):
    z = e.z
    for row in range(z.rows):
        columns[half, row] = dot(table, source[row, :, lane_slice(e, half)]).astype(narrow)
    moved = dot(e.slot_rows[...], columns[half].reshape(z.rows * z.group, z.lanes))
    moved = moved.astype(narrow)
    for d in range(z.n_sp):
        slots[half, d] = moved[d * z.slot : (d + 1) * z.slot]


def send_slots(e, slots, landed, send, recv, half):
    copies = [
        remote(
            slots.at[half, peer[0]], landed.at[half, e.sp],
            send.at[half, i], recv.at[half, i], peer,
        )
        for i, peer in enumerate(e.sp_peers)
    ]
    landed[half, e.sp] = slots[half, e.sp]
    return copies


def arrived_slots(e, landed, copies, half):
    for copy in copies:
        copy.wait_recv()
    z = e.z
    rows = landed[half].astype(wide).reshape(z.n_sp * z.slot, z.lanes)
    return rows.astype(narrow)


def finish(copies):
    for copy in copies:
        copy.wait_send()


def modes_from_slots(e, rows):
    z = e.z
    real = dot(e.lat[: z.count], rows)
    imag = dot(e.lat[z.count :], rows)
    return jnp.concatenate([real, imag], 1)


def slots_from_modes(e, values, slots, half):
    z = e.z
    stacked = jnp.concatenate([values[:, : z.lanes], values[:, z.lanes :]], 0)
    moved = dot(e.lat_cols[...], stacked).astype(narrow)
    for d in range(z.n_sp):
        slots[half, d] = moved[d * z.slot : (d + 1) * z.slot]


def gather_start(e, rows, gathered, sems, half):
    z = e.z
    send_y, recv_y, send_core, recv_core = sems
    ordered = dot(e.slot_cols[...], rows).astype(narrow)
    for row in range(z.rows):
        gathered[half, row, e.wa] = ordered[row * z.group : (row + 1) * z.group]
    own = gathered.at[half, :, e.wa]
    copies_y = [
        remote(own, own, send_y.at[half, j], recv_y.at[half, j], peer)
        for j, peer in enumerate(e.y_peers)
    ]
    copies_core = [remote(own, own, send_core.at[half, 0], recv_core.at[half, 0], e.sibling)]
    return copies_y, copies_core


def gather_forward(e, copies, gathered, sems, half):
    z = e.z
    send_y, recv_y, send_core, recv_core = sems
    copies_y, copies_core = copies
    for j, copy in enumerate(copies_y):
        copy.wait_recv()
        origin = lax.rem(e.wa + z.n_wa - 2 * (j + 1), z.n_wa)
        slab = gathered.at[half, :, origin]
        copies_core.append(
            remote(slab, slab, send_core.at[half, j + 1], recv_core.at[half, j + 1], e.sibling)
        )
    for copy in copies_core:
        copy.wait_recv()
    finish(copies_y + copies_core)


def rows_from_gathered(e, table, gathered, half, row):
    z = e.z
    return dot(table, gathered[half, row].reshape(z.n_wa * z.group, z.lanes))


def pack_weights(e):
    z = e.z
    for i in range(z.own_blocks):
        at = e.wa * z.own_blocks + i
        e.packed[at, : 2 * z.block] = e.w1[i]
        e.packed[at, 2 * z.block : 4 * z.block] = e.w2[i]
        line = lax.broadcasted_iota(jnp.int32, (16, z.block), 0)
        bias = jnp.zeros((16, z.block), wide)
        for k in range(2):
            bias = jnp.where(line == k, e.b1[i, k : k + 1].astype(wide), bias)
            bias = jnp.where(line == 2 + k, e.b2[i, k : k + 1].astype(wide), bias)
        e.packed[at, 4 * z.block : 4 * z.block + 16] = bias.astype(narrow)


def send_weights(e, send, recv):
    z = e.z
    own = e.packed.at[pl.ds(e.wa * z.own_blocks, z.own_blocks)]
    return [
        remote(own, own, send.at[j], recv.at[j], peer) for j, peer in enumerate(e.wa_peers)
    ]


def spread(z, index):
    row = lax.broadcasted_iota(jnp.int32, (z.block, z.lanes), 0)
    lane = lax.broadcasted_iota(jnp.int32, (z.block, z.lanes), 1)
    return jnp.where(lane == row + index * z.block, 1.0, 0.0).astype(narrow)


def build_weights(e):
    z = e.z
    n, lanes = z.block, z.lanes
    for half in range(halves):
        bias = jnp.zeros((16, lanes), wide)
        for i in range(z.half_blocks):
            source = e.packed[half * z.half_blocks + i, : 4 * n + 16]
            placed = dot(source, spread(z, i))
            bias = bias + placed[4 * n :]
            for k, target in ((0, e.big1), (1, e.big2)):
                real = placed[2 * k * n : (2 * k + 1) * n]
                imag = placed[(2 * k + 1) * n : (2 * k + 2) * n]
                up, down = pl.ds(i * n, n), pl.ds(lanes + i * n, n)
                target[half, up, :lanes] = real.astype(narrow)
                target[half, up, lanes:] = imag.astype(narrow)
                target[half, down, :lanes] = (-imag).astype(narrow)
                target[half, down, lanes:] = real.astype(narrow)
        e.bias[half] = bias


def modes_forward(e, rows, half):
    z = e.z
    spec = modes_from_slots(e, rows).astype(narrow)
    e.spec[half] = spec
    bias = e.bias[half]
    bias1 = jnp.concatenate([bias[0:1], bias[1:2]], 1)
    bias2 = jnp.concatenate([bias[2:3], bias[3:4]], 1)
    hid, slope = gelu_with_slope(dot(spec, e.big1[half]) + bias1)
    e.slope1[half] = slope
    hid = hid.astype(narrow)
    e.hid[half] = hid
    two = dot(hid, e.big2[half]) + bias2
    bent = jnp.tanh(two * (1.0 / threshold))
    e.slope2[half] = bent * bent
    return (two - threshold * bent).astype(narrow)


def modes_backward(e, rows, half):
    z = e.z
    grad_two = (modes_from_slots(e, rows) * e.slope2[half]).astype(narrow)
    e.grad_two[half] = grad_two
    grad_hid = dot_right_transposed(grad_two, e.big2[half])
    grad_one = (grad_hid * e.slope1[half]).astype(narrow)
    e.grad_one[half] = grad_one
    return dot_right_transposed(grad_one, e.big1[half]).astype(narrow)


def outer_parts(z, left, right):
    lanes = z.lanes
    product = dot_left_transposed(left, right)
    real = product[:lanes, :lanes] + product[lanes:, lanes:]
    imag = product[:lanes, lanes:] - product[lanes:, :lanes]
    return real.astype(narrow), imag.astype(narrow)


def spectral_grads(e, half):
    z = e.z
    n, lanes = z.block, z.lanes
    real1, imag1 = outer_parts(z, e.spec[half], e.grad_one[half])
    real2, imag2 = outer_parts(z, e.hid[half], e.grad_two[half])
    bias1 = jnp.sum(e.grad_one[half].astype(wide), 0, keepdims=True)
    bias2 = jnp.sum(e.grad_two[half].astype(wide), 0, keepdims=True)
    line = lax.broadcasted_iota(jnp.int32, (16, lanes), 0)
    bias = jnp.zeros((16, lanes), wide)
    for k, row in enumerate((bias1[:, :lanes], bias1[:, lanes:], bias2[:, :lanes], bias2[:, lanes:])):
        bias = jnp.where(line == k, row, bias)
    bias = bias.astype(narrow)
    for i in range(z.half_blocks):
        at = half * z.half_blocks + i
        parts = [value[i * n : (i + 1) * n] for value in (real1, imag1, real2, imag2)]
        stacked = jnp.concatenate(parts + [bias], 0)
        e.grad_pack[at, : 4 * n + 16] = dot_right_transposed(stacked, spread(z, i)).astype(narrow)
        if z.pack > 4 * n + 16:
            e.grad_pack[at, 4 * n + 16 :] = jnp.zeros((z.pack - 4 * n - 16, n), narrow)


class Names:
    def __init__(self):
        self.names, self.shapes = [], []

    def add(self, name, shape):
        self.names.append(name)
        self.shapes.append(shape)

    def vmem(self, name, shape, dtype=narrow):
        self.add(name, pltpu.VMEM(shape, dtype))

    def dma(self, name, shape):
        self.add(name, pltpu.SemaphoreType.DMA(shape))


def exchange_scratch(s, z, tag):
    s.vmem("columns", (halves, z.rows, z.group, z.lanes))
    for name in ("slots_a", "slots_b", "landed_a", "landed_b"):
        s.vmem(name, (halves, z.n_sp, z.slot, z.lanes))
    for name in ("send_a", "recv_a", "send_b", "recv_b"):
        s.dma(name, (halves, z.n_sp - 1))
    s.vmem("gathered", (halves, z.rows, z.n_wa, z.group, z.lanes))
    for name in ("send_y", "recv_y"):
        s.dma(name, (halves, max(z.n_y - 1, 1)))
    for name in ("send_core", "recv_core"):
        s.dma(name, (halves, z.n_y))


def call_kernel(body, z, inputs, outputs, scratch, collective):
    names = [name for name, _ in inputs] + [name for name, _, _ in outputs]

    def kernel(*refs):
        e = types.SimpleNamespace(z=z)
        for name, ref in zip(names + scratch.names, refs):
            setattr(e, name, ref)
        place(e)
        body(e)

    in_specs = [
        pl.BlockSpec(memory_space=pl.ANY if name.startswith("hbm_") else pltpu.VMEM)
        for name, _ in inputs
    ]
    out_specs = [
        pl.BlockSpec(memory_space=pl.ANY if name.startswith("hbm_") else pltpu.VMEM)
        for name, _, _ in outputs
    ]
    return pl.pallas_call(
        kernel,
        out_shape=[jax.ShapeDtypeStruct(shape, dtype) for _, shape, dtype in outputs],
        in_specs=in_specs,
        out_specs=out_specs,
        scratch_shapes=scratch.shapes,
        compiler_params=pltpu.CompilerParams(
            collective_id=collective, has_side_effects=True, vmem_limit_bytes=60 * 1024 * 1024
        ),
    )(*[value for _, value in inputs])


def forward_body(e):
    z = e.z
    loads = [
        pltpu.make_async_copy(e.hbm_x.at[row], e.xs.at[row], e.load.at[row])
        for row in range(z.rows)
    ]
    for load in loads:
        load.start()
    greet(e)
    pack_weights(e)
    clear_padding(e, e.xn)
    gain, shift = e.gain1[...], e.shift1[...]
    for row in range(z.rows):
        loads[row].wait()
        for start, size in row_parts(z):
            values = e.xs[row, start : start + size].astype(wide)
            centred, inv_std = norm_parts(values)
            normed = centred * inv_std * gain + shift
            e.xn[row, start : start + size] = normed.astype(narrow)
    greeted(e)
    weights = send_weights(e, e.send_w, e.recv_w)
    table = e.long_rows[e.wa]
    first = []
    for half in range(halves):
        to_slots(e, e.xn, table, e.columns, e.slots_a, half)
        first.append(send_slots(e, e.slots_a, e.landed_a, e.send_a, e.recv_a, half))
    for copy in weights:
        copy.wait_recv()
    build_weights(e)
    second = []
    for half in range(halves):
        rows = arrived_slots(e, e.landed_a, first[half], half)
        slots_from_modes(e, modes_forward(e, rows, half), e.slots_b, half)
        second.append(send_slots(e, e.slots_b, e.landed_b, e.send_b, e.recv_b, half))
    sems = (e.send_y, e.recv_y, e.send_core, e.recv_core)
    gathers = []
    for half in range(halves):
        rows = arrived_slots(e, e.landed_b, second[half], half)
        gathers.append(gather_start(e, rows, e.gathered, sems, half))
    for half in range(halves):
        gather_forward(e, gathers[half], e.gathered, sems, half)
        for row in range(z.rows):
            filtered = rows_from_gathered(e, e.long_out[...], e.gathered, half, row)
            filtered = filtered[: z.width].astype(narrow).astype(wide)
            lanes = lane_slice(e, half)
            e.mixed[row, :, lanes] = e.xs[row, :, lanes].astype(wide) + filtered
    for copies in first + second:
        finish(copies)
    finish(weights)


def backward_body(e):
    z = e.z
    clear_padding(e, e.gf)
    greet(e)
    for row in range(z.rows):
        for start, size in row_parts(z):
            e.gf[row, start : start + size] = e.grad_filter[row, start : start + size]
    greeted(e)
    table = e.long_rows[e.wa]
    first, second, gathers = [], [], []
    for half in range(halves):
        to_slots(e, e.gf, table, e.columns, e.slots_a, half)
        first.append(send_slots(e, e.slots_a, e.landed_a, e.send_a, e.recv_a, half))
    for half in range(halves):
        rows = arrived_slots(e, e.landed_a, first[half], half)
        slots_from_modes(e, modes_backward(e, rows, half), e.slots_b, half)
        second.append(send_slots(e, e.slots_b, e.landed_b, e.send_b, e.recv_b, half))
    for half in range(halves):
        spectral_grads(e, half)
    sems = (e.send_y, e.recv_y, e.send_core, e.recv_core)
    for half in range(halves):
        rows = arrived_slots(e, e.landed_b, second[half], half)
        gathers.append(gather_start(e, rows, e.gathered, sems, half))
    for half in range(halves):
        gather_forward(e, gathers[half], e.gathered, sems, half)
        for row in range(z.rows):
            grad = rows_from_gathered(e, e.long_out[...], e.gathered, half, row)
            e.grad_norm[row, :, lane_slice(e, half)] = grad[: z.width].astype(narrow)
    for copies in first + second:
        finish(copies)


def forward_filter(z, x, gain, shift, w1, b1, w2, b2, tables):
    long_rows, long_out, slot_rows, slot_cols, lat, lat_cols = tables
    own, n = z.own_blocks, z.block
    inputs = [
        ("hbm_x", x), ("gain1", gain.reshape(1, -1)), ("shift1", shift.reshape(1, -1)),
        ("w1", w1.reshape(own, 2 * n, n)), ("b1", b1),
        ("w2", w2.reshape(own, 2 * n, n)), ("b2", b2),
        ("long_rows", long_rows[0]), ("long_out", long_out[1]),
        ("slot_rows", slot_rows), ("slot_cols", slot_cols), ("lat", lat), ("lat_cols", lat_cols),
    ]
    both = (halves, z.count, 2 * z.lanes)
    outputs = [
        ("mixed", (z.rows, z.width, z.channels), wide),
        ("spec", both, narrow), ("hid", both, narrow),
        ("slope1", both, wide), ("slope2", both, wide),
        ("big1", (halves, 2 * z.lanes, 2 * z.lanes), narrow),
        ("big2", (halves, 2 * z.lanes, 2 * z.lanes), narrow),
    ]
    s = Names()
    s.vmem("xs", (z.rows, z.width, z.channels))
    s.dma("load", (z.rows,))
    s.vmem("xn", (z.rows, z.pitch, z.channels))
    s.vmem("packed", (z.blocks, z.pack, z.block))
    s.vmem("bias", (halves, 16, z.lanes), wide)
    s.dma("send_w", (z.n_wa - 1,))
    s.dma("recv_w", (z.n_wa - 1,))
    exchange_scratch(s, z, "")
    return call_kernel(forward_body, z, inputs, outputs, s, 0)


def backward_filter(z, grad_filter, kept, tables):
    long_rows, long_out, slot_rows, slot_cols, lat, lat_cols = tables
    spec, hid, slope1, slope2, big1, big2 = kept
    inputs = [
        ("grad_filter", grad_filter), ("spec", spec), ("hid", hid), ("slope1", slope1),
        ("slope2", slope2), ("big1", big1), ("big2", big2),
        ("long_rows", long_rows[1]), ("long_out", long_out[0]),
        ("slot_rows", slot_rows), ("slot_cols", slot_cols), ("lat", lat), ("lat_cols", lat_cols),
    ]
    outputs = [
        ("grad_norm", (z.rows, z.width, z.channels), narrow),
        ("grad_pack", (z.blocks, z.pack, z.block), narrow),
    ]
    s = Names()
    s.vmem("gf", (z.rows, z.pitch, z.channels))
    s.vmem("grad_one", (halves, z.count, 2 * z.lanes))
    s.vmem("grad_two", (halves, z.count, 2 * z.lanes))
    exchange_scratch(s, z, "")
    return call_kernel(backward_body, z, inputs, outputs, s, 1)


def layer_norm(values, gain, shift):
    centred = values - jnp.mean(values, -1, keepdims=True)
    variance = jnp.mean(centred * centred, -1, keepdims=True)
    inv_std = lax.rsqrt(variance + 1e-05)
    normal_hat = centred * inv_std
    return (normal_hat * gain + shift, normal_hat, inv_std)


def norm_backward(grad, normal_hat, inv_std, gain):
    scaled = grad * gain
    return inv_std * (
        scaled
        - jnp.mean(scaled, -1, keepdims=True)
        - normal_hat * jnp.mean(scaled * normal_hat, -1, keepdims=True)
    )


def local(
    fields_in,
    norm1_gain,
    norm1_shift,
    spec_w1,
    spec_b1,
    spec_w2,
    spec_b2,
    norm2_gain,
    norm2_shift,
    fc1_weight,
    fc1_bias,
    fc2_weight,
    fc2_bias,
    out_grad,
):
    fields, rows_here, width, channels = fields_in.shape
    n_sp, n_wa = lax.axis_size("sp"), lax.axis_size("wa")
    block = spec_w1.shape[2]
    z = plan(
        n_sp, n_wa, fields, rows_here, width, channels, channels // block, block,
        fc1_weight.shape[1],
    )
    long_rows, long_out = longitude_tables(z)
    long_rows = long_rows.reshape(2, z.n_wa, z.group, z.pitch)
    index, lat = slot_index(z), latitude_table(z)
    tables = (long_rows, long_out, index, index.T, lat, lat.T)
    tables = [jnp.asarray(np.ascontiguousarray(table)) for table in tables]
    flat = (z.rows, width, channels)
    both_axes = (0, 1)
    rows_in = fields_in.reshape(flat)
    mixed, *kept = forward_filter(
        z, rows_in, norm1_gain, norm1_shift, spec_w1, spec_b1, spec_w2, spec_b2, tables
    )
    normed_two, hat_two, inv_std_two = layer_norm(mixed, norm2_gain, norm2_shift)
    normed_rows = normed_two.astype(narrow).reshape(-1, channels)
    hidden_pre = dot(normed_rows, fc1_weight) + fc1_bias.astype(wide)
    activated, gelu_pull = jax.vjp(jax.nn.gelu, hidden_pre)
    activated = activated.astype(narrow)
    grad_rows = out_grad.reshape(-1, channels)
    grad_act = dot_right_transposed(grad_rows, fc2_weight)
    grad_hidden = gelu_pull(grad_act)[0].astype(narrow)
    grad_norm_part = dot_right_transposed(grad_hidden, fc1_weight)
    grad_norm_two = lax.psum(grad_norm_part.astype(narrow), "wa").astype(wide).reshape(flat)
    branch = lax.psum(dot(activated, fc2_weight).astype(narrow), "wa")
    output = mixed + (branch.astype(wide) + fc2_bias.astype(wide)).reshape(flat)
    fc2_weight_grad = dot_left_transposed(activated, grad_rows)
    fc2_bias_grad = jnp.sum(grad_rows, 0, dtype=wide)
    fc1_weight_grad = dot_left_transposed(normed_rows, grad_hidden)
    fc1_bias_grad = jnp.sum(grad_hidden, 0, dtype=wide)
    fc_sums = lax.psum((fc1_weight_grad.astype(narrow), fc2_weight_grad.astype(narrow)), "sp")
    norm2_gain_grad = jnp.sum(grad_norm_two * hat_two, both_axes)
    norm2_shift_grad = jnp.sum(grad_norm_two, both_axes)
    grad_mixed = out_grad.reshape(flat).astype(wide) + norm_backward(
        grad_norm_two, hat_two, inv_std_two, norm2_gain
    )
    grad_norm_one, grad_pack = backward_filter(z, grad_mixed.astype(narrow), kept, tables)
    grad_norm_one = grad_norm_one.astype(wide)
    _, hat_one, inv_std_one = layer_norm(rows_in.astype(wide), norm1_gain, norm1_shift)
    norm1_gain_grad = jnp.sum(grad_norm_one * hat_one, both_axes)
    norm1_shift_grad = jnp.sum(grad_norm_one, both_axes)
    fields_grad = grad_mixed + norm_backward(grad_norm_one, hat_one, inv_std_one, norm1_gain)
    pack = lax.psum(grad_pack, ("sp", "wa"))
    pack = lax.dynamic_slice_in_dim(pack, lax.axis_index("wa") * z.own_blocks, z.own_blocks, 0)
    pack = pack.astype(wide)
    spec_w1_grad = pack[:, : 2 * block].reshape(-1, 2, block, block)
    spec_w2_grad = pack[:, 2 * block : 4 * block].reshape(-1, 2, block, block)
    spec_b1_grad = pack[:, 4 * block : 4 * block + 2]
    spec_b2_grad = pack[:, 4 * block + 2 : 4 * block + 4]
    sums = lax.psum(
        (
            fc1_bias_grad,
            fc2_bias_grad,
            norm1_gain_grad,
            norm1_shift_grad,
            norm2_gain_grad,
            norm2_shift_grad,
        ),
        "sp",
    )
    return (
        output.reshape(fields_in.shape),
        fields_grad.reshape(fields_in.shape),
        sums[2],
        sums[3],
        spec_w1_grad,
        spec_b1_grad,
        spec_w2_grad,
        spec_b2_grad,
        sums[4],
        sums[5],
        fc_sums[0].astype(wide),
        sums[0],
        fc_sums[1].astype(wide),
        sums[1],
    )


def solution(mesh):
    return jax.shard_map(
        local,
        mesh=mesh,
        in_specs=(
            P(None, "sp", None, None),
            P(),
            P(),
            P("wa", None, None, None),
            P("wa", None, None),
            P("wa", None, None, None),
            P("wa", None, None),
            P(),
            P(),
            P(None, "wa"),
            P("wa"),
            P("wa", None),
            P(),
            P(None, "sp", None, None),
        ),
        out_specs=(
            P(None, "sp", None, None),
            P(None, "sp", None, None),
            P(),
            P(),
            P("wa", None, None, None),
            P("wa", None, None),
            P("wa", None, None, None),
            P("wa", None, None),
            P(),
            P(),
            P(None, "wa"),
            P("wa"),
            P("wa", None),
            P(),
        ),
        check_vma=False,
    )
```

```python
import functools
import math
import types

import jax
import jax.numpy as jnp
import numpy as np
from jax import lax
from jax.experimental import pallas as pl
from jax.experimental.pallas import tpu as pltpu
from jax.sharding import PartitionSpec as P

threshold = 0.01
narrow = jnp.bfloat16
wide = jnp.float32
MESH = pl.DeviceIdType.MESH
halves = 2


def round_up(value, step):
    return -(-value // step) * step


def phase_angles(rows, columns, period):
    product = rows[:, None] * columns[None, :] % period
    return (np.float32(2.0 * math.pi / period) * product.astype(np.float32)).astype(np.float32)


def plan(n_sp, n_wa, fields, rows_here, width, channels, blocks, block, hidden):
    z = types.SimpleNamespace(
        n_sp=n_sp, n_wa=n_wa, n_y=n_wa // 2, width=width, channels=channels, hidden=hidden,
        blocks=blocks, block=block, fields=fields, planes=rows_here,
    )
    z.period = rows_here * n_sp
    z.modes = width // 2 + 1
    z.each = -(-z.modes // (n_sp * n_wa))
    z.plane = fields * width
    z.pitch = round_up(z.plane, 64)
    z.chunk = z.pitch // 2
    z.chunks = 2 * rows_here
    z.part = z.chunk // 2
    z.lanes = channels // halves
    z.slot = round_up(2 * rows_here * fields * z.each, 8)
    z.group = round_up(2 * n_sp * fields * z.each, 16)
    z.count = z.period * fields * z.each
    z.half_blocks = blocks // halves
    z.own_blocks = blocks // n_wa
    z.pack = round_up(4 * block + 16, 16 * n_sp // math.gcd(16 * n_sp, z.own_blocks))
    z.pack_share = z.own_blocks * z.pack // n_sp
    z.small = max(channels, hidden)
    return z


def longitude_tables(z):
    angles = phase_angles(np.arange(z.width), np.arange(z.modes), z.width)
    scale = np.float32(1.0 / math.sqrt(z.width))
    padded = z.each * z.n_sp * z.n_wa
    table = np.zeros((2, padded, z.width), np.float32)
    table[0, : z.modes] = (np.cos(angles) * scale).T
    table[1, : z.modes] = (-np.sin(angles) * scale).T
    k = np.arange(padded)
    weights = np.where((k == 0) | (2 * k == z.width), 1.0, 2.0).astype(np.float32)
    both = np.stack([table, table * weights[None, :, None]])
    both = both.reshape(2, 2, z.n_wa, z.n_sp, z.each, z.width).transpose(0, 2, 1, 3, 4, 5)
    rows = np.zeros((2, z.n_wa, 2, z.n_sp, z.fields, z.each, z.width, z.fields), np.float32)
    for f in range(z.fields):
        rows[:, :, :, :, f, :, :, f] = both
    padded = np.zeros((2, z.n_wa, z.group, z.pitch), np.float32)
    used = 2 * z.n_sp * z.fields * z.each
    padded[:, :, :used, : z.plane] = rows.reshape(2, z.n_wa, used, z.plane)
    out = padded.reshape(2, z.n_wa * z.group, z.pitch).transpose(0, 2, 1)
    return padded.astype(narrow), np.ascontiguousarray(out).astype(narrow)


def slot_index(z):
    table = np.zeros((z.n_sp, z.slot, z.planes, z.group), np.float32)
    for d in range(z.n_sp):
        for c in range(2):
            for h in range(z.planes):
                for f in range(z.fields):
                    for j in range(z.each):
                        r = ((c * z.planes + h) * z.fields + f) * z.each + j
                        table[d, r, h, ((c * z.n_sp + d) * z.fields + f) * z.each + j] = 1.0
    return table.reshape(z.n_sp * z.slot, z.planes * z.group).astype(narrow)


def latitude_table(z):
    angles = phase_angles(np.arange(z.period), np.arange(z.period), z.period)
    scale = np.float32(1.0 / math.sqrt(z.period))
    inner = z.fields * z.each
    cosine = (np.cos(angles) * scale).reshape(z.period, z.n_sp, z.planes)
    sine = (np.sin(angles) * scale).reshape(z.period, z.n_sp, z.planes)
    table = np.zeros((2, z.period, inner, z.n_sp, 2, z.planes, inner), np.float32)
    for i in range(inner):
        table[0, :, i, :, 0, :, i] = cosine
        table[0, :, i, :, 1, :, i] = sine
        table[1, :, i, :, 1, :, i] = cosine
        table[1, :, i, :, 0, :, i] = -sine
    padded = np.zeros((2 * z.count, z.n_sp, z.slot), np.float32)
    padded[:, :, : 2 * z.planes * inner] = table.reshape(2 * z.count, z.n_sp, -1)
    return padded.reshape(2 * z.count, z.n_sp * z.slot).astype(narrow)


def dot(left, right):
    return jnp.dot(left, right, preferred_element_type=wide)


def dot_right_transposed(left, right):
    return lax.dot_general(left, right, (((1,), (1,)), ((), ())), preferred_element_type=wide)


def dot_left_transposed(left, right):
    return lax.dot_general(left, right, (((0,), (0,)), ((), ())), preferred_element_type=wide)


def gelu_with_slope(v):
    scale = np.float32(math.sqrt(2.0 / math.pi))
    square = v * v
    bent = jnp.tanh(scale * v * (1.0 + 0.044715 * square))
    above = 0.5 + 0.5 * bent
    slope = above + 0.5 * v * (1.0 - bent * bent) * (scale * (1.0 + (3 * 0.044715) * square))
    return v * above, slope


def chunk_rows(z, c):
    return min(z.chunk, z.plane - (c % 2) * z.chunk)


def row_parts(z, c, step=48):
    rows = chunk_rows(z, c)
    return [(start, min(step, rows - start)) for start in range(0, rows, step)]


def place(e):
    z = e.z
    sp, wa = lax.axis_index("sp"), lax.axis_index("wa")
    e.sp, e.wa = sp, wa
    e.core, e.y = lax.rem(wa, 2), lax.div(wa, 2)
    e.sibling = (sp, wa + 1 - 2 * e.core)
    e.sp_peers = [(lax.rem(sp + i, z.n_sp), wa) for i in range(1, z.n_sp)]
    e.y_peers = [(sp, lax.rem(wa + 2 * j, z.n_wa)) for j in range(1, z.n_y)]
    e.wa_peers = [(sp, lax.rem(wa + j, z.n_wa)) for j in range(1, z.n_wa)]


def greet(e):
    barrier = pltpu.get_barrier_semaphore()
    for peer in e.sp_peers + e.wa_peers:
        pl.semaphore_signal(barrier, inc=1, device_id=peer, device_id_type=MESH)


def greeted(e):
    barrier = pltpu.get_barrier_semaphore()
    pl.semaphore_wait(barrier, len(e.sp_peers) + len(e.wa_peers))


def remote(source, target, send, recv, peer):
    copy = pltpu.make_async_remote_copy(
        src_ref=source, dst_ref=target, send_sem=send, recv_sem=recv,
        device_id=peer, device_id_type=MESH,
    )
    copy.start()
    return copy


def arrive(copies):
    for copy in copies:
        copy.wait_recv()


def finish(copies):
    for copy in copies:
        copy.wait_send()


def mean(values):
    return jnp.mean(values, -1, keepdims=True)


def total(values):
    return jnp.sum(values, 0, keepdims=True)


def lane_slice(e, half):
    return pl.ds(half * e.z.lanes, e.z.lanes)


def clear_padding(e, buffer):
    z = e.z
    start = chunk_rows(z, 1) // 16 * 16
    for c in range(1, z.chunks, 2):
        if start < z.chunk:
            buffer[c, start:] = jnp.zeros_like(buffer[c, start:])


def field_rows(e, source, c, start, size):
    z = e.z
    first = ((c % 2) * z.chunk + start) // z.fields
    return source[c // 2, first : first + size // z.fields].reshape(size, z.channels)


def to_slots(e, source, table, slots, half):
    z = e.z
    for p in range(z.planes):
        rows = source[2 * p : 2 * p + 2, :, lane_slice(e, half)].reshape(z.pitch, z.lanes)
        e.columns[half, p] = dot(table, rows).astype(narrow)
    moved = dot(e.slot_rows[...], e.columns[half].reshape(z.planes * z.group, z.lanes))
    moved = moved.astype(narrow)
    for d in range(z.n_sp):
        slots[half, d] = moved[d * z.slot : (d + 1) * z.slot]


def send_slots(e, slots, landed, send, recv, half):
    copies = [
        remote(
            slots.at[half, peer[0]], landed.at[half, e.sp],
            send.at[half, i], recv.at[half, i], peer,
        )
        for i, peer in enumerate(e.sp_peers)
    ]
    landed[half, e.sp] = slots[half, e.sp]
    return copies


def arrived_slots(e, landed, copies, half):
    arrive(copies)
    z = e.z
    rows = landed[half].astype(wide).reshape(z.n_sp * z.slot, z.lanes)
    return rows.astype(narrow)


def modes_from_slots(e, rows):
    z = e.z
    real = dot(e.lat[: z.count], rows)
    imag = dot(e.lat[z.count :], rows)
    return jnp.concatenate([real, imag], 1)


def slots_from_modes(e, values, slots, half):
    z = e.z
    stacked = jnp.concatenate([values[:, : z.lanes], values[:, z.lanes :]], 0)
    moved = dot(e.lat_cols[...], stacked).astype(narrow)
    for d in range(z.n_sp):
        slots[half, d] = moved[d * z.slot : (d + 1) * z.slot]


def gather_start(e, rows, gathered, sems, half):
    z = e.z
    send_y, recv_y, send_core, recv_core = sems
    ordered = dot(e.slot_cols[...], rows).astype(narrow)
    for p in range(z.planes):
        gathered[half, p, e.wa] = ordered[p * z.group : (p + 1) * z.group]
    own = gathered.at[half, :, e.wa]
    copies_y = [
        remote(own, own, send_y.at[half, j], recv_y.at[half, j], peer)
        for j, peer in enumerate(e.y_peers)
    ]
    copies_core = [remote(own, own, send_core.at[half, 0], recv_core.at[half, 0], e.sibling)]
    return copies_y, copies_core


def gather_forward(e, copies, gathered, sems, half):
    z = e.z
    send_y, recv_y, send_core, recv_core = sems
    copies_y, copies_core = copies
    for j, copy in enumerate(copies_y):
        copy.wait_recv()
        origin = lax.rem(e.wa + z.n_wa - 2 * (j + 1), z.n_wa)
        slab = gathered.at[half, :, origin]
        copies_core.append(
            remote(slab, slab, send_core.at[half, j + 1], recv_core.at[half, j + 1], e.sibling)
        )
    arrive(copies_core)


def plane_from_gathered(e, table, gathered, half, p):
    z = e.z
    return dot(table, gathered[half, p].reshape(z.n_wa * z.group, z.lanes))


def pack_weights(e):
    z = e.z
    for i in range(z.own_blocks):
        at = e.wa * z.own_blocks + i
        e.packed[at, : 2 * z.block] = e.w1[i]
        e.packed[at, 2 * z.block : 4 * z.block] = e.w2[i]
        line = lax.broadcasted_iota(jnp.int32, (16, z.block), 0)
        bias = jnp.zeros((16, z.block), wide)
        for k in range(2):
            bias = jnp.where(line == k, e.b1[i, k : k + 1].astype(wide), bias)
            bias = jnp.where(line == 2 + k, e.b2[i, k : k + 1].astype(wide), bias)
        e.packed[at, 4 * z.block : 4 * z.block + 16] = bias.astype(narrow)


def send_weights(e, send, recv):
    z = e.z
    own = e.packed.at[pl.ds(e.wa * z.own_blocks, z.own_blocks)]
    return [
        remote(own, own, send.at[j], recv.at[j], peer) for j, peer in enumerate(e.wa_peers)
    ]


def spread(z, index):
    row = lax.broadcasted_iota(jnp.int32, (z.block, z.lanes), 0)
    lane = lax.broadcasted_iota(jnp.int32, (z.block, z.lanes), 1)
    return jnp.where(lane == row + index * z.block, 1.0, 0.0).astype(narrow)


def build_weights(e):
    z = e.z
    n, lanes = z.block, z.lanes
    for half in range(halves):
        bias = jnp.zeros((16, lanes), wide)
        for i in range(z.half_blocks):
            source = e.packed[half * z.half_blocks + i, : 4 * n + 16]
            placed = dot(source, spread(z, i))
            bias = bias + placed[4 * n :]
            for k, target in ((0, e.big1), (1, e.big2)):
                real = placed[2 * k * n : (2 * k + 1) * n]
                imag = placed[(2 * k + 1) * n : (2 * k + 2) * n]
                up, down = pl.ds(i * n, n), pl.ds(lanes + i * n, n)
                target[half, up, :lanes] = real.astype(narrow)
                target[half, up, lanes:] = imag.astype(narrow)
                target[half, down, :lanes] = (-imag).astype(narrow)
                target[half, down, lanes:] = real.astype(narrow)
        e.bias[half] = bias


def modes_forward(e, rows, half):
    z = e.z
    spec = modes_from_slots(e, rows).astype(narrow)
    e.spec[half] = spec
    bias = e.bias[half]
    bias1 = jnp.concatenate([bias[0:1], bias[1:2]], 1)
    bias2 = jnp.concatenate([bias[2:3], bias[3:4]], 1)
    hid, slope = gelu_with_slope(dot(spec, e.big1[half]) + bias1)
    e.slope1[half] = slope
    hid = hid.astype(narrow)
    e.hid[half] = hid
    two = dot(hid, e.big2[half]) + bias2
    bent = jnp.tanh(two * (1.0 / threshold))
    e.slope2[half] = bent * bent
    return (two - threshold * bent).astype(narrow)


def modes_backward(e, rows, half):
    z = e.z
    grad_two = (modes_from_slots(e, rows) * e.slope2[half]).astype(narrow)
    e.grad_two[half] = grad_two
    grad_hid = dot_right_transposed(grad_two, e.big2[half])
    grad_one = (grad_hid * e.slope1[half]).astype(narrow)
    e.grad_one[half] = grad_one
    return dot_right_transposed(grad_one, e.big1[half]).astype(narrow)


def outer_parts(z, left, right):
    lanes = z.lanes
    product = dot_left_transposed(left, right)
    real = product[:lanes, :lanes] + product[lanes:, lanes:]
    imag = product[:lanes, lanes:] - product[lanes:, :lanes]
    return real.astype(narrow), imag.astype(narrow)


def spectral_grads(e, half):
    z = e.z
    n, lanes = z.block, z.lanes
    real1, imag1 = outer_parts(z, e.spec[half], e.grad_one[half])
    real2, imag2 = outer_parts(z, e.hid[half], e.grad_two[half])
    bias1 = jnp.sum(e.grad_one[half].astype(wide), 0, keepdims=True)
    bias2 = jnp.sum(e.grad_two[half].astype(wide), 0, keepdims=True)
    line = lax.broadcasted_iota(jnp.int32, (16, lanes), 0)
    bias = jnp.zeros((16, lanes), wide)
    for k, row in enumerate((bias1[:, :lanes], bias1[:, lanes:], bias2[:, :lanes], bias2[:, lanes:])):
        bias = jnp.where(line == k, row, bias)
    bias = bias.astype(narrow)
    for i in range(z.half_blocks):
        at = half * z.half_blocks + i
        owner = at // z.own_blocks
        target = e.grad_pack.at[owner // 2, owner % 2, at % z.own_blocks]
        parts = [value[i * n : (i + 1) * n] for value in (real1, imag1, real2, imag2)]
        stacked = jnp.concatenate(parts + [bias], 0)
        target[: 4 * n + 16] = dot_right_transposed(stacked, spread(z, i)).astype(narrow)
        if z.pack > 4 * n + 16:
            target[4 * n + 16 :] = jnp.zeros((z.pack - 4 * n - 16, n), narrow)


class WaSum:
    def __init__(self, e, name, partial):
        self.e, self.partial = e, partial
        for part in ("recv_core", "slots_y", "done"):
            setattr(self, part, getattr(e, name + "_" + part))
        self.sems = {
            part: getattr(e, name + "_" + part)
            for part in ("ss_core", "rs_core", "ss_y", "rs_y", "ss_done", "rs_done")
        }
        self.core, self.y, self.last = {}, {}, {}

    def own(self):
        part = self.e.z.part
        return pl.ds(pl.multiple_of(self.e.core * part, 16), part)

    def other(self):
        part = self.e.z.part
        return pl.ds(pl.multiple_of((1 - self.e.core) * part, 16), part)

    def start(self, c, values):
        e, s = self.e, self.sems
        self.partial[c] = values.astype(narrow)
        self.core[c] = remote(
            self.partial.at[c, self.other()], self.recv_core.at[c],
            s["ss_core"].at[c], s["rs_core"].at[c], e.sibling,
        )

    def middle(self, c):
        e, s = self.e, self.sems
        self.core[c].wait_recv()
        both = self.partial[c, self.own()].astype(wide) + self.recv_core[c].astype(wide)
        self.slots_y[c, e.y] = both.astype(narrow)
        slot = self.slots_y.at[c, e.y]
        self.y[c] = [
            remote(slot, slot, s["ss_y"].at[c, j], s["rs_y"].at[c, j], peer)
            for j, peer in enumerate(e.y_peers)
        ]

    def end(self, c):
        e, s = self.e, self.sems
        arrive(self.y[c])
        value = self.slots_y[c, 0].astype(wide)
        for k in range(1, e.z.n_y):
            value = value + self.slots_y[c, k].astype(wide)
        self.done[c, self.own()] = value.astype(narrow)
        rows = self.done.at[c, self.own()]
        self.last[c] = remote(rows, rows, s["ss_done"].at[c], s["rs_done"].at[c], e.sibling)

    def value(self, c):
        self.last[c].wait_recv()

    def finish(self):
        for c in self.y:
            finish(self.y[c])
        finish(self.last.values())


def wa_sum_scratch(s, z, name):
    s.vmem(name + "_recv_core", (z.chunks, z.part, z.channels))
    s.vmem(name + "_slots_y", (z.chunks, z.n_y, z.part, z.channels))
    s.vmem(name + "_done", (z.chunks, z.chunk, z.channels))
    for part in ("ss_core", "rs_core", "ss_done", "rs_done"):
        s.dma(name + "_" + part, (z.chunks,))
    for part in ("ss_y", "rs_y"):
        s.dma(name + "_" + part, (z.chunks, max(z.n_y - 1, 1)))


def cube_levels(rows, n_sp):
    levels, bit = [], 1
    while bit < n_sp:
        halve = rows % 32 == 0
        rows = rows // 2 if halve else rows
        levels.append((bit, halve, rows))
        bit *= 2
    return levels


class CubeSum:
    def __init__(self, e, block, landed, out, send, recv, chunk):
        self.e, self.block, self.landed, self.out = e, block, landed, out
        self.send, self.recv, self.chunk = send, recv, chunk
        self.rows = block.shape[0]
        self.levels = cube_levels(self.rows, e.z.n_sp)
        self.start, self.size = 0, self.rows
        self.step, self.copies, self.spans = 0, [], []
        self.steps = self.begin()

    def peer(self, bit):
        e = self.e
        mine = lax.rem(lax.div(e.sp, bit), 2)
        return mine, (e.sp + bit - 2 * bit * mine, e.wa)

    def rows_at(self, start, size):
        return pl.ds(pl.multiple_of(start, 16), size)

    def post(self, source, target, peer):
        k = self.step
        self.step += 1
        copy = remote(source, target, self.send.at[self.chunk, k], self.recv.at[self.chunk, k], peer)
        self.copies.append(copy)
        return copy

    def begin(self):
        offset = 0
        for bit, halve, size in self.levels:
            mine, peer = self.peer(bit)
            self.spans.append((bit, halve, self.start, self.size))
            if halve:
                keep = self.start + mine * size
                give = self.start + (1 - mine) * size
            else:
                keep = give = self.start
            target = self.landed.at[offset : offset + size]
            copy = self.post(self.block.at[self.rows_at(give, size)], target, peer)
            yield
            copy.wait_recv()
            own = self.rows_at(keep, size)
            value = self.block[own].astype(wide) + target[...].astype(wide)
            if not halve:
                copy.wait_send()
            self.block[own] = value.astype(narrow)
            self.start, self.size = keep, size
            offset += size
        own = self.rows_at(self.start, self.size)
        self.out[own] = self.block[own]
        for bit, halve, start, size in reversed(self.spans):
            if halve:
                mine, peer = self.peer(bit)
                rows = self.out.at[self.rows_at(self.start, self.size)]
                copy = self.post(rows, rows, peer)
                yield
                copy.wait_recv()
            self.start, self.size = start, size

    def advance(self):
        return next(self.steps, None)

    def drain(self):
        for _ in self.steps:
            pass
        finish([copy for k, copy in enumerate(self.copies) if not self.waited(k)])

    def waited(self, k):
        return k < len(self.levels) and not self.levels[k][1]


def cube_landed_rows(rows, n_sp):
    return sum(size for _, _, size in cube_levels(rows, n_sp))


class Background:
    def __init__(self):
        self.items = []

    def step(self, count=1):
        for _ in range(count):
            for item in self.items:
                next(item.steps, None)


def exchange_small(e, own, landed, send, recv):
    landed[e.sp] = own
    slot = landed.at[e.sp]
    return [
        remote(slot, slot, send.at[i], recv.at[i], peer) for i, peer in enumerate(e.sp_peers)
    ]


def sum_small(e, landed, copies):
    arrive(copies)
    value = landed[0]
    for k in range(1, e.z.n_sp):
        value = value + landed[k]
    return value


def place_rows(rows, width):
    line = lax.broadcasted_iota(jnp.int32, (8, width), 0)
    result = jnp.zeros((8, width), wide)
    for k, row in rows:
        if row.shape[1] < width:
            row = jnp.concatenate([row, jnp.zeros((1, width - row.shape[1]), wide)], 1)
        result = jnp.where(line == k, row, result)
    return result


def spec_sum_start(e):
    z = e.z
    return [
        remote(
            e.grad_pack.at[:, 1 - e.core], e.pack_core, e.ss_pack.at[0], e.rs_pack.at[0], e.sibling
        )
    ]


def spec_sum_middle(e, copies):
    z = e.z
    arrive(copies)
    for k in range(z.n_y):
        both = e.grad_pack[k, e.core].astype(wide) + e.pack_core[k].astype(wide)
        e.pack_send[k] = both.astype(narrow)
    new = [
        remote(
            e.pack_send.at[lax.rem(e.y + j + 1, z.n_y)], e.pack_y.at[e.y],
            e.ss_pack.at[1 + j], e.rs_pack.at[1 + j], peer,
        )
        for j, peer in enumerate(e.y_peers)
    ]
    e.pack_y[e.y] = e.pack_send[e.y]
    return new


def spec_sum_scatter(e, copies):
    z = e.z
    arrive(copies)
    value = e.pack_y[0].astype(wide)
    for k in range(1, z.n_y):
        value = value + e.pack_y[k].astype(wide)
    e.pack_sum[...] = value.reshape(z.n_sp, z.pack_share, z.block).astype(narrow)
    e.pack_landed[e.sp] = e.pack_sum[e.sp]
    return [
        remote(
            e.pack_sum.at[peer[0]], e.pack_landed.at[e.sp],
            e.ss_share.at[i], e.rs_share.at[i], peer,
        )
        for i, peer in enumerate(e.sp_peers)
    ]


def spec_sum_gather(e, copies):
    z = e.z
    arrive(copies)
    value = e.pack_landed[0].astype(wide)
    for k in range(1, z.n_sp):
        value = value + e.pack_landed[k].astype(wide)
    e.pack_out[e.sp] = value.astype(narrow)
    slot = e.pack_out.at[e.sp]
    return [
        remote(slot, slot, e.ss_whole.at[i], e.rs_whole.at[i], peer)
        for i, peer in enumerate(e.sp_peers)
    ]


def first_norm(e, c):
    gain, shift = e.gain1[...], e.shift1[...]
    for start, size in row_parts(e.z, c):
        values = field_rows(e, e.xs, c, start, size).astype(wide)
        center = mean(values)
        centred = values - center
        inv_std = lax.rsqrt(mean(centred * centred) + 1e-05)
        rows = pl.ds(start, size)
        e.xn[c, rows] = (centred * inv_std * gain + shift).astype(narrow)
        e.stats[c, rows, 0:1] = center
        e.stats[c, rows, 1:2] = inv_std


def second_norm(e, c):
    gain, shift = e.gain2[...], e.shift2[...]
    for start, size in row_parts(e.z, c):
        rows = pl.ds(start, size)
        values = e.mixed[c, rows]
        center = mean(values)
        centred = values - center
        inv_std = lax.rsqrt(mean(centred * centred) + 1e-05)
        e.xn2[c, rows] = (centred * inv_std * gain + shift).astype(narrow)
        e.stats[c, rows, 2:3] = center
        e.stats[c, rows, 3:4] = inv_std


def second_norm_backward(e, c, gain_grad, shift_grad):
    gain = e.gain2[...]
    for start, size in row_parts(e.z, c):
        rows = pl.ds(start, size)
        grad = e.grads_done[c, rows].astype(wide)
        inv_std = e.stats[c, rows, 3:4]
        hat = (e.mixed[c, rows] - e.stats[c, rows, 2:3]) * inv_std
        gain_grad = gain_grad + total(grad * hat)
        shift_grad = shift_grad + total(grad)
        scaled = grad * gain
        back = inv_std * (scaled - mean(scaled) - hat * mean(scaled * hat))
        e.xn[c, rows] = (e.gp[c, rows].astype(wide) + back).astype(narrow)
    return gain_grad, shift_grad


def first_norm_sums(e, half):
    lanes = lane_slice(e, half)
    gain_grad = jnp.zeros((1, e.z.lanes), wide)
    shift_grad = jnp.zeros((1, e.z.lanes), wide)
    for c in range(e.z.chunks):
        for start, size in row_parts(e.z, c):
            rows = pl.ds(start, size)
            grad = e.xn2[c, rows, lanes].astype(wide)
            values = field_rows(e, e.xs, c, start, size)
            values = values[:, half * e.z.lanes : (half + 1) * e.z.lanes].astype(wide)
            hat = (values - e.stats[c, rows, 0:1]) * e.stats[c, rows, 1:2]
            gain_grad = gain_grad + total(grad * hat)
            shift_grad = shift_grad + total(grad)
    return gain_grad, shift_grad


def first_norm_backward(e, c):
    gain = e.gain1[...]
    for start, size in row_parts(e.z, c):
        rows = pl.ds(start, size)
        grad = e.xn2[c, rows].astype(wide)
        inv_std = e.stats[c, rows, 1:2]
        values = field_rows(e, e.xs, c, start, size).astype(wide)
        hat = (values - e.stats[c, rows, 0:1]) * inv_std
        scaled = grad * gain
        back = inv_std * (scaled - mean(scaled) - hat * mean(scaled * hat))
        e.mixed[c, rows] = e.xn[c, rows].astype(wide) + back


def chunk_target(e, target, c):
    rows = chunk_rows(e.z, c)
    return target.at[c // 2, pl.ds((c % 2) * e.z.chunk, rows)], rows


def write_chunk(e, target, sem, c):
    place_at, rows = chunk_target(e, target, c)
    copy = pltpu.make_async_copy(e.mixed.at[c, pl.ds(0, rows)], place_at, sem.at[c])
    copy.start()
    return copy


def whole_body(e):
    z = e.z
    chunks = range(z.chunks)
    x_loads = [
        pltpu.make_async_copy(e.hbm_x.at[p], e.xs.at[p], e.load_x.at[p]) for p in range(z.planes)
    ]
    loads = [
        pltpu.make_async_copy(e.hbm_g.at[0], e.gs.at[0], e.load.at[0]),
        pltpu.make_async_copy(e.hbm_fc1, e.fc1, e.load.at[1]),
        pltpu.make_async_copy(e.hbm_fc2, e.fc2, e.load.at[2]),
    ]
    for load in x_loads + loads:
        load.start()
    greet(e)
    pack_weights(e)
    clear_padding(e, e.xn)
    clear_padding(e, e.xn2)
    clear_padding(e, e.gp)
    for c in chunks:
        if c % 2 == 0:
            x_loads[c // 2].wait()
        first_norm(e, c)
    greeted(e)
    weights = send_weights(e, e.send_w, e.recv_w)

    table = e.long_rows[0, e.wa]
    first, second, gathers = [], [], []
    for half in range(halves):
        to_slots(e, e.xn, table, e.slots_a, half)
        first.append(send_slots(e, e.slots_a, e.landed_a, e.send_a, e.recv_a, half))
    for load in loads:
        load.wait()
    bias2_grad = jnp.zeros((1, z.channels), wide)
    for c in chunks:
        for start, size in row_parts(z, c):
            values = field_rows(e, e.gs, c % 2, start, size)
            e.gp[c, start : start + size] = values
            bias2_grad = bias2_grad + total(values.astype(wide))
        if c % 2 == 1 and c // 2 + 1 < z.planes:
            load = pltpu.make_async_copy(e.hbm_g.at[c // 2 + 1], e.gs.at[0], e.load.at[0])
            load.start()
            load.wait()
    arrive(weights)
    build_weights(e)
    for half in range(halves):
        rows = arrived_slots(e, e.landed_a, first[half], half)
        slots_from_modes(e, modes_forward(e, rows, half), e.slots_b, half)
        second.append(send_slots(e, e.slots_b, e.landed_b, e.send_b, e.recv_b, half))
    sems = (e.send_y, e.recv_y, e.send_core, e.recv_core)
    for half in range(halves):
        rows = arrived_slots(e, e.landed_b, second[half], half)
        gathers.append(gather_start(e, rows, e.gathered, sems, half))
    for half in range(halves):
        gather_forward(e, gathers[half], e.gathered, sems, half)
        lanes = lane_slice(e, half)
        for p in range(z.planes):
            filtered = plane_from_gathered(e, e.long_out[1], e.gathered, half, p)
            for c in (2 * p, 2 * p + 1):
                size = chunk_rows(z, c)
                at = (c % 2) * z.chunk
                values = field_rows(e, e.xs, c, 0, size)
                values = values[:, half * z.lanes : (half + 1) * z.lanes].astype(wide)
                step = filtered[at : at + size].astype(narrow).astype(wide)
                e.mixed[c, pl.ds(0, size), lanes] = values + step
    for copies in first + second:
        finish(copies)
    for pair in gathers:
        finish(pair[0] + pair[1])
    finish(weights)

    grads = WaSum(e, "grads", e.xn)
    bias1 = e.fc1_bias[...].astype(wide)
    bias1_grad = jnp.zeros((1, z.hidden), wide)
    for c in chunks:
        second_norm(e, c)
        hidden, slope = gelu_with_slope(dot(e.xn2[c], e.fc1[...]) + bias1)
        e.act[c] = hidden.astype(narrow)
        grad_hidden = (dot_right_transposed(e.gp[c], e.fc2[...]) * slope).astype(narrow)
        e.gh[c] = grad_hidden
        bias1_grad = bias1_grad + total(grad_hidden.astype(wide))
        grads.start(c, dot_right_transposed(grad_hidden, e.fc1[...]))
        if c >= 1:
            grads.middle(c - 1)
    grads.middle(z.chunks - 1)

    all_rows = z.chunks * z.chunk
    background = Background()
    sources = (
        (e.xn2, e.gh, e.sum1, e.landed1, e.out_fc1, z.channels),
        (e.act, e.gp, e.sum2, e.landed2, e.out_fc2, z.hidden),
    )
    cubes = []
    for index, (left, right, block, landed, out, rows) in enumerate(sources):
        size = rows // 2
        for k in range(2):
            part = left[:, :, k * size : (k + 1) * size].reshape(all_rows, size)
            value = dot_left_transposed(part, right[...].reshape(all_rows, right.shape[-1]))
            block[k] = value.astype(narrow)
            cube = CubeSum(
                e, block.at[k], landed.at[k], out.at[pl.ds(k * size, size)],
                e.send_cube, e.recv_cube, 2 * index + k,
            )
            cube.advance()
            cubes.append(cube)
    background.items = cubes

    gain2_grad = jnp.zeros((1, z.channels), wide)
    shift2_grad = jnp.zeros((1, z.channels), wide)
    for c in chunks:
        grads.end(c)
        if c >= 1:
            grads.value(c - 1)
            finish([grads.core[c - 1]])
            gain2_grad, shift2_grad = second_norm_backward(e, c - 1, gain2_grad, shift2_grad)
        if c % 2 == 1:
            background.step()
    grads.value(z.chunks - 1)
    finish([grads.core[z.chunks - 1]])
    gain2_grad, shift2_grad = second_norm_backward(e, z.chunks - 1, gain2_grad, shift2_grad)

    table = e.long_rows[1, e.wa]
    third, fourth, back_gathers = [], [], []
    for half in range(halves):
        to_slots(e, e.xn, table, e.slots_a, half)
        third.append(send_slots(e, e.slots_a, e.landed_c, e.send_c, e.recv_c, half))
    branch = WaSum(e, "branch", e.xn2)
    for c in chunks:
        branch.start(c, dot(e.act[c], e.fc2[...]))
    rows = [(0, bias1_grad), (1, bias2_grad), (2, gain2_grad), (3, shift2_grad)]
    small_one = exchange_small(
        e, place_rows(rows, z.small), e.small_one, e.send_one, e.recv_one
    )
    for c in chunks:
        branch.middle(c)
    for half in range(halves):
        rows = arrived_slots(e, e.landed_c, third[half], half)
        slots_from_modes(e, modes_backward(e, rows, half), e.slots_b, half)
        fourth.append(send_slots(e, e.slots_b, e.landed_d, e.send_d, e.recv_d, half))
    background.step()
    for half in range(halves):
        spectral_grads(e, half)
    packs = [spec_sum_start(e)]
    sems = (e.send_y2, e.recv_y2, e.send_core2, e.recv_core2)
    for half in range(halves):
        rows = arrived_slots(e, e.landed_d, fourth[half], half)
        back_gathers.append(gather_start(e, rows, e.gathered2, sems, half))
    packs.append(spec_sum_middle(e, packs[-1]))
    background.step()
    writes = []
    bias = e.fc2_bias[...].astype(wide)
    for c in chunks:
        branch.end(c)
    for c in chunks:
        branch.value(c)
        for start, size in row_parts(z, c):
            rows = pl.ds(start, size)
            e.mixed[c, rows] = e.mixed[c, rows] + (e.branch_done[c, rows].astype(wide) + bias)
        writes.append(write_chunk(e, e.hbm_output, e.write_sems, c))
    packs.append(spec_sum_scatter(e, packs[-1]))
    lane_sums = []
    finish(branch.core.values())
    for half in range(halves):
        gather_forward(e, back_gathers[half], e.gathered2, sems, half)
        for p in range(z.planes):
            grad = plane_from_gathered(e, e.long_out[0], e.gathered2, half, p).astype(narrow)
            for c in (2 * p, 2 * p + 1):
                at = (c % 2) * z.chunk
                e.xn2[c, :, lane_slice(e, half)] = grad[at : at + z.chunk]
        lane_sums.append(first_norm_sums(e, half))
        background.step()
    gain1_grad = jnp.concatenate([pair[0] for pair in lane_sums], 1)
    shift1_grad = jnp.concatenate([pair[1] for pair in lane_sums], 1)
    small_two = exchange_small(
        e, place_rows([(0, gain1_grad), (1, shift1_grad)], z.small),
        e.small_two, e.send_two, e.recv_two,
    )
    packs.append(spec_sum_gather(e, packs[-1]))
    for write in writes:
        write.wait()
    writes = []
    for c in chunks:
        first_norm_backward(e, c)
        writes.append(write_chunk(e, e.hbm_fields_grad, e.write_sems, c))
    background.step()
    arrive(packs[-1])
    e.small_out[0] = sum_small(e, e.small_one, small_one)
    e.small_out[1] = sum_small(e, e.small_two, small_two)
    for cube in cubes:
        cube.drain()
    for copies in third + fourth + packs + [small_one, small_two]:
        finish(copies)
    for pair in back_gathers:
        finish(pair[0] + pair[1])
    grads.finish()
    branch.finish()
    for write in writes:
        write.wait()


class Names:
    def __init__(self):
        self.names, self.shapes = [], []

    def add(self, name, shape):
        self.names.append(name)
        self.shapes.append(shape)

    def vmem(self, name, shape, dtype=narrow):
        self.add(name, pltpu.VMEM(shape, dtype))

    def dma(self, name, shape):
        self.add(name, pltpu.SemaphoreType.DMA(shape))


def scratch_of(z):
    s = Names()
    fields = (z.planes, z.width, z.fields, z.channels)
    rows = (z.chunks, z.chunk, z.channels)
    hidden = (z.chunks, z.chunk, z.hidden)
    s.vmem("xs", fields)
    s.vmem("gs", (1,) + fields[1:])
    s.vmem("fc1", (z.channels, z.hidden))
    s.vmem("fc2", (z.hidden, z.channels))
    s.dma("load_x", (z.planes,))
    s.dma("load", (3,))
    s.dma("write_sems", (z.chunks,))
    for name in ("xn", "gp", "xn2"):
        s.vmem(name, rows)
    s.vmem("act", hidden)
    s.vmem("gh", hidden)
    s.vmem("mixed", rows, wide)
    s.vmem("stats", (z.chunks, z.chunk, 4), wide)
    s.vmem("columns", (halves, z.planes, z.group, z.lanes))
    for name in ("slots_a", "slots_b", "landed_a", "landed_b", "landed_c", "landed_d"):
        s.vmem(name, (halves, z.n_sp, z.slot, z.lanes))
    for tag in "abcd":
        s.dma("send_" + tag, (halves, z.n_sp - 1))
        s.dma("recv_" + tag, (halves, z.n_sp - 1))
    for tag in ("", "2"):
        s.vmem("gathered" + tag, (halves, z.planes, z.n_wa, z.group, z.lanes))
        for name in ("send_y", "recv_y"):
            s.dma(name + tag, (halves, max(z.n_y - 1, 1)))
        for name in ("send_core", "recv_core"):
            s.dma(name + tag, (halves, z.n_y))
    s.vmem("packed", (z.blocks, z.pack, z.block))
    s.vmem("bias", (halves, 16, z.lanes), wide)
    s.dma("send_w", (z.n_wa - 1,))
    s.dma("recv_w", (z.n_wa - 1,))
    both = (halves, z.count, 2 * z.lanes)
    for name in ("spec", "hid", "grad_one", "grad_two"):
        s.vmem(name, both)
    s.vmem("slope1", both, wide)
    s.vmem("slope2", both, wide)
    for name in ("big1", "big2"):
        s.vmem(name, (halves, 2 * z.lanes, 2 * z.lanes))
    s.vmem("grad_pack", (z.n_y, 2, z.own_blocks, z.pack, z.block))
    for name in ("pack_core", "pack_send", "pack_y"):
        s.vmem(name, (z.n_y, z.own_blocks, z.pack, z.block))
    s.vmem("pack_sum", (z.n_sp, z.pack_share, z.block))
    s.vmem("pack_landed", (z.n_sp, z.pack_share, z.block))
    for name in ("ss_pack", "rs_pack"):
        s.dma(name, (z.n_y,))
    for name in ("ss_share", "rs_share", "ss_whole", "rs_whole"):
        s.dma(name, (z.n_sp - 1,))
    wa_sum_scratch(s, z, "grads")
    wa_sum_scratch(s, z, "branch")
    for tag, rows, lanes in (("1", z.channels, z.hidden), ("2", z.hidden, z.channels)):
        s.vmem("sum" + tag, (2, rows // 2, lanes))
        s.vmem("landed" + tag, (2, cube_landed_rows(rows // 2, z.n_sp), lanes))
    steps = 2 * len(cube_levels(z.channels, z.n_sp))
    s.dma("send_cube", (4, steps))
    s.dma("recv_cube", (4, steps))
    for tag in ("one", "two"):
        s.vmem("small_" + tag, (z.n_sp, 8, z.small), wide)
        s.dma("send_" + tag, (z.n_sp - 1,))
        s.dma("recv_" + tag, (z.n_sp - 1,))
    return s


def call_kernel(body, z, inputs, outputs, scratch, collective):
    names = [name for name, _ in inputs] + [name for name, _, _ in outputs]

    def kernel(*refs):
        e = types.SimpleNamespace(z=z)
        for name, ref in zip(names + scratch.names, refs):
            setattr(e, name, ref)
        place(e)
        body(e)

    def spec(name):
        return pl.BlockSpec(memory_space=pl.ANY if name.startswith("hbm_") else pltpu.VMEM)

    return pl.pallas_call(
        kernel,
        out_shape=[jax.ShapeDtypeStruct(shape, dtype) for _, shape, dtype in outputs],
        in_specs=[spec(name) for name, _ in inputs],
        out_specs=[spec(name) for name, _, _ in outputs],
        scratch_shapes=scratch.shapes,
        compiler_params=pltpu.CompilerParams(
            collective_id=collective, has_side_effects=True, vmem_limit_bytes=60 * 1024 * 1024
        ),
    )(*[value for _, value in inputs])


def local(
    fields_in,
    norm1_gain,
    norm1_shift,
    spec_w1,
    spec_b1,
    spec_w2,
    spec_b2,
    norm2_gain,
    norm2_shift,
    fc1_weight,
    fc1_bias,
    fc2_weight,
    fc2_bias,
    out_grad,
):
    fields, rows_here, width, channels = fields_in.shape
    n_sp, n_wa = lax.axis_size("sp"), lax.axis_size("wa")
    block, hidden = spec_w1.shape[2], fc1_weight.shape[1]
    z = plan(
        n_sp, n_wa, fields, rows_here, width, channels, channels // block, block, hidden
    )
    long_rows, long_out = longitude_tables(z)
    index, lat = slot_index(z), latitude_table(z)
    tables = [
        jnp.asarray(np.ascontiguousarray(table))
        for table in (long_rows, long_out, index, index.T, lat, lat.T)
    ]
    own, n = z.own_blocks, block
    line = lambda value: value.reshape(1, -1)
    turned = lambda value: jnp.transpose(value, (1, 2, 0, 3))
    inputs = [
        ("hbm_x", turned(fields_in)), ("hbm_g", turned(out_grad)),
        ("hbm_fc1", fc1_weight), ("hbm_fc2", fc2_weight),
        ("gain1", line(norm1_gain)), ("shift1", line(norm1_shift)),
        ("gain2", line(norm2_gain)), ("shift2", line(norm2_shift)),
        ("fc1_bias", line(fc1_bias)), ("fc2_bias", line(fc2_bias)),
        ("w1", spec_w1.reshape(own, 2 * n, n)), ("b1", spec_b1),
        ("w2", spec_w2.reshape(own, 2 * n, n)), ("b2", spec_b2),
    ] + list(zip(("long_rows", "long_out", "slot_rows", "slot_cols", "lat", "lat_cols"), tables))
    flat = (z.planes, z.plane, channels)
    outputs = [
        ("hbm_output", flat, wide), ("hbm_fields_grad", flat, wide),
        ("out_fc1", (channels, hidden), narrow), ("out_fc2", (hidden, channels), narrow),
        ("pack_out", (z.n_sp, z.pack_share, n), narrow), ("small_out", (2, 8, z.small), wide),
    ]
    output, fields_grad, fc1_grad, fc2_grad, pack, small = call_kernel(
        whole_body, z, inputs, outputs, scratch_of(z), 0
    )
    back = lambda value: jnp.transpose(
        value.reshape(rows_here, width, fields, channels), (2, 0, 1, 3)
    )
    pack = pack.reshape(own, z.pack, n).astype(wide)
    return (
        back(output),
        back(fields_grad),
        small[1, 0, :channels],
        small[1, 1, :channels],
        pack[:, : 2 * n].reshape(own, 2, n, n),
        pack[:, 4 * n : 4 * n + 2],
        pack[:, 2 * n : 4 * n].reshape(own, 2, n, n),
        pack[:, 4 * n + 2 : 4 * n + 4],
        small[0, 2, :channels],
        small[0, 3, :channels],
        fc1_grad.astype(wide),
        small[0, 0, :hidden],
        fc2_grad.astype(wide),
        small[0, 1, :channels],
    )


def solution(mesh):
    return jax.shard_map(
        local,
        mesh=mesh,
        in_specs=(
            P(None, "sp", None, None),
            P(),
            P(),
            P("wa", None, None, None),
            P("wa", None, None),
            P("wa", None, None, None),
            P("wa", None, None),
            P(),
            P(),
            P(None, "wa"),
            P("wa"),
            P("wa", None),
            P(),
            P(None, "sp", None, None),
        ),
        out_specs=(
            P(None, "sp", None, None),
            P(None, "sp", None, None),
            P(),
            P(),
            P("wa", None, None, None),
            P("wa", None, None),
            P("wa", None, None, None),
            P("wa", None, None),
            P(),
            P(),
            P(None, "wa"),
            P("wa"),
            P("wa", None),
            P(),
        ),
        check_vma=False,
    )
```

```python
import functools
import math
import types

import jax
import jax.numpy as jnp
import numpy as np
from jax import lax
from jax.experimental import pallas as pl
from jax.experimental.pallas import tpu as pltpu
from jax.sharding import PartitionSpec as P

threshold = 0.01
narrow = jnp.bfloat16
wide = jnp.float32
MESH = pl.DeviceIdType.MESH
halves = 2


def round_up(value, step):
    return -(-value // step) * step


def phase_angles(rows, columns, period):
    product = rows[:, None] * columns[None, :] % period
    return (np.float32(2.0 * math.pi / period) * product.astype(np.float32)).astype(np.float32)


def plan(n_sp, n_wa, fields, rows_here, width, channels, blocks, block, hidden):
    z = types.SimpleNamespace(
        n_sp=n_sp, n_wa=n_wa, n_y=n_wa // 2, width=width, channels=channels, hidden=hidden,
        blocks=blocks, block=block, fields=fields, planes=rows_here,
    )
    z.period = rows_here * n_sp
    z.modes = width // 2 + 1
    z.each = -(-z.modes // (n_sp * n_wa))
    z.plane = fields * width
    z.pitch = round_up(z.plane, 64)
    z.chunk = z.pitch // 2
    z.chunks = 2 * rows_here
    z.part = z.chunk // 2
    z.lanes = channels // halves
    z.slot = round_up(2 * rows_here * fields * z.each, 8)
    z.group = round_up(2 * n_sp * fields * z.each, 16)
    z.count = z.period * fields * z.each
    z.half_blocks = blocks // halves
    z.own_blocks = blocks // n_wa
    z.pack = round_up(4 * block + 16, 16 * n_sp // math.gcd(16 * n_sp, z.own_blocks))
    z.pack_share = z.own_blocks * z.pack // n_sp
    z.small = max(channels, hidden)
    z.plane_slot = round_up(halves * 2 * fields * z.each, 8)
    z.loaded = (
        "w1", "b1", "w2", "b2", "gain1", "shift1", "long_rows", "slot_rows", "gs", "lat", "lat_cols",
        "slot_cols", "long_out", "gain2", "shift2", "fc1", "fc1_bias", "fc2", "fc2_bias",
        "slot_rows3", "lat3",
    )
    return z


def longitude_tables(z):
    angles = phase_angles(np.arange(z.width), np.arange(z.modes), z.width)
    scale = np.float32(1.0 / math.sqrt(z.width))
    padded = z.each * z.n_sp * z.n_wa
    table = np.zeros((2, padded, z.width), np.float32)
    table[0, : z.modes] = (np.cos(angles) * scale).T
    table[1, : z.modes] = (-np.sin(angles) * scale).T
    k = np.arange(padded)
    weights = np.where((k == 0) | (2 * k == z.width), 1.0, 2.0).astype(np.float32)
    both = np.stack([table, table * weights[None, :, None]])
    both = both.reshape(2, 2, z.n_wa, z.n_sp, z.each, z.width).transpose(0, 2, 1, 3, 4, 5)
    rows = np.zeros((2, z.n_wa, 2, z.n_sp, z.fields, z.each, z.width, z.fields), np.float32)
    for f in range(z.fields):
        rows[:, :, :, :, f, :, :, f] = both
    padded = np.zeros((2, z.n_wa, z.group, z.pitch), np.float32)
    used = 2 * z.n_sp * z.fields * z.each
    padded[:, :, :used, : z.plane] = rows.reshape(2, z.n_wa, used, z.plane)
    out = padded.reshape(2, z.n_wa * z.group, z.pitch).transpose(0, 2, 1)
    return padded.astype(narrow), np.ascontiguousarray(out).astype(narrow)


def slot_index(z):
    table = np.zeros((z.n_sp, z.slot, z.planes, z.group), np.float32)
    for d in range(z.n_sp):
        for c in range(2):
            for h in range(z.planes):
                for f in range(z.fields):
                    for j in range(z.each):
                        r = ((c * z.planes + h) * z.fields + f) * z.each + j
                        table[d, r, h, ((c * z.n_sp + d) * z.fields + f) * z.each + j] = 1.0
    return table.reshape(z.n_sp * z.slot, z.planes * z.group).astype(narrow)


def latitude_table(z):
    angles = phase_angles(np.arange(z.period), np.arange(z.period), z.period)
    scale = np.float32(1.0 / math.sqrt(z.period))
    inner = z.fields * z.each
    cosine = (np.cos(angles) * scale).reshape(z.period, z.n_sp, z.planes)
    sine = (np.sin(angles) * scale).reshape(z.period, z.n_sp, z.planes)
    table = np.zeros((2, z.period, inner, z.n_sp, 2, z.planes, inner), np.float32)
    for i in range(inner):
        table[0, :, i, :, 0, :, i] = cosine
        table[0, :, i, :, 1, :, i] = sine
        table[1, :, i, :, 1, :, i] = cosine
        table[1, :, i, :, 0, :, i] = -sine
    padded = np.zeros((2 * z.count, z.n_sp, z.slot), np.float32)
    padded[:, :, : 2 * z.planes * inner] = table.reshape(2 * z.count, z.n_sp, -1)
    return padded.reshape(2 * z.count, z.n_sp * z.slot).astype(narrow)


def plane_tables(z, index, lat):
    used = 2 * z.fields * z.each
    per = z.planes * used
    shape = (z.n_sp, z.slot, z.planes, z.group)
    moved = np.zeros((halves, z.n_sp, z.plane_slot, z.group), narrow)
    turned = np.zeros((halves, 2 * z.count, z.n_sp, z.planes, z.plane_slot), narrow)
    kept = index.reshape(shape)[:, :per, 0].reshape(z.n_sp, 2, z.planes, -1, z.group)[:, :, 0]
    source = lat.reshape(-1, z.n_sp, z.slot)[:, :, :per].reshape(-1, z.n_sp, 2, z.planes, used // 2)
    source = source.transpose(0, 1, 3, 2, 4).reshape(-1, z.n_sp, z.planes, used)
    for half in range(halves):
        rows = slice(half * used, (half + 1) * used)
        moved[half, :, rows] = kept.reshape(z.n_sp, used, z.group)
        turned[half, ..., rows] = source
    return moved.reshape(halves, -1, z.group), turned.reshape(halves, 2 * z.count, -1)


def dot(left, right):
    return jnp.dot(left, right, preferred_element_type=wide)


def dot_right_transposed(left, right):
    return lax.dot_general(left, right, (((1,), (1,)), ((), ())), preferred_element_type=wide)


def dot_left_transposed(left, right):
    return lax.dot_general(left, right, (((0,), (0,)), ((), ())), preferred_element_type=wide)


def gelu_with_slope(v):
    scale = np.float32(math.sqrt(2.0 / math.pi))
    square = v * v
    bent = jnp.tanh(scale * v * (1.0 + 0.044715 * square))
    above = 0.5 + 0.5 * bent
    slope = above + 0.5 * v * (1.0 - bent * bent) * (scale * (1.0 + (3 * 0.044715) * square))
    return v * above, slope


cuts = 3
SWAPPED = (0, 2)
SCHEDULE = {'c0': (0,), 'q1': (0, 1), 'q3': (0,), 'n3': (3, 0), 'm1': (0, 1), 'm4': (0, 4, 5), 's1': (0, 4), 'q4': (3, 1, 5), 'n4': (1,), 'm3': (1,), 'w1': (3, 1), 'o1': (1, 4), 'c2': (2,), 'n1': (2,), 'm2': (3, 4, 2), 'g0': (5, 2), 'o0': (2,), 'f0': (2,), 'c3': (3,), 'n0': (3,), 'l4': (3,), 'q2': (4,), 'q5': (4,), 'l3': (4,), 'n5': (5,), 'o2': (5,), 'f1': (5,)}


def chunk_rows(z, c):
    return min(z.chunk, z.plane - (c % 2) * z.chunk)


def row_parts(z, c, step=48):
    rows = chunk_rows(z, c)
    return [(start, min(step, rows - start)) for start in range(0, rows, step)]


def place(e):
    z = e.z
    sp, wa = lax.axis_index("sp"), lax.axis_index("wa")
    e.sp, e.wa = sp, wa
    e.core, e.y = lax.rem(wa, 2), lax.div(wa, 2)
    e.sibling = (sp, wa + 1 - 2 * e.core)
    e.sp_peers = [(lax.rem(sp + i, z.n_sp), wa) for i in range(1, z.n_sp)]
    e.y_peers = [(sp, lax.rem(wa + 2 * j, z.n_wa)) for j in range(1, z.n_y)]
    e.wa_peers = [(sp, lax.rem(wa + j, z.n_wa)) for j in range(1, z.n_wa)]


def greet(e):
    barrier = pltpu.get_barrier_semaphore()
    for peer in e.sp_peers + e.wa_peers:
        pl.semaphore_signal(barrier, inc=1, device_id=peer, device_id_type=MESH)


def greeted(e):
    barrier = pltpu.get_barrier_semaphore()
    pl.semaphore_wait(barrier, len(e.sp_peers) + len(e.wa_peers))


class Copy:
    def __init__(self, copy):
        self.copy, self.received, self.sent = copy, False, False

    def wait_recv(self):
        if not self.received:
            self.copy.wait_recv()
        self.received = True

    def wait_send(self):
        if not self.sent:
            self.copy.wait_send()
        self.sent = True


class Group:
    def __init__(self, e, sent, landed, send, recv):
        self.ends = {"recv": (landed, recv), "send": (sent, send)}
        e.copies.append(self)

    def wait(self, end):
        if end in self.ends:
            ref, sem = self.ends.pop(end)
            pltpu.make_async_copy(ref, ref, sem).wait()

    def wait_recv(self):
        self.wait("recv")

    def wait_send(self):
        self.wait("send")


def start_remote(source, target, send, recv, peer):
    pltpu.make_async_remote_copy(
        src_ref=source, dst_ref=target, send_sem=send, recv_sem=recv,
        device_id=peer, device_id_type=MESH,
    ).start()


def remote(e, source, target, send, recv, peer):
    copy = pltpu.make_async_remote_copy(
        src_ref=source, dst_ref=target, send_sem=send, recv_sem=recv,
        device_id=peer, device_id_type=MESH,
    )
    copy.start()
    e.copies.append(Copy(copy))
    return e.copies[-1]


def arrive(copies):
    for copy in copies:
        copy.wait_recv()


def finish(copies):
    for copy in copies:
        copy.wait_send()


def line(ref):
    return ref[...].reshape(1, -1)


def local_copy(e, source, target, sem):
    copy = pltpu.make_async_copy(source, target, sem)
    copy.start()
    return copy


def mean(values):
    return jnp.mean(values, -1, keepdims=True)


def total(values):
    return jnp.sum(values, 0, keepdims=True)


def lane_slice(e, half):
    return pl.ds(half * e.z.lanes, e.z.lanes)


def clear_padding(e, buffer):
    z = e.z
    start = chunk_rows(z, 1) // 16 * 16
    for c in range(1, z.chunks, 2):
        if start < z.chunk:
            buffer[c, start:] = jnp.zeros_like(buffer[c, start:])


def field_rows(e, source, c, start, size):
    z = e.z
    first = ((c % 2) * z.chunk + start) // z.fields
    return source[c // 2, first : first + size // z.fields].reshape(size, z.channels)


def to_slots(e, source, table, slots, half):
    z = e.z
    for p in range(z.planes):
        rows = source[2 * p : 2 * p + 2, :, lane_slice(e, half)].reshape(z.pitch, z.lanes)
        e.columns[half, p] = dot(table, rows).astype(narrow)
    moved = dot(e.slot_rows[...], e.columns[half].reshape(z.planes * z.group, z.lanes))
    moved = moved.astype(narrow)
    for d in range(z.n_sp):
        slots[half, d] = moved[d * z.slot : (d + 1) * z.slot]


def others(e):
    return pl.ds(0, e.z.n_sp - 1)


def send_plane(e, table, p):
    z = e.z
    source = e.xn[2 * p : 2 * p + 2].reshape(z.pitch, z.channels)
    columns = dot(table, source).astype(narrow)
    moved = dot(e.slot_rows3[0], columns[:, : z.lanes]) + dot(e.slot_rows3[1], columns[:, z.lanes :])
    moved = moved.astype(narrow)
    for d in range(z.n_sp):
        e.slots_c[d, p] = moved[d * z.plane_slot : (d + 1) * z.plane_slot]
    for peer in e.sp_peers:
        target = e.landed_c.at[e.sp, p]
        start_remote(e.slots_c.at[peer[0], p], target, e.send_c.at[0], e.recv_c.at[0], peer)
    e.landed_c[e.sp, p] = e.slots_c[e.sp, p]
    if p + 1 < z.planes:
        return None
    rest = others(e)
    return Group(e, e.slots_c.at[rest], e.landed_c.at[rest], e.send_c.at[0], e.recv_c.at[0])


def plane_slots(e):
    z = e.z
    rows = e.landed_c[...].astype(wide)
    return rows.reshape(z.n_sp * z.planes * z.plane_slot, z.lanes).astype(narrow)


def send_slots(e, slots, landed, send, recv, half):
    for peer in e.sp_peers:
        start_remote(
            slots.at[half, peer[0]], landed.at[half, e.sp], send.at[half], recv.at[half], peer
        )
    landed[half, e.sp] = slots[half, e.sp]
    rest = others(e)
    return Group(e, slots.at[half, rest], landed.at[half, rest], send.at[half], recv.at[half])


def arrived_slots(e, landed, group, half):
    group.wait_recv()
    z = e.z
    rows = landed[half].astype(wide).reshape(z.n_sp * z.slot, z.lanes)
    return rows.astype(narrow)


def modes_from_slots(e, rows, table):
    z = e.z
    real = dot(table[: z.count], rows)
    imag = dot(table[z.count :], rows)
    return jnp.concatenate([real, imag], 1)


def slots_from_modes(e, values, slots, half):
    z = e.z
    stacked = jnp.concatenate([values[:, : z.lanes], values[:, z.lanes :]], 0)
    moved = dot(e.lat_cols[...], stacked).astype(narrow)
    for d in range(z.n_sp):
        slots[half, d] = moved[d * z.slot : (d + 1) * z.slot]


def gather_start(e, rows, gathered, sems, half):
    z = e.z
    send_y, recv_y, send_core, recv_core = sems
    ordered = dot(e.slot_cols[...], rows).astype(narrow)
    for p in range(z.planes):
        gathered[half, p, e.wa] = ordered[p * z.group : (p + 1) * z.group]
    own = gathered.at[half, :, e.wa]
    copies_y = [
        remote(e, own, own, send_y.at[half, j], recv_y.at[half, j], peer)
        for j, peer in enumerate(e.y_peers)
    ]
    copies_core = [remote(e, own, own, send_core.at[half, 0], recv_core.at[half, 0], e.sibling)]
    return copies_y, copies_core


def gather_forward(e, copies, gathered, sems, half):
    z = e.z
    send_y, recv_y, send_core, recv_core = sems
    copies_y, copies_core = copies
    for j, copy in enumerate(copies_y):
        copy.wait_recv()
        origin = lax.rem(e.wa + z.n_wa - 2 * (j + 1), z.n_wa)
        slab = gathered.at[half, :, origin]
        copies_core.append(
            remote(e, slab, slab, send_core.at[half, j + 1], recv_core.at[half, j + 1], e.sibling)
        )
    arrive(copies_core)


def plane_from_gathered(e, table, gathered, half, p):
    z = e.z
    return dot(table, gathered[half, p].reshape(z.n_wa * z.group, z.lanes))


def pack_weights(e):
    z = e.z
    for i in range(z.own_blocks):
        at = e.wa * z.own_blocks + i
        e.packed[at, : 2 * z.block] = e.w1[i]
        e.packed[at, 2 * z.block : 4 * z.block] = e.w2[i]
        line = lax.broadcasted_iota(jnp.int32, (16, z.block), 0)
        bias = jnp.zeros((16, z.block), wide)
        for k in range(2):
            bias = jnp.where(line == k, e.b1[i, k : k + 1].astype(wide), bias)
            bias = jnp.where(line == 2 + k, e.b2[i, k : k + 1].astype(wide), bias)
        e.packed[at, 4 * z.block : 4 * z.block + 16] = bias.astype(narrow)


def own_weights(e, wa):
    z = e.z
    return e.packed.at[pl.ds(wa * z.own_blocks, z.own_blocks)]


def send_weights(e):
    own = own_weights(e, e.wa)
    peers = [e.sibling] + e.y_peers
    return [
        remote(e, own, own, e.send_w.at[j], e.recv_w.at[j], peer) for j, peer in enumerate(peers)
    ]


def forward_weights(e, copies):
    z = e.z
    arrive(copies[1:])
    more = []
    for j in range(1, z.n_y):
        slab = own_weights(e, lax.rem(e.wa + z.n_wa - 2 * j, z.n_wa))
        at = z.n_y + j - 1
        more.append(remote(e, slab, slab, e.send_w.at[at], e.recv_w.at[at], e.sibling))
    return copies + more


def spread(z, index):
    row = lax.broadcasted_iota(jnp.int32, (z.block, z.lanes), 0)
    lane = lax.broadcasted_iota(jnp.int32, (z.block, z.lanes), 1)
    return jnp.where(lane == row + index * z.block, 1.0, 0.0).astype(narrow)


def build_weights(e):
    z = e.z
    n, lanes = z.block, z.lanes
    for half in range(halves):
        bias = jnp.zeros((16, lanes), wide)
        for i in range(z.half_blocks):
            source = e.packed[half * z.half_blocks + i, : 4 * n + 16]
            placed = dot(source, spread(z, i))
            bias = bias + placed[4 * n :]
            for k, target in ((0, e.big1), (1, e.big2)):
                real = placed[2 * k * n : (2 * k + 1) * n]
                imag = placed[(2 * k + 1) * n : (2 * k + 2) * n]
                up, down = pl.ds(i * n, n), pl.ds(lanes + i * n, n)
                target[half, up, :lanes] = real.astype(narrow)
                target[half, up, lanes:] = imag.astype(narrow)
                target[half, down, :lanes] = (-imag).astype(narrow)
                target[half, down, lanes:] = real.astype(narrow)
        e.bias[half] = bias


def modes_forward(e, rows, half):
    z = e.z
    spec = modes_from_slots(e, rows, e.lat).astype(narrow)
    e.spec[half] = spec
    bias = e.bias[half]
    bias1 = jnp.concatenate([bias[0:1], bias[1:2]], 1)
    bias2 = jnp.concatenate([bias[2:3], bias[3:4]], 1)
    hid, slope = gelu_with_slope(dot(spec, e.big1[half]) + bias1)
    e.slope1[half] = slope
    hid = hid.astype(narrow)
    e.hid[half] = hid
    two = dot(hid, e.big2[half]) + bias2
    bent = jnp.tanh(two * (1.0 / threshold))
    e.slope2[half] = bent * bent
    return (two - threshold * bent).astype(narrow)


def modes_backward(e, rows, half):
    z = e.z
    grad_two = (modes_from_slots(e, rows, e.lat3[half]) * e.slope2[half]).astype(narrow)
    e.grad_two[half] = grad_two
    grad_hid = dot_right_transposed(grad_two, e.big2[half])
    grad_one = (grad_hid * e.slope1[half]).astype(narrow)
    e.grad_one[half] = grad_one
    return dot_right_transposed(grad_one, e.big1[half]).astype(narrow)


def outer_parts(z, left, right):
    lanes = z.lanes
    product = dot_left_transposed(left, right)
    real = product[:lanes, :lanes] + product[lanes:, lanes:]
    imag = product[:lanes, lanes:] - product[lanes:, :lanes]
    return real.astype(narrow), imag.astype(narrow)


def spectral_grads(e, half):
    z = e.z
    n, lanes = z.block, z.lanes
    real1, imag1 = outer_parts(z, e.spec[half], e.grad_one[half])
    real2, imag2 = outer_parts(z, e.hid[half], e.grad_two[half])
    bias1 = jnp.sum(e.grad_one[half].astype(wide), 0, keepdims=True)
    bias2 = jnp.sum(e.grad_two[half].astype(wide), 0, keepdims=True)
    line = lax.broadcasted_iota(jnp.int32, (16, lanes), 0)
    bias = jnp.zeros((16, lanes), wide)
    for k, row in enumerate((bias1[:, :lanes], bias1[:, lanes:], bias2[:, :lanes], bias2[:, lanes:])):
        bias = jnp.where(line == k, row, bias)
    bias = bias.astype(narrow)
    for i in range(z.half_blocks):
        at = half * z.half_blocks + i
        owner = at // z.own_blocks
        target = e.grad_pack.at[owner // 2, owner % 2, at % z.own_blocks]
        parts = [value[i * n : (i + 1) * n] for value in (real1, imag1, real2, imag2)]
        stacked = jnp.concatenate(parts + [bias], 0)
        target[: 4 * n + 16] = dot_right_transposed(stacked, spread(z, i)).astype(narrow)
        if z.pack > 4 * n + 16:
            target[4 * n + 16 :] = jnp.zeros((z.pack - 4 * n - 16, n), narrow)


class WaSum:
    def __init__(self, e, name, partial):
        self.e, self.partial = e, partial
        for part in ("recv_core", "slots_y", "done"):
            setattr(self, part, getattr(e, name + "_" + part))
        self.sems = {
            part: getattr(e, name + "_" + part)
            for part in ("ss_core", "rs_core", "ss_y", "rs_y", "ss_done", "rs_done")
        }
        self.core, self.y, self.last = {}, {}, {}

    def own(self):
        part = self.e.z.part
        return pl.ds(pl.multiple_of(self.e.core * part, 16), part)

    def other(self):
        part = self.e.z.part
        return pl.ds(pl.multiple_of((1 - self.e.core) * part, 16), part)

    def start(self, c, values):
        e, s = self.e, self.sems
        self.partial[c] = values.astype(narrow)
        self.core[c] = remote(
            e,
            self.partial.at[c, self.other()], self.recv_core.at[c],
            s["ss_core"].at[c], s["rs_core"].at[c], e.sibling,
        )

    def middle(self, c):
        e, s = self.e, self.sems
        self.core[c].wait_recv()
        both = self.partial[c, self.own()].astype(wide) + self.recv_core[c].astype(wide)
        self.slots_y[c, e.y] = both.astype(narrow)
        slot = self.slots_y.at[c, e.y]
        self.y[c] = [
            remote(e, slot, slot, s["ss_y"].at[c, j], s["rs_y"].at[c, j], peer)
            for j, peer in enumerate(e.y_peers)
        ]

    def end(self, c):
        e, s = self.e, self.sems
        arrive(self.y[c])
        value = self.slots_y[c, 0].astype(wide)
        for k in range(1, e.z.n_y):
            value = value + self.slots_y[c, k].astype(wide)
        self.done[c, self.own()] = value.astype(narrow)
        rows = self.done.at[c, self.own()]
        self.last[c] = remote(e, rows, rows, s["ss_done"].at[c], s["rs_done"].at[c], e.sibling)

    def value(self, c):
        self.last[c].wait_recv()


def wa_sum_scratch(s, z, name):
    s.vmem(name + "_recv_core", (z.chunks, z.part, z.channels))
    s.vmem(name + "_slots_y", (z.chunks, z.n_y, z.part, z.channels))
    s.vmem(name + "_done", (z.chunks, z.chunk, z.channels))
    for part in ("ss_core", "rs_core", "ss_done", "rs_done"):
        s.dma(name + "_" + part, (z.chunks,))
    for part in ("ss_y", "rs_y"):
        s.dma(name + "_" + part, (z.chunks, max(z.n_y - 1, 1)))


def cube_levels(rows, n_sp, swap=False):
    bits = [2**k for k in range(n_sp.bit_length() - 1)]
    if swap:
        bits[:2] = bits[1::-1]
    levels = []
    for bit in bits:
        halve = rows % 32 == 0
        rows = rows // 2 if halve else rows
        levels.append((bit, halve, rows))
    return levels


class CubeSum:
    def __init__(self, e, block, landed, out, send, recv, chunk):
        self.e, self.block, self.landed, self.out = e, block, landed, out
        self.send, self.recv, self.chunk = send, recv, chunk
        self.rows = block.shape[0]
        self.levels = cube_levels(self.rows, e.z.n_sp, chunk in SWAPPED)
        self.start, self.size = 0, self.rows
        self.step, self.copies, self.spans = 0, [], []
        self.steps = self.begin()

    def peer(self, bit):
        e = self.e
        mine = lax.rem(lax.div(e.sp, bit), 2)
        return mine, (e.sp + bit - 2 * bit * mine, e.wa)

    def rows_at(self, start, size):
        return pl.ds(pl.multiple_of(start, 16), size)

    def post(self, source, target, peer):
        k = self.step
        self.step += 1
        sems = (self.send.at[self.chunk, k], self.recv.at[self.chunk, k])
        copy = remote(self.e, source, target, *sems, peer)
        self.copies.append(copy)
        return copy

    def begin(self):
        offset = 0
        for bit, halve, size in self.levels:
            mine, peer = self.peer(bit)
            self.spans.append((bit, halve, self.start, self.size))
            if halve:
                keep = self.start + mine * size
                give = self.start + (1 - mine) * size
            else:
                keep = give = self.start
            target = self.landed.at[offset : offset + size]
            copy = self.post(self.block.at[self.rows_at(give, size)], target, peer)
            yield
            copy.wait_recv()
            own = self.rows_at(keep, size)
            value = self.block[own].astype(wide) + target[...].astype(wide)
            if not halve:
                copy.wait_send()
            self.block[own] = value.astype(narrow)
            self.start, self.size = keep, size
            offset += size
        own = self.rows_at(self.start, self.size)
        self.out[own] = self.block[own]
        for bit, halve, start, size in reversed(self.spans):
            if halve:
                mine, peer = self.peer(bit)
                rows = self.out.at[self.rows_at(self.start, self.size)]
                copy = self.post(rows, rows, peer)
                yield
                copy.wait_recv()
            self.start, self.size = start, size

    def advance(self):
        return next(self.steps, None)

    def drain(self):
        for _ in self.steps:
            pass


def cube_landed_rows(rows, n_sp):
    return sum(size for _, _, size in cube_levels(rows, n_sp))


def exchange_small(e, own, landed, send, recv):
    landed[e.sp] = own
    return spread_slot(e, landed, send, recv)


def spread_slot(e, landed, send, recv):
    slot = landed.at[e.sp]
    for peer in e.sp_peers:
        start_remote(slot, slot, send.at[0], recv.at[0], peer)
    rest = others(e)
    return Group(e, landed.at[rest], landed.at[rest], send.at[0], recv.at[0])


def sum_small(e, landed, group):
    group.wait_recv()
    value = landed[0]
    for k in range(1, e.z.n_sp):
        value = value + landed[k]
    return value


def place_rows(rows, width):
    line = lax.broadcasted_iota(jnp.int32, (8, width), 0)
    result = jnp.zeros((8, width), wide)
    for k, row in rows:
        if row.shape[1] < width:
            row = jnp.concatenate([row, jnp.zeros((1, width - row.shape[1]), wide)], 1)
        result = jnp.where(line == k, row, result)
    return result


def spec_sum_start(e):
    z = e.z
    return [
        remote(
            e,
            e.grad_pack.at[:, 1 - e.core], e.pack_core, e.ss_pack.at[0], e.rs_pack.at[0], e.sibling
        )
    ]


def spec_sum_middle(e, copies):
    z = e.z
    arrive(copies)
    for k in range(z.n_y):
        both = e.grad_pack[k, e.core].astype(wide) + e.pack_core[k].astype(wide)
        e.pack_send[k] = both.astype(narrow)
    new = [
        remote(
            e,
            e.pack_send.at[lax.rem(e.y + j + 1, z.n_y)], e.pack_y.at[e.y],
            e.ss_pack.at[1 + j], e.rs_pack.at[1 + j], peer,
        )
        for j, peer in enumerate(e.y_peers)
    ]
    e.pack_y[e.y] = e.pack_send[e.y]
    return new


def spec_sum_scatter(e, copies):
    z = e.z
    arrive(copies)
    value = e.pack_y[0].astype(wide)
    for k in range(1, z.n_y):
        value = value + e.pack_y[k].astype(wide)
    e.pack_sum[...] = value.reshape(z.n_sp, z.pack_share, z.block).astype(narrow)
    e.pack_landed[e.sp] = e.pack_sum[e.sp]
    for peer in e.sp_peers:
        start_remote(
            e.pack_sum.at[peer[0]], e.pack_landed.at[e.sp], e.ss_share.at[0], e.rs_share.at[0], peer
        )
    rest = others(e)
    return [
        Group(e, e.pack_sum.at[rest], e.pack_landed.at[rest], e.ss_share.at[0], e.rs_share.at[0])
    ]


def spec_sum_gather(e, copies):
    z = e.z
    arrive(copies)
    value = e.pack_landed[0].astype(wide)
    for k in range(1, z.n_sp):
        value = value + e.pack_landed[k].astype(wide)
    e.pack_out[e.sp] = value.astype(narrow)
    return [spread_slot(e, e.pack_out, e.ss_whole, e.rs_whole)]


def first_norm(e, c):
    gain, shift = line(e.gain1), line(e.shift1)
    for start, size in row_parts(e.z, c):
        values = field_rows(e, e.xs, c, start, size).astype(wide)
        center = mean(values)
        centred = values - center
        inv_std = lax.rsqrt(mean(centred * centred) + 1e-05)
        rows = pl.ds(start, size)
        e.xn[c, rows] = (centred * inv_std * gain + shift).astype(narrow)
        e.stats[c, rows, 0:1] = center
        e.stats[c, rows, 1:2] = inv_std


def second_norm(e, c):
    gain, shift = line(e.gain2), line(e.shift2)
    for start, size in row_parts(e.z, c):
        rows = pl.ds(start, size)
        values = e.mixed[c, rows]
        center = mean(values)
        centred = values - center
        inv_std = lax.rsqrt(mean(centred * centred) + 1e-05)
        e.xn2[c, rows] = (centred * inv_std * gain + shift).astype(narrow)
        e.stats[c, rows, 2:3] = center
        e.stats[c, rows, 3:4] = inv_std


def second_norm_backward(e, c, gain_grad, shift_grad):
    gain = line(e.gain2)
    for start, size in row_parts(e.z, c):
        rows = pl.ds(start, size)
        grad = e.grads_done[c, rows].astype(wide)
        inv_std = e.stats[c, rows, 3:4]
        hat = (e.mixed[c, rows] - e.stats[c, rows, 2:3]) * inv_std
        gain_grad = gain_grad + total(grad * hat)
        shift_grad = shift_grad + total(grad)
        scaled = grad * gain
        back = inv_std * (scaled - mean(scaled) - hat * mean(scaled * hat))
        e.xn[c, rows] = (e.gp[c, rows].astype(wide) + back).astype(narrow)
    return gain_grad, shift_grad


def first_norm_sums(e, half):
    lanes = lane_slice(e, half)
    gain_grad = jnp.zeros((1, e.z.lanes), wide)
    shift_grad = jnp.zeros((1, e.z.lanes), wide)
    for c in range(e.z.chunks):
        for start, size in row_parts(e.z, c):
            rows = pl.ds(start, size)
            grad = e.xn2[c, rows, lanes].astype(wide)
            values = field_rows(e, e.xs, c, start, size)
            values = values[:, half * e.z.lanes : (half + 1) * e.z.lanes].astype(wide)
            hat = (values - e.stats[c, rows, 0:1]) * e.stats[c, rows, 1:2]
            gain_grad = gain_grad + total(grad * hat)
            shift_grad = shift_grad + total(grad)
    return gain_grad, shift_grad


def first_norm_backward(e, c):
    gain = line(e.gain1)
    for start, size in row_parts(e.z, c):
        rows = pl.ds(start, size)
        grad = e.xn2[c, rows].astype(wide)
        inv_std = e.stats[c, rows, 1:2]
        values = field_rows(e, e.xs, c, start, size).astype(wide)
        hat = (values - e.stats[c, rows, 0:1]) * inv_std
        scaled = grad * gain
        back = inv_std * (scaled - mean(scaled) - hat * mean(scaled * hat))
        e.xn[c, rows] = (e.xn[c, rows].astype(wide) + back).astype(narrow)


def whole_body(e):
    z = e.z
    chunks = range(z.chunks)
    x_loads = [
        local_copy(e, e.hbm_x.at[p], e.xs.at[p], e.load_x.at[p]) for p in range(z.planes)
    ]
    loads = {}
    for index, name in enumerate(z.loaded):
        source = getattr(e, "hbm_" + name)
        if name == "long_rows":
            source = source.at[:, e.wa]
        elif name == "gs":
            source = source.at[pl.ds(0, 1)]
        loads[name] = local_copy(e, source, getattr(e, name), e.load.at[index])

    def need(*names):
        for name in names:
            loads.pop(name).wait()

    greet(e)
    clear_padding(e, e.xn)
    clear_padding(e, e.xn2)
    clear_padding(e, e.gp)
    need("w1", "b1", "w2", "b2")
    pack_weights(e)
    need("gain1", "shift1")
    for c in chunks:
        if c % 2 == 0:
            x_loads[c // 2].wait()
        first_norm(e, c)
    greeted(e)
    weights = send_weights(e)
    need("long_rows", "slot_rows")
    table = e.long_rows[0]
    first, second, gathers = [], [], []
    for half in range(halves):
        to_slots(e, e.xn, table, e.slots_a, half)
        first.append(send_slots(e, e.slots_a, e.landed_a, e.send_a, e.recv_a, half))
    need("gs")
    bias2_grad = jnp.zeros((1, z.channels), wide)
    for c in chunks:
        for start, size in row_parts(z, c):
            values = field_rows(e, e.gs, c % 2, start, size)
            e.gp[c, start : start + size] = values
            bias2_grad = bias2_grad + total(values.astype(wide))
        if c % 2 == 1 and c // 2 + 1 < z.planes:
            source = e.hbm_gs.at[pl.ds(c // 2 + 1, 1)]
            local_copy(e, source, e.gs, e.load.at[z.loaded.index("gs")]).wait()
    need("fc2")
    for c in chunks:
        e.gh[c] = dot_right_transposed(e.gp[c], e.fc2[...]).astype(narrow)
    weights = forward_weights(e, weights)
    arrive(weights)
    build_weights(e)
    need("lat", "lat_cols")
    for half in range(halves):
        rows = arrived_slots(e, e.landed_a, first[half], half)
        slots_from_modes(e, modes_forward(e, rows, half), e.slots_b, half)
        second.append(send_slots(e, e.slots_b, e.landed_b, e.send_b, e.recv_b, half))
    need("slot_cols", "long_out")
    sems = (e.send_y, e.recv_y, e.send_core, e.recv_core)
    for half in range(halves):
        rows = arrived_slots(e, e.landed_b, second[half], half)
        gathers.append(gather_start(e, rows, e.gathered, sems, half))
    for half in range(halves):
        gather_forward(e, gathers[half], e.gathered, sems, half)
        lanes = lane_slice(e, half)
        for p in range(z.planes):
            filtered = plane_from_gathered(e, e.long_out[1], e.gathered, half, p)
            for c in (2 * p, 2 * p + 1):
                size = chunk_rows(z, c)
                at = (c % 2) * z.chunk
                values = field_rows(e, e.xs, c, 0, size)
                values = values[:, half * z.lanes : (half + 1) * z.lanes].astype(wide)
                step = filtered[at : at + size].astype(narrow).astype(wide)
                e.mixed[c, pl.ds(0, size), lanes] = values + step
    finish(first + second)

    need("gain2", "shift2", "fc1", "fc1_bias", "fc2_bias")
    grads = WaSum(e, "grads", e.xn)
    bias1 = line(e.fc1_bias).astype(wide)
    bias1_grad = jnp.zeros((1, z.hidden), wide)
    for c in chunks:
        second_norm(e, c)
        hidden, slope = gelu_with_slope(dot(e.xn2[c], e.fc1[...]) + bias1)
        e.act[c] = hidden.astype(narrow)
        grad_hidden = (e.gh[c].astype(wide) * slope).astype(narrow)
        e.gh[c] = grad_hidden
        bias1_grad = bias1_grad + total(grad_hidden.astype(wide))
        grads.start(c, dot_right_transposed(grad_hidden, e.fc1[...]))
        if c >= 1:
            grads.middle(c - 1)

    all_rows = z.chunks * z.chunk
    sources = (
        (e.xn2, e.gh, e.sum1, e.landed1, e.total1, z.channels),
        (e.act, e.gp, e.sum2, e.landed2, e.total2, z.hidden),
    )
    cubes = []

    def tick(name):
        for index in SCHEDULE.get(name, ()):
            cubes[index].advance()

    for index, (left, right, block, landed, out, rows) in enumerate(sources):
        size = rows // cuts
        for k in range(cuts):
            part = left[:, :, k * size : (k + 1) * size].reshape(all_rows, size)
            value = dot_left_transposed(part, right[...].reshape(all_rows, right.shape[-1]))
            block[k] = value.astype(narrow)
            cube = CubeSum(
                e, block.at[k], landed.at[k], out.at[pl.ds(k * size, size)],
                e.send_cube, e.recv_cube, cuts * index + k,
            )
            cubes.append(cube)
            if len(cubes) == 1:
                grads.middle(z.chunks - 1)
            tick("c%d" % (cuts * index + k))
    gain2_grad = jnp.zeros((1, z.channels), wide)
    shift2_grad = jnp.zeros((1, z.channels), wide)
    table = e.long_rows[1]
    branch = WaSum(e, "branch", e.xn2)
    need("slot_rows3", "lat3")
    for c in range(z.chunks + 1):
        if c < z.chunks:
            tick("q%d" % c)
            grads.end(c)
        if c >= 1:
            last = c - 1
            grads.value(last)
            finish([grads.core[last]])
            gain2_grad, shift2_grad = second_norm_backward(e, last, gain2_grad, shift2_grad)
            if last % 2 == 1:
                third = send_plane(e, table, last // 2)
            branch.start(last, dot(e.act[last], e.fc2[...]))
            tick("n%d" % last)

    rows = [(0, bias1_grad), (1, bias2_grad), (2, gain2_grad), (3, shift2_grad)]
    small_one = exchange_small(
        e, place_rows(rows, z.small), e.small_one, e.send_one, e.recv_one
    )
    early, late = chunks[: z.chunks // 2], chunks[z.chunks // 2 :]
    for c in early:
        branch.middle(c)
        tick("m%d" % c)
    fourth, back_gathers = [], []
    third.wait_recv()
    planes = plane_slots(e)
    for half in range(halves):
        slots_from_modes(e, modes_backward(e, planes, half), e.slots_b, half)
        fourth.append(send_slots(e, e.slots_b, e.landed_d, e.send_d, e.recv_d, half))
        tick("w%d" % half)
        spectral_grads(e, half)
        tick("s%d" % half)
    packs = [spec_sum_start(e)]
    sems = (e.send_y2, e.recv_y2, e.send_core2, e.recv_core2)
    writes = []
    bias = e.fc2_bias[...].reshape(1, -1).astype(wide)

    def write_output(c):
        branch.value(c)
        finish([branch.last[c]])
        for start, size in row_parts(z, c):
            rows = pl.ds(start, size)
            value = e.mixed[c, rows] + (e.branch_done[c, rows].astype(wide) + bias)
            e.branch_done[c, rows] = value.astype(narrow)
        writes.append(local_copy(e, e.branch_done.at[c], e.hbm_output.at[c], e.write_sems.at[c]))

    packs.append(spec_sum_middle(e, packs[-1]))
    for half in range(halves):
        rows = arrived_slots(e, e.landed_d, fourth[half], half)
        back_gathers.append(gather_start(e, rows, e.gathered2, sems, half))
        tick("g%d" % half)
    packs.append(spec_sum_scatter(e, packs[-1]))
    for c in late:
        branch.middle(c)
        tick("m%d" % c)
    for c in early:
        branch.end(c)
    for c in early:
        write_output(c)
        tick("o%d" % c)
    lane_sums = []
    finish(branch.core.values())
    for half in range(halves):
        gather_forward(e, back_gathers[half], e.gathered2, sems, half)
        for p in range(z.planes):
            grad = plane_from_gathered(e, e.long_out[0], e.gathered2, half, p).astype(narrow)
            for c in (2 * p, 2 * p + 1):
                at = (c % 2) * z.chunk
                e.xn2[c, :, lane_slice(e, half)] = grad[at : at + z.chunk]
        lane_sums.append(first_norm_sums(e, half))
        tick("f%d" % half)
        if half == 0:
            packs.append(spec_sum_gather(e, packs[-1]))
    gain1_grad = jnp.concatenate([pair[0] for pair in lane_sums], 1)
    shift1_grad = jnp.concatenate([pair[1] for pair in lane_sums], 1)
    small_two = exchange_small(
        e, place_rows([(0, gain1_grad), (1, shift1_grad)], z.small),
        e.small_two, e.send_two, e.recv_two,
    )
    for c in late:
        branch.end(c)
    for c in chunks:
        first_norm_backward(e, c)
        writes.append(local_copy(e, e.xn.at[c], e.hbm_fields_grad.at[c], e.write_sems2.at[c]))
        if c in late:
            write_output(c)
        tick("l%d" % c)
    tick("p")
    arrive(packs[-1])
    writes.append(local_copy(e, e.pack_out, e.hbm_pack, e.store.at[0]))
    e.small_out[0] = sum_small(e, e.small_one, small_one)
    e.small_out[1] = sum_small(e, e.small_two, small_two)
    writes.append(local_copy(e, e.small_out, e.hbm_small, e.store.at[1]))
    for index, cube in enumerate(cubes):
        cube.drain()
        target = e.hbm_fc1_grad if index < cuts else e.hbm_fc2_grad
        rows = cube.rows
        target = target.at[pl.ds((index % cuts) * rows, rows)]
        writes.append(local_copy(e, cube.out, target, e.store.at[2 + index]))
    arrive(e.copies)
    finish(e.copies)
    for write in writes:
        write.wait()


class Names:
    def __init__(self):
        self.names, self.shapes = [], []

    def add(self, name, shape):
        self.names.append(name)
        self.shapes.append(shape)

    def vmem(self, name, shape, dtype=narrow):
        self.add(name, pltpu.VMEM(shape, dtype))

    def dma(self, name, shape):
        self.add(name, pltpu.SemaphoreType.DMA(shape))


def scratch_of(z):
    s = Names()
    fields = (z.planes, z.width, z.fields, z.channels)
    rows = (z.chunks, z.chunk, z.channels)
    hidden = (z.chunks, z.chunk, z.hidden)
    s.vmem("xs", fields)
    lat_rows = z.n_sp * z.slot
    n = z.block
    for name, shape, dtype in (
        ("w1", (z.own_blocks, 2 * n, n), narrow), ("b1", (z.own_blocks, 2, n), narrow),
        ("w2", (z.own_blocks, 2 * n, n), narrow), ("b2", (z.own_blocks, 2, n), narrow),
        ("gain1", (z.channels,), wide), ("shift1", (z.channels,), wide),
        ("gain2", (z.channels,), wide), ("shift2", (z.channels,), wide),
        ("fc1", (z.channels, z.hidden), narrow), ("fc1_bias", (z.hidden,), narrow),
        ("fc2", (z.hidden, z.channels), narrow), ("fc2_bias", (z.channels,), narrow),
        ("gs", (1,) + fields[1:], narrow), ("long_rows", (2, z.group, z.pitch), narrow),
        ("slot_rows", (lat_rows, z.planes * z.group), narrow),
        ("slot_cols", (z.planes * z.group, lat_rows), narrow),
        ("lat", (2 * z.count, lat_rows), narrow), ("lat_cols", (lat_rows, 2 * z.count), narrow),
        ("long_out", (2, z.pitch, z.n_wa * z.group), narrow),
        ("slot_rows3", (halves, z.n_sp * z.plane_slot, z.group), narrow),
        ("lat3", (halves, 2 * z.count, z.n_sp * z.planes * z.plane_slot), narrow),
    ):
        s.vmem(name, shape, dtype)
    s.dma("load_x", (z.planes,))
    s.dma("load", (len(z.loaded),))
    s.dma("store", (2 + 2 * cuts,))
    s.dma("write_sems", (z.chunks,))
    s.dma("write_sems2", (z.chunks,))
    for name in ("xn", "gp", "xn2"):
        s.vmem(name, rows)
    s.vmem("act", hidden)
    s.vmem("gh", hidden)
    s.vmem("mixed", rows, wide)
    s.vmem("stats", (z.chunks, z.chunk, 4), wide)
    s.vmem("columns", (halves, z.planes, z.group, z.lanes))
    for name in ("slots_a", "slots_b", "landed_a", "landed_b", "landed_d"):
        s.vmem(name, (halves, z.n_sp, z.slot, z.lanes))
    for tag in "abd":
        s.dma("send_" + tag, (halves,))
        s.dma("recv_" + tag, (halves,))
    s.vmem("slots_c", (z.n_sp, z.planes, z.plane_slot, z.lanes))
    s.vmem("landed_c", (z.n_sp, z.planes, z.plane_slot, z.lanes))
    s.dma("send_c", (1,))
    s.dma("recv_c", (1,))
    for tag in ("", "2"):
        s.vmem("gathered" + tag, (halves, z.planes, z.n_wa, z.group, z.lanes))
        for name in ("send_y", "recv_y"):
            s.dma(name + tag, (halves, max(z.n_y - 1, 1)))
        for name in ("send_core", "recv_core"):
            s.dma(name + tag, (halves, z.n_y))
    s.vmem("packed", (z.blocks, z.pack, z.block))
    s.vmem("bias", (halves, 16, z.lanes), wide)
    s.dma("send_w", (2 * z.n_y - 1,))
    s.dma("recv_w", (2 * z.n_y - 1,))
    both = (halves, z.count, 2 * z.lanes)
    for name in ("spec", "hid", "grad_one", "grad_two"):
        s.vmem(name, both)
    s.vmem("slope1", both, wide)
    s.vmem("slope2", both, wide)
    for name in ("big1", "big2"):
        s.vmem(name, (halves, 2 * z.lanes, 2 * z.lanes))
    s.vmem("grad_pack", (z.n_y, 2, z.own_blocks, z.pack, z.block))
    for name in ("pack_core", "pack_send", "pack_y"):
        s.vmem(name, (z.n_y, z.own_blocks, z.pack, z.block))
    s.vmem("pack_out", (z.n_sp, z.pack_share, z.block))
    s.vmem("small_out", (2, 8, z.small), wide)
    s.vmem("pack_sum", (z.n_sp, z.pack_share, z.block))
    s.vmem("pack_landed", (z.n_sp, z.pack_share, z.block))
    for name in ("ss_pack", "rs_pack"):
        s.dma(name, (z.n_y,))
    for name in ("ss_share", "rs_share", "ss_whole", "rs_whole"):
        s.dma(name, (1,))
    wa_sum_scratch(s, z, "grads")
    wa_sum_scratch(s, z, "branch")
    for tag, rows, lanes in (("1", z.channels, z.hidden), ("2", z.hidden, z.channels)):
        s.vmem("sum" + tag, (cuts, rows // cuts, lanes))
        s.vmem("total" + tag, (rows, lanes))
        s.vmem("landed" + tag, (cuts, cube_landed_rows(rows // cuts, z.n_sp), lanes))
    steps = 2 * len(cube_levels(z.channels, z.n_sp))
    s.dma("send_cube", (2 * cuts, steps))
    s.dma("recv_cube", (2 * cuts, steps))
    for tag in ("one", "two"):
        s.vmem("small_" + tag, (z.n_sp, 8, z.small), wide)
        s.dma("send_" + tag, (1,))
        s.dma("recv_" + tag, (1,))
    return s


def call_kernel(body, z, inputs, outputs, scratch, collective):
    names = [name for name, _ in inputs] + [name for name, _, _ in outputs]

    def kernel(*refs):
        e = types.SimpleNamespace(z=z)
        for name, ref in zip(names + scratch.names, refs):
            setattr(e, name, ref)
        e.copies = []
        place(e)
        body(e)

    def spec(name):
        return pl.BlockSpec(memory_space=pl.ANY if name.startswith("hbm_") else pltpu.VMEM)

    return pl.pallas_call(
        kernel,
        out_shape=[jax.ShapeDtypeStruct(shape, dtype) for _, shape, dtype in outputs],
        in_specs=[spec(name) for name, _ in inputs],
        out_specs=[spec(name) for name, _, _ in outputs],
        scratch_shapes=scratch.shapes,
        compiler_params=pltpu.CompilerParams(
            collective_id=collective,
            has_side_effects=collective is not None,
            vmem_limit_bytes=61 * 1024 * 1024,
        ),
    )(*[value for _, value in inputs])


def finish_body(e):
    z = e.z
    loads, writes = [], []
    pairs = [
        (source.at[c], target.at[c])
        for source, target in ((e.hbm_output, e.rows_output), (e.hbm_fields, e.rows_fields))
        for c in range(z.chunks)
    ]
    pairs += [
        (e.hbm_fc1, e.rows_fc1), (e.hbm_fc2, e.rows_fc2), (e.hbm_pack, e.pack), (e.hbm_small, e.small)
    ]
    for index, (source, target) in enumerate(pairs):
        loads.append(local_copy(e, source, target, e.load.at[index]))

    def write(source, target):
        writes.append(local_copy(e, source, target, e.store.at[len(writes)]))

    for index, (rows, wide_rows, target) in enumerate(
        (
            (e.rows_output, e.wide_output, e.hbm_output_out),
            (e.rows_fields, e.wide_fields, e.hbm_fields_out),
        )
    ):
        for c in range(z.chunks):
            loads[index * z.chunks + c].wait()
            for start, size in row_parts(z, c, 96):
                values = rows[c, start : start + size].astype(wide)
                first = ((c % 2) * z.chunk + start) // z.fields
                wide_rows[c // 2, first : first + size // z.fields] = values.reshape(
                    size // z.fields, z.fields, z.channels
                )
            if c % 2 == 1:
                write(wide_rows.at[c // 2], target.at[c // 2])
    for index, (rows, wide_rows, target) in enumerate(
        ((e.rows_fc1, e.wide_fc1, e.hbm_fc1_out), (e.rows_fc2, e.wide_fc2, e.hbm_fc2_out))
    ):
        loads[2 * z.chunks + index].wait()
        wide_rows[...] = rows[...].astype(wide)
        write(wide_rows, target)
    for load in loads[2 * z.chunks + 2 :]:
        load.wait()
    n = z.block
    e.w1[...] = e.pack[:, : 2 * n].astype(wide)
    e.w2[...] = e.pack[:, 2 * n : 4 * n].astype(wide)
    bias = e.pack[:, 4 * n : 4 * n + 16].astype(wide)
    e.b1[...] = bias[:, 0:2]
    e.b2[...] = bias[:, 2:4]
    small = e.small[...]
    e.gain1[...] = small[1, 0, : z.channels]
    e.shift1[...] = small[1, 1, : z.channels]
    e.gain2[...] = small[0, 2, : z.channels]
    e.shift2[...] = small[0, 3, : z.channels]
    e.fc1_bias[...] = small[0, 0, : z.hidden]
    e.fc2_bias[...] = small[0, 1, : z.channels]
    for name in z.small_names:
        write(getattr(e, name), getattr(e, "hbm_out_" + name))
    for copy in writes:
        copy.wait()


def finish_call(z, output, fields_grad, fc1, fc2, pack, small):
    channels, hidden, n = z.channels, z.hidden, z.block
    inputs = [
        ("hbm_output", output), ("hbm_fields", fields_grad), ("hbm_fc1", fc1), ("hbm_fc2", fc2),
        ("hbm_pack", pack.reshape(z.own_blocks, z.pack, n)), ("hbm_small", small),
    ]
    fields = (z.planes, z.width, z.fields, channels)
    smalls = {
        "gain1": (channels,), "shift1": (channels,),
        "w1": (z.own_blocks, 2 * n, n), "b1": (z.own_blocks, 2, n),
        "w2": (z.own_blocks, 2 * n, n), "b2": (z.own_blocks, 2, n),
        "gain2": (channels,), "shift2": (channels,),
        "fc1_bias": (hidden,), "fc2_bias": (channels,),
    }
    z.small_names = tuple(smalls)
    outputs = [("hbm_output_out", fields, wide), ("hbm_fields_out", fields, wide)]
    outputs += [("hbm_out_" + name, shape, wide) for name, shape in smalls.items()]
    outputs += [
        ("hbm_fc1_out", (channels, hidden), wide), ("hbm_fc2_out", (hidden, channels), wide),
    ]
    s = Names()
    s.vmem("rows_output", output.shape)
    s.vmem("rows_fields", fields_grad.shape)
    s.vmem("rows_fc1", fc1.shape)
    s.vmem("rows_fc2", fc2.shape)
    s.vmem("pack", (z.own_blocks, z.pack, n))
    s.vmem("small", small.shape, wide)
    s.vmem("wide_output", fields, wide)
    s.vmem("wide_fields", fields, wide)
    s.vmem("wide_fc1", fc1.shape, wide)
    s.vmem("wide_fc2", fc2.shape, wide)
    for name, shape in smalls.items():
        s.vmem(name, shape, wide)
    s.dma("load", (2 * z.chunks + 4,))
    s.dma("store", (2 * z.planes + 2 + len(smalls),))
    results = call_kernel(finish_body, z, inputs, outputs, s, None)
    named = dict(zip(smalls, results[2:-2]))
    return results[0], results[1], results[-2], results[-1], named


def local(
    fields_in,
    norm1_gain,
    norm1_shift,
    spec_w1,
    spec_b1,
    spec_w2,
    spec_b2,
    norm2_gain,
    norm2_shift,
    fc1_weight,
    fc1_bias,
    fc2_weight,
    fc2_bias,
    out_grad,
):
    fields, rows_here, width, channels = fields_in.shape
    n_sp, n_wa = lax.axis_size("sp"), lax.axis_size("wa")
    block, hidden = spec_w1.shape[2], fc1_weight.shape[1]
    z = plan(
        n_sp, n_wa, fields, rows_here, width, channels, channels // block, block, hidden
    )
    long_rows, long_out = longitude_tables(z)
    index, lat = slot_index(z), latitude_table(z)
    index3, lat3 = plane_tables(z, index, lat)
    tables = [
        jnp.asarray(np.ascontiguousarray(table))
        for table in (long_rows, long_out, index, index.T, lat, lat.T, index3, lat3)
    ]
    own, n = z.own_blocks, block
    turned = lambda value: jnp.transpose(value, (1, 2, 0, 3))
    inputs = [
        ("hbm_x", turned(fields_in)), ("hbm_gs", turned(out_grad)),
        ("hbm_fc1", fc1_weight), ("hbm_fc2", fc2_weight),
        ("hbm_gain1", norm1_gain), ("hbm_shift1", norm1_shift),
        ("hbm_gain2", norm2_gain), ("hbm_shift2", norm2_shift),
        ("hbm_fc1_bias", fc1_bias), ("hbm_fc2_bias", fc2_bias),
        ("hbm_w1", spec_w1.reshape(own, 2 * n, n)), ("hbm_b1", spec_b1),
        ("hbm_w2", spec_w2.reshape(own, 2 * n, n)), ("hbm_b2", spec_b2),
    ]
    names = (
        "long_rows", "long_out", "slot_rows", "slot_cols", "lat", "lat_cols", "slot_rows3", "lat3",
    )
    inputs += [("hbm_" + name, table) for name, table in zip(names, tables)]
    flat = (z.chunks, z.chunk, channels)
    outputs = [
        ("hbm_output", flat, narrow), ("hbm_fields_grad", flat, narrow),
        ("hbm_fc1_grad", (channels, hidden), narrow), ("hbm_fc2_grad", (hidden, channels), narrow),
        ("hbm_pack", (z.n_sp, z.pack_share, n), narrow), ("hbm_small", (2, 8, z.small), wide),
    ]
    output, fields_grad, fc1, fc2, named = finish_call(
        z, *call_kernel(whole_body, z, inputs, outputs, scratch_of(z), 0)
    )
    back = lambda value: jnp.transpose(value, (2, 0, 1, 3))
    shaped = lambda value: value.reshape(own, 2, n, n)
    return (
        back(output), back(fields_grad), named["gain1"], named["shift1"],
        shaped(named["w1"]), named["b1"], shaped(named["w2"]), named["b2"],
        named["gain2"], named["shift2"], fc1, named["fc1_bias"], fc2, named["fc2_bias"],
    )


def solution(mesh):
    return jax.shard_map(
        local,
        mesh=mesh,
        in_specs=(
            P(None, "sp", None, None),
            P(),
            P(),
            P("wa", None, None, None),
            P("wa", None, None),
            P("wa", None, None, None),
            P("wa", None, None),
            P(),
            P(),
            P(None, "wa"),
            P("wa"),
            P("wa", None),
            P(),
            P(None, "sp", None, None),
        ),
        out_specs=(
            P(None, "sp", None, None),
            P(None, "sp", None, None),
            P(),
            P(),
            P("wa", None, None, None),
            P("wa", None, None),
            P("wa", None, None, None),
            P("wa", None, None),
            P(),
            P(),
            P(None, "wa"),
            P("wa"),
            P("wa", None),
            P(),
        ),
        check_vma=False,
    )
```

```python
import functools
import math
import types

import jax
import jax.numpy as jnp
import numpy as np
from jax import lax
from jax.experimental import pallas as pl
from jax.experimental.pallas import tpu as pltpu
from jax.sharding import PartitionSpec as P

threshold = 0.01
narrow = jnp.bfloat16
wide = jnp.float32
MESH = pl.DeviceIdType.MESH
halves = 2


def round_up(value, step):
    return -(-value // step) * step


def phase_angles(rows, columns, period):
    product = rows[:, None] * columns[None, :] % period
    return (np.float32(2.0 * math.pi / period) * product.astype(np.float32)).astype(np.float32)


def plan(n_sp, n_wa, fields, rows_here, width, channels, blocks, block, hidden):
    z = types.SimpleNamespace(
        n_sp=n_sp, n_wa=n_wa, n_y=n_wa // 2, width=width, channels=channels, hidden=hidden,
        blocks=blocks, block=block, fields=fields, planes=rows_here,
    )
    z.period = rows_here * n_sp
    z.modes = width // 2 + 1
    z.each = -(-z.modes // (n_sp * n_wa))
    z.plane = fields * width
    z.pitch = round_up(z.plane, 64)
    z.chunk = z.pitch // 2
    z.chunks = 2 * rows_here
    z.part = z.chunk // 2
    z.lanes = channels // halves
    z.slot = round_up(2 * rows_here * fields * z.each, 8)
    z.group = round_up(2 * n_sp * fields * z.each, 16)
    z.count = z.period * fields * z.each
    z.half_blocks = blocks // halves
    z.own_blocks = blocks // n_wa
    z.pack = round_up(4 * block + 16, 16 * n_sp // math.gcd(16 * n_sp, z.own_blocks))
    z.pack_share = z.own_blocks * z.pack // n_sp
    z.small = max(channels, hidden)
    z.plane_slot = round_up(halves * 2 * fields * z.each, 8)
    z.loaded = (
        "w1", "b1", "w2", "b2", "gain1", "shift1", "long_rows", "slot_rows", "gs", "lat", "lat_cols",
        "slot_cols", "long_out", "gain2", "shift2", "fc1", "fc1_bias", "fc2", "fc2_bias",
    )
    return z


def longitude_tables(z):
    angles = phase_angles(np.arange(z.width), np.arange(z.modes), z.width)
    scale = np.float32(1.0 / math.sqrt(z.width))
    padded = z.each * z.n_sp * z.n_wa
    table = np.zeros((2, padded, z.width), np.float32)
    table[0, : z.modes] = (np.cos(angles) * scale).T
    table[1, : z.modes] = (-np.sin(angles) * scale).T
    k = np.arange(padded)
    weights = np.where((k == 0) | (2 * k == z.width), 1.0, 2.0).astype(np.float32)
    both = np.stack([table, table * weights[None, :, None]])
    both = both.reshape(2, 2, z.n_wa, z.n_sp, z.each, z.width).transpose(0, 2, 1, 3, 4, 5)
    rows = np.zeros((2, z.n_wa, 2, z.n_sp, z.fields, z.each, z.width, z.fields), np.float32)
    for f in range(z.fields):
        rows[:, :, :, :, f, :, :, f] = both
    padded = np.zeros((2, z.n_wa, z.group, z.pitch), np.float32)
    used = 2 * z.n_sp * z.fields * z.each
    padded[:, :, :used, : z.plane] = rows.reshape(2, z.n_wa, used, z.plane)
    out = padded.reshape(2, z.n_wa * z.group, z.pitch).transpose(0, 2, 1)
    return padded.astype(narrow), np.ascontiguousarray(out).astype(narrow)


def slot_index(z):
    table = np.zeros((z.n_sp, z.slot, z.planes, z.group), np.float32)
    for d in range(z.n_sp):
        for c in range(2):
            for h in range(z.planes):
                for f in range(z.fields):
                    for j in range(z.each):
                        r = ((c * z.planes + h) * z.fields + f) * z.each + j
                        table[d, r, h, ((c * z.n_sp + d) * z.fields + f) * z.each + j] = 1.0
    return table.reshape(z.n_sp * z.slot, z.planes * z.group).astype(narrow)


def latitude_table(z):
    angles = phase_angles(np.arange(z.period), np.arange(z.period), z.period)
    scale = np.float32(1.0 / math.sqrt(z.period))
    inner = z.fields * z.each
    cosine = (np.cos(angles) * scale).reshape(z.period, z.n_sp, z.planes)
    sine = (np.sin(angles) * scale).reshape(z.period, z.n_sp, z.planes)
    table = np.zeros((2, z.period, inner, z.n_sp, 2, z.planes, inner), np.float32)
    for i in range(inner):
        table[0, :, i, :, 0, :, i] = cosine
        table[0, :, i, :, 1, :, i] = sine
        table[1, :, i, :, 1, :, i] = cosine
        table[1, :, i, :, 0, :, i] = -sine
    padded = np.zeros((2 * z.count, z.n_sp, z.slot), np.float32)
    padded[:, :, : 2 * z.planes * inner] = table.reshape(2 * z.count, z.n_sp, -1)
    return padded.reshape(2 * z.count, z.n_sp * z.slot).astype(narrow)


def plane_tables(z, index, lat):
    used = 2 * z.fields * z.each
    per = z.planes * used
    shape = (z.n_sp, z.slot, z.planes, z.group)
    moved = np.zeros((halves, z.n_sp, z.plane_slot, z.group), narrow)
    turned = np.zeros((halves, 2 * z.count, z.n_sp, z.planes, z.plane_slot), narrow)
    kept = index.reshape(shape)[:, :per, 0].reshape(z.n_sp, 2, z.planes, -1, z.group)[:, :, 0]
    source = lat.reshape(-1, z.n_sp, z.slot)[:, :, :per].reshape(-1, z.n_sp, 2, z.planes, used // 2)
    source = source.transpose(0, 1, 3, 2, 4).reshape(-1, z.n_sp, z.planes, used)
    for half in range(halves):
        rows = slice(half * used, (half + 1) * used)
        moved[half, :, rows] = kept.reshape(z.n_sp, used, z.group)
        turned[half, ..., rows] = source
    return moved.reshape(halves, -1, z.group), turned.reshape(halves, 2 * z.count, -1)


def dot(left, right):
    return jnp.dot(left, right, preferred_element_type=wide)


def dot_right_transposed(left, right):
    return lax.dot_general(left, right, (((1,), (1,)), ((), ())), preferred_element_type=wide)


def dot_left_transposed(left, right):
    return lax.dot_general(left, right, (((0,), (0,)), ((), ())), preferred_element_type=wide)


def gelu_with_slope(v):
    scale = np.float32(math.sqrt(2.0 / math.pi))
    square = v * v
    bent = jnp.tanh(scale * v * (1.0 + 0.044715 * square))
    above = 0.5 + 0.5 * bent
    slope = above + 0.5 * v * (1.0 - bent * bent) * (scale * (1.0 + (3 * 0.044715) * square))
    return v * above, slope


cuts = 3
EARLY = 4
SWAPPED = (0,)
SCHEDULE = {'c0': (0,), 'q4': (2, 5, 0), 'n4': (2, 5, 0), 'm2': (2, 0), 'g1': (5, 0), 'o2': (0,), 'n1': (1,), 'q5': (1, 3), 'm0': (1, 4), 'v': (5, 1, 3, 4), 's0': (1, 4), 'g2': (1,), 'p': (1,), 'c2': (2,), 'q2': (2,), 'g0': (2, 3), 'o1': (2, 5, 4), 'm1': (3,), 'o0': (3,), 'o3': (3,), 'l4': (3,), 'm4': (4,), 'f0': (4,), 'c5': (5,)}


def chunk_rows(z, c):
    return min(z.chunk, z.plane - (c % 2) * z.chunk)


def row_parts(z, c, step=48):
    rows = chunk_rows(z, c)
    return [(start, min(step, rows - start)) for start in range(0, rows, step)]


def place(e):
    z = e.z
    sp, wa = lax.axis_index("sp"), lax.axis_index("wa")
    e.sp, e.wa = sp, wa
    e.core, e.y = lax.rem(wa, 2), lax.div(wa, 2)
    e.sibling = (sp, wa + 1 - 2 * e.core)
    e.sp_peers = [(lax.rem(sp + i, z.n_sp), wa) for i in range(1, z.n_sp)]
    e.y_peers = [(sp, lax.rem(wa + 2 * j, z.n_wa)) for j in range(1, z.n_y)]
    e.wa_peers = [(sp, lax.rem(wa + j, z.n_wa)) for j in range(1, z.n_wa)]


def greet(e):
    barrier = pltpu.get_barrier_semaphore()
    for peer in e.sp_peers + e.wa_peers:
        pl.semaphore_signal(barrier, inc=1, device_id=peer, device_id_type=MESH)


def greeted(e):
    barrier = pltpu.get_barrier_semaphore()
    pl.semaphore_wait(barrier, len(e.sp_peers) + len(e.wa_peers))


class Copy:
    def __init__(self, copy):
        self.copy, self.received, self.sent = copy, False, False

    def wait_recv(self):
        if not self.received:
            self.copy.wait_recv()
        self.received = True

    def wait_send(self):
        if not self.sent:
            self.copy.wait_send()
        self.sent = True


class Group:
    def __init__(self, e, sent, landed, send, recv):
        self.ends = {"recv": (landed, recv), "send": (sent, send)}
        e.copies.append(self)

    def wait(self, end):
        if end in self.ends:
            ref, sem = self.ends.pop(end)
            pltpu.make_async_copy(ref, ref, sem).wait()

    def wait_recv(self):
        self.wait("recv")

    def wait_send(self):
        self.wait("send")


def start_remote(source, target, send, recv, peer):
    pltpu.make_async_remote_copy(
        src_ref=source, dst_ref=target, send_sem=send, recv_sem=recv,
        device_id=peer, device_id_type=MESH,
    ).start()


def remote(e, source, target, send, recv, peer):
    copy = pltpu.make_async_remote_copy(
        src_ref=source, dst_ref=target, send_sem=send, recv_sem=recv,
        device_id=peer, device_id_type=MESH,
    )
    copy.start()
    e.copies.append(Copy(copy))
    return e.copies[-1]


def arrive(copies):
    for copy in copies:
        copy.wait_recv()


def finish(copies):
    for copy in copies:
        copy.wait_send()


def line(ref):
    return ref[...].reshape(1, -1)


def local_copy(e, source, target, sem):
    copy = pltpu.make_async_copy(source, target, sem)
    copy.start()
    return copy


def mean(values):
    return jnp.mean(values, -1, keepdims=True)


def total(values):
    return jnp.sum(values, 0, keepdims=True)


def lane_slice(e, half):
    return pl.ds(half * e.z.lanes, e.z.lanes)


def clear_padding(e, buffer):
    z = e.z
    start = chunk_rows(z, 1) // 16 * 16
    for c in range(1, z.chunks, 2):
        if start < z.chunk:
            buffer[c, start:] = jnp.zeros_like(buffer[c, start:])


def field_rows(e, source, c, start, size):
    z = e.z
    first = ((c % 2) * z.chunk + start) // z.fields
    return source[c // 2, first : first + size // z.fields].reshape(size, z.channels)


def others(e):
    return pl.ds(0, e.z.n_sp - 1)


def send_plane(e, tag, p, together):
    z = e.z
    slots, landed = getattr(e, "slots_" + tag), getattr(e, "landed_" + tag)
    at = 0 if together else p
    send, recv = getattr(e, "send_" + tag).at[at], getattr(e, "recv_" + tag).at[at]
    for peer in e.sp_peers:
        start_remote(slots.at[peer[0], p], landed.at[e.sp, p], send, recv, peer)
    landed[e.sp, p] = slots[e.sp, p]
    rest = others(e)
    if not together:
        return Group(e, slots.at[rest, p], landed.at[rest, p], send, recv)
    if p + 1 < z.planes:
        return None
    return Group(e, slots.at[rest], landed.at[rest], send, recv)


def columns_to_slots(e, table, tag, p):
    z = e.z
    source = e.xn[2 * p : 2 * p + 2].reshape(z.pitch, z.channels)
    columns = dot(table, source).astype(narrow)
    moved = dot(e.slot_rows[0], columns[:, : z.lanes]) + dot(e.slot_rows[1], columns[:, z.lanes :])
    moved = moved.astype(narrow)
    slots = getattr(e, "slots_" + tag)
    for d in range(z.n_sp):
        slots[d, p] = moved[d * z.plane_slot : (d + 1) * z.plane_slot]
    return send_plane(e, tag, p, True)


def mode_rows(e, landed):
    z = e.z
    rows = landed[...].astype(wide)
    return rows.reshape(z.n_sp * z.planes * z.plane_slot, z.lanes).astype(narrow)


def modes_from_slots(e, rows, table):
    z = e.z
    real = dot(table[: z.count], rows)
    imag = dot(table[z.count :], rows)
    return jnp.concatenate([real, imag], 1)


def modes_to_slots(e, values, tag):
    z = e.z
    moved = jnp.zeros((z.n_sp * z.planes * z.plane_slot, z.lanes), wide)
    for half, value in enumerate(values):
        stacked = jnp.concatenate([value[:, : z.lanes], value[:, z.lanes :]], 0)
        moved = moved + dot(e.lat_cols[half], stacked)
    moved = moved.astype(narrow)
    slots = getattr(e, "slots_" + tag)
    for d in range(z.n_sp):
        for p in range(z.planes):
            at = (d * z.planes + p) * z.plane_slot
            slots[d, p] = moved[at : at + z.plane_slot]
    return [send_plane(e, tag, p, False) for p in range(z.planes)]


class Gather:
    def __init__(self, e, gathered, tag):
        self.e, self.gathered = e, gathered
        self.sems = [
            getattr(e, name + tag) for name in ("send_y", "recv_y", "send_core", "recv_core")
        ]
        self.y, self.core = {}, {}

    def start(self, group, landed, p):
        e, z = self.e, self.e.z
        send_y, recv_y, send_core, recv_core = self.sems
        group.wait_recv()
        rows = landed[:, p].astype(wide).reshape(z.n_sp * z.plane_slot, z.lanes).astype(narrow)
        for half in range(halves):
            ordered = dot(e.slot_cols[half], rows).astype(narrow)
            self.gathered[p, e.wa, :, lane_slice(e, half)] = ordered
        own = self.gathered.at[p, e.wa]
        self.y[p] = [
            remote(e, own, own, send_y.at[p, j], recv_y.at[p, j], peer)
            for j, peer in enumerate(e.y_peers)
        ]
        self.core[p] = [
            remote(e, own, own, send_core.at[p, 0], recv_core.at[p, 0], e.sibling)
        ]

    def forward(self, p):
        e, z = self.e, self.e.z
        send_y, recv_y, send_core, recv_core = self.sems
        for j, copy in enumerate(self.y[p]):
            copy.wait_recv()
            slab = self.gathered.at[p, lax.rem(e.wa + z.n_wa - 2 * (j + 1), z.n_wa)]
            sems = send_core.at[p, j + 1], recv_core.at[p, j + 1]
            self.core[p].append(remote(e, slab, slab, *sems, e.sibling))

    def rows(self, table, p):
        z = self.e.z
        arrive(self.core[p])
        return dot(table, self.gathered[p].reshape(z.n_wa * z.group, z.channels))


def pack_weights(e):
    z = e.z
    for i in range(z.own_blocks):
        at = e.wa * z.own_blocks + i
        e.packed[at, : 2 * z.block] = e.w1[i]
        e.packed[at, 2 * z.block : 4 * z.block] = e.w2[i]
        line = lax.broadcasted_iota(jnp.int32, (16, z.block), 0)
        bias = jnp.zeros((16, z.block), wide)
        for k in range(2):
            bias = jnp.where(line == k, e.b1[i, k : k + 1].astype(wide), bias)
            bias = jnp.where(line == 2 + k, e.b2[i, k : k + 1].astype(wide), bias)
        e.packed[at, 4 * z.block : 4 * z.block + 16] = bias.astype(narrow)


def own_weights(e, wa):
    z = e.z
    return e.packed.at[pl.ds(wa * z.own_blocks, z.own_blocks)]


def send_weights(e):
    own = own_weights(e, e.wa)
    peers = [e.sibling] + e.y_peers
    return [
        remote(e, own, own, e.send_w.at[j], e.recv_w.at[j], peer) for j, peer in enumerate(peers)
    ]


def forward_weights(e, copies):
    z = e.z
    arrive(copies[1:])
    more = []
    for j in range(1, z.n_y):
        slab = own_weights(e, lax.rem(e.wa + z.n_wa - 2 * j, z.n_wa))
        at = z.n_y + j - 1
        more.append(remote(e, slab, slab, e.send_w.at[at], e.recv_w.at[at], e.sibling))
    return copies + more


def spread(z, index):
    row = lax.broadcasted_iota(jnp.int32, (z.block, z.lanes), 0)
    lane = lax.broadcasted_iota(jnp.int32, (z.block, z.lanes), 1)
    return jnp.where(lane == row + index * z.block, 1.0, 0.0).astype(narrow)


def build_weights(e):
    z = e.z
    n, lanes = z.block, z.lanes
    for half in range(halves):
        bias = jnp.zeros((16, lanes), wide)
        for i in range(z.half_blocks):
            source = e.packed[half * z.half_blocks + i, : 4 * n + 16]
            placed = dot(source, spread(z, i))
            bias = bias + placed[4 * n :]
            for k, target in ((0, e.big1), (1, e.big2)):
                real = placed[2 * k * n : (2 * k + 1) * n]
                imag = placed[(2 * k + 1) * n : (2 * k + 2) * n]
                up, down = pl.ds(i * n, n), pl.ds(lanes + i * n, n)
                target[half, up, :lanes] = real.astype(narrow)
                target[half, up, lanes:] = imag.astype(narrow)
                target[half, down, :lanes] = (-imag).astype(narrow)
                target[half, down, lanes:] = real.astype(narrow)
        e.bias[half] = bias


def modes_forward(e, rows, half):
    z = e.z
    spec = modes_from_slots(e, rows, e.lat[half]).astype(narrow)
    e.spec[half] = spec
    bias = e.bias[half]
    bias1 = jnp.concatenate([bias[0:1], bias[1:2]], 1)
    bias2 = jnp.concatenate([bias[2:3], bias[3:4]], 1)
    hid, slope = gelu_with_slope(dot(spec, e.big1[half]) + bias1)
    e.slope1[half] = slope
    hid = hid.astype(narrow)
    e.hid[half] = hid
    two = dot(hid, e.big2[half]) + bias2
    bent = jnp.tanh(two * (1.0 / threshold))
    e.slope2[half] = bent * bent
    return (two - threshold * bent).astype(narrow)


def modes_backward(e, rows, half):
    z = e.z
    grad_two = (modes_from_slots(e, rows, e.lat[half]) * e.slope2[half]).astype(narrow)
    e.grad_two[half] = grad_two
    grad_hid = dot_right_transposed(grad_two, e.big2[half])
    grad_one = (grad_hid * e.slope1[half]).astype(narrow)
    e.grad_one[half] = grad_one
    return dot_right_transposed(grad_one, e.big1[half]).astype(narrow)


def outer_parts(z, left, right):
    lanes = z.lanes
    product = dot_left_transposed(left, right)
    real = product[:lanes, :lanes] + product[lanes:, lanes:]
    imag = product[:lanes, lanes:] - product[lanes:, :lanes]
    return real.astype(narrow), imag.astype(narrow)


def spectral_grads(e, half):
    z = e.z
    n, lanes = z.block, z.lanes
    real1, imag1 = outer_parts(z, e.spec[half], e.grad_one[half])
    real2, imag2 = outer_parts(z, e.hid[half], e.grad_two[half])
    bias1 = jnp.sum(e.grad_one[half].astype(wide), 0, keepdims=True)
    bias2 = jnp.sum(e.grad_two[half].astype(wide), 0, keepdims=True)
    line = lax.broadcasted_iota(jnp.int32, (16, lanes), 0)
    bias = jnp.zeros((16, lanes), wide)
    for k, row in enumerate((bias1[:, :lanes], bias1[:, lanes:], bias2[:, :lanes], bias2[:, lanes:])):
        bias = jnp.where(line == k, row, bias)
    bias = bias.astype(narrow)
    for i in range(z.half_blocks):
        at = half * z.half_blocks + i
        owner = at // z.own_blocks
        target = e.grad_pack.at[owner // 2, owner % 2, at % z.own_blocks]
        parts = [value[i * n : (i + 1) * n] for value in (real1, imag1, real2, imag2)]
        stacked = jnp.concatenate(parts + [bias], 0)
        target[: 4 * n + 16] = dot_right_transposed(stacked, spread(z, i)).astype(narrow)
        if z.pack > 4 * n + 16:
            target[4 * n + 16 :] = jnp.zeros((z.pack - 4 * n - 16, n), narrow)


class WaSum:
    def __init__(self, e, name, partial):
        self.e, self.partial = e, partial
        for part in ("recv_core", "slots_y", "done"):
            setattr(self, part, getattr(e, name + "_" + part))
        self.sems = {
            part: getattr(e, name + "_" + part)
            for part in ("ss_core", "rs_core", "ss_y", "rs_y", "ss_done", "rs_done")
        }
        self.core, self.y, self.last = {}, {}, {}

    def own(self):
        part = self.e.z.part
        return pl.ds(pl.multiple_of(self.e.core * part, 16), part)

    def other(self):
        part = self.e.z.part
        return pl.ds(pl.multiple_of((1 - self.e.core) * part, 16), part)

    def start(self, c, values):
        e, s = self.e, self.sems
        self.partial[c] = values.astype(narrow)
        self.core[c] = remote(
            e,
            self.partial.at[c, self.other()], self.recv_core.at[c],
            s["ss_core"].at[c], s["rs_core"].at[c], e.sibling,
        )

    def middle(self, c):
        e, s = self.e, self.sems
        self.core[c].wait_recv()
        both = self.partial[c, self.own()].astype(wide) + self.recv_core[c].astype(wide)
        self.slots_y[c, e.y] = both.astype(narrow)
        slot = self.slots_y.at[c, e.y]
        self.y[c] = [
            remote(e, slot, slot, s["ss_y"].at[c, j], s["rs_y"].at[c, j], peer)
            for j, peer in enumerate(e.y_peers)
        ]

    def end(self, c):
        e, s = self.e, self.sems
        arrive(self.y[c])
        value = self.slots_y[c, 0].astype(wide)
        for k in range(1, e.z.n_y):
            value = value + self.slots_y[c, k].astype(wide)
        self.done[c, self.own()] = value.astype(narrow)
        rows = self.done.at[c, self.own()]
        self.last[c] = remote(e, rows, rows, s["ss_done"].at[c], s["rs_done"].at[c], e.sibling)

    def value(self, c):
        self.last[c].wait_recv()


def wa_sum_scratch(s, z, name):
    s.vmem(name + "_recv_core", (z.chunks, z.part, z.channels))
    s.vmem(name + "_slots_y", (z.chunks, z.n_y, z.part, z.channels))
    s.vmem(name + "_done", (z.chunks, z.chunk, z.channels))
    for part in ("ss_core", "rs_core", "ss_done", "rs_done"):
        s.dma(name + "_" + part, (z.chunks,))
    for part in ("ss_y", "rs_y"):
        s.dma(name + "_" + part, (z.chunks, max(z.n_y - 1, 1)))


def cube_levels(rows, n_sp, swap=False):
    bits = [2**k for k in range(n_sp.bit_length() - 1)]
    if swap:
        bits[:2] = bits[1::-1]
    levels = []
    for bit in bits:
        halve = rows % 32 == 0
        rows = rows // 2 if halve else rows
        levels.append((bit, halve, rows))
    return levels


class CubeSum:
    def __init__(self, e, block, landed, out, send, recv, chunk):
        self.e, self.block, self.landed, self.out = e, block, landed, out
        self.send, self.recv, self.chunk = send, recv, chunk
        self.rows = block.shape[0]
        self.levels = cube_levels(self.rows, e.z.n_sp, chunk in SWAPPED)
        self.start, self.size = 0, self.rows
        self.step, self.copies, self.spans = 0, [], []
        self.steps = self.begin()

    def peer(self, bit):
        e = self.e
        mine = lax.rem(lax.div(e.sp, bit), 2)
        return mine, (e.sp + bit - 2 * bit * mine, e.wa)

    def rows_at(self, start, size):
        return pl.ds(pl.multiple_of(start, 16), size)

    def post(self, source, target, peer):
        k = self.step
        self.step += 1
        sems = (self.send.at[self.chunk, k], self.recv.at[self.chunk, k])
        copy = remote(self.e, source, target, *sems, peer)
        self.copies.append(copy)
        return copy

    def begin(self):
        offset = 0
        for bit, halve, size in self.levels:
            mine, peer = self.peer(bit)
            self.spans.append((bit, halve, self.start, self.size))
            if halve:
                keep = self.start + mine * size
                give = self.start + (1 - mine) * size
            else:
                keep = give = self.start
            target = self.landed.at[offset : offset + size]
            copy = self.post(self.block.at[self.rows_at(give, size)], target, peer)
            yield
            copy.wait_recv()
            own = self.rows_at(keep, size)
            value = self.block[own].astype(wide) + target[...].astype(wide)
            if not halve:
                copy.wait_send()
            self.block[own] = value.astype(narrow)
            self.start, self.size = keep, size
            offset += size
        own = self.rows_at(self.start, self.size)
        self.out[own] = self.block[own]
        for bit, halve, start, size in reversed(self.spans):
            if halve:
                mine, peer = self.peer(bit)
                rows = self.out.at[self.rows_at(self.start, self.size)]
                copy = self.post(rows, rows, peer)
                yield
                copy.wait_recv()
            self.start, self.size = start, size

    def advance(self):
        return next(self.steps, None)


def cube_landed_rows(rows, n_sp):
    return sum(size for _, _, size in cube_levels(rows, n_sp))


def exchange_small(e, own, landed, send, recv):
    landed[e.sp] = own
    return spread_slot(e, landed, send, recv)


def spread_slot(e, landed, send, recv):
    slot = landed.at[e.sp]
    for peer in e.sp_peers:
        start_remote(slot, slot, send.at[0], recv.at[0], peer)
    rest = others(e)
    return Group(e, landed.at[rest], landed.at[rest], send.at[0], recv.at[0])


def sum_small(e, landed, group):
    group.wait_recv()
    value = landed[0]
    for k in range(1, e.z.n_sp):
        value = value + landed[k]
    return value


def place_rows(rows, width):
    line = lax.broadcasted_iota(jnp.int32, (8, width), 0)
    result = jnp.zeros((8, width), wide)
    for k, row in rows:
        if row.shape[1] < width:
            row = jnp.concatenate([row, jnp.zeros((1, width - row.shape[1]), wide)], 1)
        result = jnp.where(line == k, row, result)
    return result


def spec_sum_start(e):
    z = e.z
    return [
        remote(
            e,
            e.grad_pack.at[:, 1 - e.core], e.pack_core, e.ss_pack.at[0], e.rs_pack.at[0], e.sibling
        )
    ]


def spec_sum_middle(e, copies):
    z = e.z
    arrive(copies)
    for k in range(z.n_y):
        both = e.grad_pack[k, e.core].astype(wide) + e.pack_core[k].astype(wide)
        e.pack_send[k] = both.astype(narrow)
    new = [
        remote(
            e,
            e.pack_send.at[lax.rem(e.y + j + 1, z.n_y)], e.pack_y.at[e.y],
            e.ss_pack.at[1 + j], e.rs_pack.at[1 + j], peer,
        )
        for j, peer in enumerate(e.y_peers)
    ]
    e.pack_y[e.y] = e.pack_send[e.y]
    return new


def spec_sum_scatter(e, copies):
    z = e.z
    arrive(copies)
    value = e.pack_y[0].astype(wide)
    for k in range(1, z.n_y):
        value = value + e.pack_y[k].astype(wide)
    e.pack_sum[...] = value.reshape(z.n_sp, z.pack_share, z.block).astype(narrow)
    e.pack_landed[e.sp] = e.pack_sum[e.sp]
    for peer in e.sp_peers:
        start_remote(
            e.pack_sum.at[peer[0]], e.pack_landed.at[e.sp], e.ss_share.at[0], e.rs_share.at[0], peer
        )
    rest = others(e)
    return [
        Group(e, e.pack_sum.at[rest], e.pack_landed.at[rest], e.ss_share.at[0], e.rs_share.at[0])
    ]


def spec_sum_gather(e, copies):
    z = e.z
    arrive(copies)
    value = e.pack_landed[0].astype(wide)
    for k in range(1, z.n_sp):
        value = value + e.pack_landed[k].astype(wide)
    e.pack_out[e.sp] = value.astype(narrow)
    return [spread_slot(e, e.pack_out, e.ss_whole, e.rs_whole)]


def first_norm(e, c):
    gain, shift = line(e.gain1), line(e.shift1)
    for start, size in row_parts(e.z, c):
        values = field_rows(e, e.xs, c, start, size).astype(wide)
        center = mean(values)
        centred = values - center
        inv_std = lax.rsqrt(mean(centred * centred) + 1e-05)
        rows = pl.ds(start, size)
        e.xn[c, rows] = (centred * inv_std * gain + shift).astype(narrow)
        e.stats[c, rows, 0:1] = center
        e.stats[c, rows, 1:2] = inv_std


def second_norm(e, c):
    gain, shift = line(e.gain2), line(e.shift2)
    for start, size in row_parts(e.z, c):
        rows = pl.ds(start, size)
        values = e.mixed[c, rows]
        center = mean(values)
        centred = values - center
        inv_std = lax.rsqrt(mean(centred * centred) + 1e-05)
        e.xn2[c, rows] = (centred * inv_std * gain + shift).astype(narrow)
        e.stats[c, rows, 2:3] = center
        e.stats[c, rows, 3:4] = inv_std


def second_norm_backward(e, c, gain_grad, shift_grad):
    gain = line(e.gain2)
    for start, size in row_parts(e.z, c):
        rows = pl.ds(start, size)
        grad = e.grads_done[c, rows].astype(wide)
        inv_std = e.stats[c, rows, 3:4]
        hat = (e.mixed[c, rows] - e.stats[c, rows, 2:3]) * inv_std
        gain_grad = gain_grad + total(grad * hat)
        shift_grad = shift_grad + total(grad)
        scaled = grad * gain
        back = inv_std * (scaled - mean(scaled) - hat * mean(scaled * hat))
        e.xn[c, rows] = (e.gp[c, rows].astype(wide) + back).astype(narrow)
    return gain_grad, shift_grad


def first_norm_sums(e, c, gain_grad, shift_grad):
    for start, size in row_parts(e.z, c):
        rows = pl.ds(start, size)
        grad = e.xn2[c, rows].astype(wide)
        values = field_rows(e, e.xs, c, start, size).astype(wide)
        hat = (values - e.stats[c, rows, 0:1]) * e.stats[c, rows, 1:2]
        gain_grad = gain_grad + total(grad * hat)
        shift_grad = shift_grad + total(grad)
    return gain_grad, shift_grad


def first_norm_backward(e, c):
    gain = line(e.gain1)
    for start, size in row_parts(e.z, c):
        rows = pl.ds(start, size)
        grad = e.xn2[c, rows].astype(wide)
        inv_std = e.stats[c, rows, 1:2]
        values = field_rows(e, e.xs, c, start, size).astype(wide)
        hat = (values - e.stats[c, rows, 0:1]) * inv_std
        scaled = grad * gain
        back = inv_std * (scaled - mean(scaled) - hat * mean(scaled * hat))
        e.xn[c, rows] = (e.xn[c, rows].astype(wide) + back).astype(narrow)


def whole_body(e):
    z = e.z
    chunks = range(z.chunks)
    x_loads = [
        local_copy(e, e.hbm_x.at[p], e.xs.at[p], e.load_x.at[p]) for p in range(z.planes)
    ]
    loads = {}
    for index, name in enumerate(z.loaded):
        source = getattr(e, "hbm_" + name)
        if name == "long_rows":
            source = source.at[:, e.wa]
        elif name == "gs":
            source = source.at[pl.ds(0, 1)]
        loads[name] = local_copy(e, source, getattr(e, name), e.load.at[index])

    def need(*names):
        for name in names:
            loads.pop(name).wait()

    greet(e)
    clear_padding(e, e.xn)
    clear_padding(e, e.xn2)
    clear_padding(e, e.gp)
    need("w1", "b1", "w2", "b2")
    pack_weights(e)
    need("gain1", "shift1", "long_rows", "slot_rows")
    table = e.long_rows[0]
    for p in range(z.planes):
        x_loads[p].wait()
        first_norm(e, 2 * p)
        first_norm(e, 2 * p + 1)
        if p == 0:
            greeted(e)
            weights = send_weights(e)
        first = columns_to_slots(e, table, "a", p)

    need("gs")
    bias2_grad = jnp.zeros((1, z.channels), wide)
    for c in chunks:
        for start, size in row_parts(z, c):
            values = field_rows(e, e.gs, c % 2, start, size)
            e.gp[c, start : start + size] = values
            bias2_grad = bias2_grad + total(values.astype(wide))
        if c % 2 == 1 and c // 2 + 1 < z.planes:
            source = e.hbm_gs.at[pl.ds(c // 2 + 1, 1)]
            local_copy(e, source, e.gs, e.load.at[z.loaded.index("gs")]).wait()
    need("fc2")
    for p in range(z.planes):
        rows = e.gp[2 * p : 2 * p + 2].reshape(z.pitch, z.channels)
        grad_act = dot_right_transposed(rows, e.fc2[...]).astype(narrow)
        e.gh[2 * p : 2 * p + 2] = grad_act.reshape(2, z.chunk, z.hidden)
    weights = forward_weights(e, weights)
    arrive(weights)
    build_weights(e)
    need("lat", "lat_cols")
    first.wait_recv()
    rows = mode_rows(e, e.landed_a)
    second = modes_to_slots(e, [modes_forward(e, rows, half) for half in range(halves)], "b")
    need("slot_cols", "long_out", "gain2", "shift2", "fc1", "fc1_bias", "fc2_bias")
    gather = Gather(e, e.gathered, "")
    gather.start(second[0], e.landed_b, 0)
    gather.start(second[1], e.landed_b, 1)
    gather.forward(0)
    for p in range(2, z.planes):
        gather.start(second[p], e.landed_b, p)
    finish(second)

    grads = WaSum(e, "grads", e.xn)
    bias1 = line(e.fc1_bias).astype(wide)
    bias1_grad = jnp.zeros((1, z.hidden), wide)
    for p in range(z.planes):
        filtered = gather.rows(e.long_out[1], p).astype(narrow).astype(wide)
        pair = (2 * p, 2 * p + 1)
        for c in pair:
            size = chunk_rows(z, c)
            at = (c % 2) * z.chunk
            values = field_rows(e, e.xs, c, 0, size).astype(wide)
            e.mixed[c, pl.ds(0, size)] = values + filtered[at : at + size]
            second_norm(e, c)
        if p >= 1:
            grads.middle(2 * p - 2)
            grads.middle(2 * p - 1)
        both = slice(2 * p, 2 * p + 2)
        rows = e.xn2[both].reshape(z.pitch, z.channels)
        hidden, slope = gelu_with_slope(dot(rows, e.fc1[...]) + bias1)
        e.act[both] = hidden.astype(narrow).reshape(2, z.chunk, z.hidden)
        grad_hidden = e.gh[both].reshape(z.pitch, z.hidden).astype(wide) * slope
        grad_hidden = grad_hidden.astype(narrow)
        e.gh[both] = grad_hidden.reshape(2, z.chunk, z.hidden)
        if p + 1 < z.planes:
            gather.forward(p + 1)
        part = dot_right_transposed(grad_hidden, e.fc1[...])
        for c in pair:
            grads.start(c, part[(c % 2) * z.chunk : (c % 2 + 1) * z.chunk])
        bias1_grad = bias1_grad + total(grad_hidden.astype(wide))
    all_rows = z.chunks * z.chunk
    sources = (
        (e.xn2, e.gh, e.sum1, e.landed1, e.total1, z.channels),
        (e.act, e.gp, e.sum2, e.landed2, e.total2, z.hidden),
    )
    cubes = []

    def tick(name):
        for index in SCHEDULE.get(name, ()):
            cubes[index].advance()

    for index, (left, right, block, landed, out, rows) in enumerate(sources):
        size = rows // cuts
        for k in range(cuts):
            part = left[:, :, k * size : (k + 1) * size].reshape(all_rows, size)
            value = dot_left_transposed(part, right[...].reshape(all_rows, right.shape[-1]))
            block[k] = value.astype(narrow)
            cube = CubeSum(
                e, block.at[k], landed.at[k], out.at[pl.ds(k * size, size)],
                e.send_cube, e.recv_cube, cuts * index + k,
            )
            cubes.append(cube)
            if len(cubes) == 1:
                grads.middle(z.chunks - 2)
                grads.middle(z.chunks - 1)
            tick("c%d" % (cuts * index + k))
    gain2_grad = jnp.zeros((1, z.channels), wide)
    shift2_grad = jnp.zeros((1, z.channels), wide)
    table = e.long_rows[1]
    branch = WaSum(e, "branch", e.xn2)
    for c in range(z.chunks + 1):
        if c < z.chunks:
            tick("q%d" % c)
            grads.end(c)
        if c >= 1:
            last = c - 1
            grads.value(last)
            finish([grads.core[last]])
            gain2_grad, shift2_grad = second_norm_backward(e, last, gain2_grad, shift2_grad)
            if last % 2 == 1:
                third = columns_to_slots(e, table, "c", last // 2)
                rows = e.act[last - 1 : last + 1].reshape(z.pitch, z.hidden)
                part = dot(rows, e.fc2[...])
                branch.start(last - 1, part[: z.chunk])
                branch.start(last, part[z.chunk :])
            tick("n%d" % last)

    rows = [(0, bias1_grad), (1, bias2_grad), (2, gain2_grad), (3, shift2_grad)]
    small_one = exchange_small(
        e, place_rows(rows, z.small), e.small_one, e.send_one, e.recv_one
    )
    early, late = chunks[:EARLY], chunks[EARLY:]
    for c in early:
        branch.middle(c)
        tick("m%d" % c)
    third.wait_recv()
    tick("v")
    rows = mode_rows(e, e.landed_c)
    fourth = modes_to_slots(e, [modes_backward(e, rows, half) for half in range(halves)], "d")
    tick("w0")
    for half in range(halves):
        spectral_grads(e, half)
        tick("s%d" % half)
    packs = [spec_sum_start(e)]
    writes = []
    bias = e.fc2_bias[...].reshape(1, -1).astype(wide)

    def write_output(c):
        branch.value(c)
        finish([branch.last[c]])
        for start, size in row_parts(z, c):
            rows = pl.ds(start, size)
            value = e.mixed[c, rows] + (e.branch_done[c, rows].astype(wide) + bias)
            e.branch_done[c, rows] = value.astype(narrow)
        writes.append(local_copy(e, e.branch_done.at[c], e.hbm_output.at[c], e.write_sems.at[c]))

    packs.append(spec_sum_middle(e, packs[-1]))
    gather = Gather(e, e.gathered2, "2")
    for p in range(z.planes):
        gather.start(fourth[p], e.landed_d, p)
        if p + 1 == z.planes:
            packs.append(spec_sum_scatter(e, packs[-1]))
        tick("g%d" % p)
    for c in late:
        branch.middle(c)
        tick("m%d" % c)
    for c in early:
        branch.end(c)
    for c in early:
        write_output(c)
        tick("o%d" % c)
    finish(branch.core.values())
    packs.append(spec_sum_gather(e, packs[-1]))
    gain1_grad = jnp.zeros((1, z.channels), wide)
    shift1_grad = jnp.zeros((1, z.channels), wide)
    for p in range(z.planes):
        gather.forward(p)
        grad = gather.rows(e.long_out[0], p).astype(narrow)
        e.xn2[2 * p : 2 * p + 2] = grad.reshape(2, z.chunk, z.channels)
        for c in (2 * p, 2 * p + 1):
            gain1_grad, shift1_grad = first_norm_sums(e, c, gain1_grad, shift1_grad)
        if p + 1 == z.planes:
            small_two = exchange_small(
                e, place_rows([(0, gain1_grad), (1, shift1_grad)], z.small),
                e.small_two, e.send_two, e.recv_two,
            )
        for c in (2 * p, 2 * p + 1):
            first_norm_backward(e, c)
            writes.append(local_copy(e, e.xn.at[c], e.hbm_fields_grad.at[c], e.write_sems2.at[c]))
        tick("f%d" % p)
    for c in late:
        branch.end(c)
    for c in late:
        write_output(c)
        tick("l%d" % c)
    tick("p")
    arrive(packs[-1])
    writes.append(local_copy(e, e.pack_out, e.hbm_pack, e.store.at[0]))
    e.small_out[0] = sum_small(e, e.small_one, small_one)
    e.small_out[1] = sum_small(e, e.small_two, small_two)
    writes.append(local_copy(e, e.small_out, e.hbm_small, e.store.at[1]))
    for _ in range(max(len(cube.levels) for cube in cubes) * 2):
        for cube in cubes:
            cube.advance()
    for index, cube in enumerate(cubes):
        cube.advance()
        target = e.hbm_fc1_grad if index < cuts else e.hbm_fc2_grad
        rows = cube.rows
        target = target.at[pl.ds((index % cuts) * rows, rows)]
        writes.append(local_copy(e, cube.out, target, e.store.at[2 + index]))
    arrive(e.copies)
    finish(e.copies)
    for write in writes:
        write.wait()


class Names:
    def __init__(self):
        self.names, self.shapes = [], []

    def add(self, name, shape):
        self.names.append(name)
        self.shapes.append(shape)

    def vmem(self, name, shape, dtype=narrow):
        self.add(name, pltpu.VMEM(shape, dtype))

    def dma(self, name, shape):
        self.add(name, pltpu.SemaphoreType.DMA(shape))


def scratch_of(z):
    s = Names()
    fields = (z.planes, z.width, z.fields, z.channels)
    rows = (z.chunks, z.chunk, z.channels)
    hidden = (z.chunks, z.chunk, z.hidden)
    s.vmem("xs", fields)
    lat_rows = z.n_sp * z.planes * z.plane_slot
    n = z.block
    for name, shape, dtype in (
        ("w1", (z.own_blocks, 2 * n, n), narrow), ("b1", (z.own_blocks, 2, n), narrow),
        ("w2", (z.own_blocks, 2 * n, n), narrow), ("b2", (z.own_blocks, 2, n), narrow),
        ("gain1", (z.channels,), wide), ("shift1", (z.channels,), wide),
        ("gain2", (z.channels,), wide), ("shift2", (z.channels,), wide),
        ("fc1", (z.channels, z.hidden), narrow), ("fc1_bias", (z.hidden,), narrow),
        ("fc2", (z.hidden, z.channels), narrow), ("fc2_bias", (z.channels,), narrow),
        ("gs", (1,) + fields[1:], narrow), ("long_rows", (2, z.group, z.pitch), narrow),
        ("slot_rows", (halves, z.n_sp * z.plane_slot, z.group), narrow),
        ("slot_cols", (halves, z.group, z.n_sp * z.plane_slot), narrow),
        ("lat", (halves, 2 * z.count, lat_rows), narrow),
        ("lat_cols", (halves, lat_rows, 2 * z.count), narrow),
        ("long_out", (2, z.pitch, z.n_wa * z.group), narrow),
    ):
        s.vmem(name, shape, dtype)
    s.dma("load_x", (z.planes,))
    s.dma("load", (len(z.loaded),))
    s.dma("store", (2 + 2 * cuts,))
    s.dma("write_sems", (z.chunks,))
    s.dma("write_sems2", (z.chunks,))
    for name in ("xn", "gp", "xn2"):
        s.vmem(name, rows)
    s.vmem("act", hidden)
    s.vmem("gh", hidden)
    s.vmem("mixed", rows, wide)
    s.vmem("stats", (z.chunks, z.chunk, 4), wide)
    for name in ("slots_a", "slots_b", "slots_c", "slots_d", "landed_a", "landed_b", "landed_c", "landed_d"):
        s.vmem(name, (z.n_sp, z.planes, z.plane_slot, z.lanes))
    for tag in "abcd":
        s.dma("send_" + tag, (z.planes,))
        s.dma("recv_" + tag, (z.planes,))
    for tag in ("", "2"):
        s.vmem("gathered" + tag, (z.planes, z.n_wa, z.group, z.channels))
        for name in ("send_y", "recv_y"):
            s.dma(name + tag, (z.planes, max(z.n_y - 1, 1)))
        for name in ("send_core", "recv_core"):
            s.dma(name + tag, (z.planes, z.n_y))
    s.vmem("packed", (z.blocks, z.pack, z.block))
    s.vmem("bias", (halves, 16, z.lanes), wide)
    s.dma("send_w", (2 * z.n_y - 1,))
    s.dma("recv_w", (2 * z.n_y - 1,))
    both = (halves, z.count, 2 * z.lanes)
    for name in ("spec", "hid", "grad_one", "grad_two"):
        s.vmem(name, both)
    s.vmem("slope1", both, wide)
    s.vmem("slope2", both, wide)
    for name in ("big1", "big2"):
        s.vmem(name, (halves, 2 * z.lanes, 2 * z.lanes))
    s.vmem("grad_pack", (z.n_y, 2, z.own_blocks, z.pack, z.block))
    for name in ("pack_core", "pack_send", "pack_y"):
        s.vmem(name, (z.n_y, z.own_blocks, z.pack, z.block))
    s.vmem("pack_out", (z.n_sp, z.pack_share, z.block))
    s.vmem("small_out", (2, 8, z.small), wide)
    s.vmem("pack_sum", (z.n_sp, z.pack_share, z.block))
    s.vmem("pack_landed", (z.n_sp, z.pack_share, z.block))
    for name in ("ss_pack", "rs_pack"):
        s.dma(name, (z.n_y,))
    for name in ("ss_share", "rs_share", "ss_whole", "rs_whole"):
        s.dma(name, (1,))
    wa_sum_scratch(s, z, "grads")
    wa_sum_scratch(s, z, "branch")
    for tag, rows, lanes in (("1", z.channels, z.hidden), ("2", z.hidden, z.channels)):
        s.vmem("sum" + tag, (cuts, rows // cuts, lanes))
        s.vmem("total" + tag, (rows, lanes))
        s.vmem("landed" + tag, (cuts, cube_landed_rows(rows // cuts, z.n_sp), lanes))
    steps = 2 * len(cube_levels(z.channels, z.n_sp))
    s.dma("send_cube", (2 * cuts, steps))
    s.dma("recv_cube", (2 * cuts, steps))
    for tag in ("one", "two"):
        s.vmem("small_" + tag, (z.n_sp, 8, z.small), wide)
        s.dma("send_" + tag, (1,))
        s.dma("recv_" + tag, (1,))
    return s


def call_kernel(body, z, inputs, outputs, scratch, collective):
    names = [name for name, _ in inputs] + [name for name, _, _ in outputs]

    def kernel(*refs):
        e = types.SimpleNamespace(z=z)
        for name, ref in zip(names + scratch.names, refs):
            setattr(e, name, ref)
        e.copies = []
        place(e)
        body(e)

    def spec(name):
        return pl.BlockSpec(memory_space=pl.ANY if name.startswith("hbm_") else pltpu.VMEM)

    return pl.pallas_call(
        kernel,
        out_shape=[jax.ShapeDtypeStruct(shape, dtype) for _, shape, dtype in outputs],
        in_specs=[spec(name) for name, _ in inputs],
        out_specs=[spec(name) for name, _, _ in outputs],
        scratch_shapes=scratch.shapes,
        compiler_params=pltpu.CompilerParams(
            collective_id=collective,
            has_side_effects=collective is not None,
            vmem_limit_bytes=61 * 1024 * 1024,
        ),
    )(*[value for _, value in inputs])


def finish_body(e):
    z = e.z
    loads, writes = [], []
    pairs = [
        (source.at[c], target.at[c])
        for source, target in ((e.hbm_output, e.rows_output), (e.hbm_fields, e.rows_fields))
        for c in range(z.chunks)
    ]
    pairs += [
        (e.hbm_fc1, e.rows_fc1), (e.hbm_fc2, e.rows_fc2), (e.hbm_pack, e.pack), (e.hbm_small, e.small)
    ]
    for index, (source, target) in enumerate(pairs):
        loads.append(local_copy(e, source, target, e.load.at[index]))

    def write(source, target):
        writes.append(local_copy(e, source, target, e.store.at[len(writes)]))

    for index, (rows, wide_rows, target) in enumerate(
        (
            (e.rows_output, e.wide_output, e.hbm_output_out),
            (e.rows_fields, e.wide_fields, e.hbm_fields_out),
        )
    ):
        for c in range(z.chunks):
            loads[index * z.chunks + c].wait()
            for start, size in row_parts(z, c, 96):
                values = rows[c, start : start + size].astype(wide)
                first = ((c % 2) * z.chunk + start) // z.fields
                wide_rows[c // 2, first : first + size // z.fields] = values.reshape(
                    size // z.fields, z.fields, z.channels
                )
            if c % 2 == 1:
                write(wide_rows.at[c // 2], target.at[c // 2])
    for index, (rows, wide_rows, target) in enumerate(
        ((e.rows_fc1, e.wide_fc1, e.hbm_fc1_out), (e.rows_fc2, e.wide_fc2, e.hbm_fc2_out))
    ):
        loads[2 * z.chunks + index].wait()
        wide_rows[...] = rows[...].astype(wide)
        write(wide_rows, target)
    for load in loads[2 * z.chunks + 2 :]:
        load.wait()
    n = z.block
    e.w1[...] = e.pack[:, : 2 * n].astype(wide)
    e.w2[...] = e.pack[:, 2 * n : 4 * n].astype(wide)
    bias = e.pack[:, 4 * n : 4 * n + 16].astype(wide)
    e.b1[...] = bias[:, 0:2]
    e.b2[...] = bias[:, 2:4]
    small = e.small[...]
    e.gain1[...] = small[1, 0, : z.channels]
    e.shift1[...] = small[1, 1, : z.channels]
    e.gain2[...] = small[0, 2, : z.channels]
    e.shift2[...] = small[0, 3, : z.channels]
    e.fc1_bias[...] = small[0, 0, : z.hidden]
    e.fc2_bias[...] = small[0, 1, : z.channels]
    for name in z.small_names:
        write(getattr(e, name), getattr(e, "hbm_out_" + name))
    for copy in writes:
        copy.wait()


def finish_call(z, output, fields_grad, fc1, fc2, pack, small):
    channels, hidden, n = z.channels, z.hidden, z.block
    inputs = [
        ("hbm_output", output), ("hbm_fields", fields_grad), ("hbm_fc1", fc1), ("hbm_fc2", fc2),
        ("hbm_pack", pack.reshape(z.own_blocks, z.pack, n)), ("hbm_small", small),
    ]
    fields = (z.planes, z.width, z.fields, channels)
    smalls = {
        "gain1": (channels,), "shift1": (channels,),
        "w1": (z.own_blocks, 2 * n, n), "b1": (z.own_blocks, 2, n),
        "w2": (z.own_blocks, 2 * n, n), "b2": (z.own_blocks, 2, n),
        "gain2": (channels,), "shift2": (channels,),
        "fc1_bias": (hidden,), "fc2_bias": (channels,),
    }
    z.small_names = tuple(smalls)
    outputs = [("hbm_output_out", fields, wide), ("hbm_fields_out", fields, wide)]
    outputs += [("hbm_out_" + name, shape, wide) for name, shape in smalls.items()]
    outputs += [
        ("hbm_fc1_out", (channels, hidden), wide), ("hbm_fc2_out", (hidden, channels), wide),
    ]
    s = Names()
    s.vmem("rows_output", output.shape)
    s.vmem("rows_fields", fields_grad.shape)
    s.vmem("rows_fc1", fc1.shape)
    s.vmem("rows_fc2", fc2.shape)
    s.vmem("pack", (z.own_blocks, z.pack, n))
    s.vmem("small", small.shape, wide)
    s.vmem("wide_output", fields, wide)
    s.vmem("wide_fields", fields, wide)
    s.vmem("wide_fc1", fc1.shape, wide)
    s.vmem("wide_fc2", fc2.shape, wide)
    for name, shape in smalls.items():
        s.vmem(name, shape, wide)
    s.dma("load", (2 * z.chunks + 4,))
    s.dma("store", (2 * z.planes + 2 + len(smalls),))
    results = call_kernel(finish_body, z, inputs, outputs, s, None)
    named = dict(zip(smalls, results[2:-2]))
    return results[0], results[1], results[-2], results[-1], named


def local(
    fields_in,
    norm1_gain,
    norm1_shift,
    spec_w1,
    spec_b1,
    spec_w2,
    spec_b2,
    norm2_gain,
    norm2_shift,
    fc1_weight,
    fc1_bias,
    fc2_weight,
    fc2_bias,
    out_grad,
):
    fields, rows_here, width, channels = fields_in.shape
    n_sp, n_wa = lax.axis_size("sp"), lax.axis_size("wa")
    block, hidden = spec_w1.shape[2], fc1_weight.shape[1]
    z = plan(
        n_sp, n_wa, fields, rows_here, width, channels, channels // block, block, hidden
    )
    long_rows, long_out = longitude_tables(z)
    index, lat = plane_tables(z, slot_index(z), latitude_table(z))
    tables = [
        jnp.asarray(np.ascontiguousarray(table))
        for table in (
            long_rows, long_out, index, index.transpose(0, 2, 1), lat, lat.transpose(0, 2, 1),
        )
    ]
    own, n = z.own_blocks, block
    turned = lambda value: jnp.transpose(value, (1, 2, 0, 3))
    inputs = [
        ("hbm_x", turned(fields_in)), ("hbm_gs", turned(out_grad)),
        ("hbm_fc1", fc1_weight), ("hbm_fc2", fc2_weight),
        ("hbm_gain1", norm1_gain), ("hbm_shift1", norm1_shift),
        ("hbm_gain2", norm2_gain), ("hbm_shift2", norm2_shift),
        ("hbm_fc1_bias", fc1_bias), ("hbm_fc2_bias", fc2_bias),
        ("hbm_w1", spec_w1.reshape(own, 2 * n, n)), ("hbm_b1", spec_b1),
        ("hbm_w2", spec_w2.reshape(own, 2 * n, n)), ("hbm_b2", spec_b2),
    ]
    names = ("long_rows", "long_out", "slot_rows", "slot_cols", "lat", "lat_cols")
    inputs += [("hbm_" + name, table) for name, table in zip(names, tables)]
    flat = (z.chunks, z.chunk, channels)
    outputs = [
        ("hbm_output", flat, narrow), ("hbm_fields_grad", flat, narrow),
        ("hbm_fc1_grad", (channels, hidden), narrow), ("hbm_fc2_grad", (hidden, channels), narrow),
        ("hbm_pack", (z.n_sp, z.pack_share, n), narrow), ("hbm_small", (2, 8, z.small), wide),
    ]
    output, fields_grad, fc1, fc2, named = finish_call(
        z, *call_kernel(whole_body, z, inputs, outputs, scratch_of(z), 0)
    )
    back = lambda value: jnp.transpose(value, (2, 0, 1, 3))
    shaped = lambda value: value.reshape(own, 2, n, n)
    return (
        back(output), back(fields_grad), named["gain1"], named["shift1"],
        shaped(named["w1"]), named["b1"], shaped(named["w2"]), named["b2"],
        named["gain2"], named["shift2"], fc1, named["fc1_bias"], fc2, named["fc2_bias"],
    )


def solution(mesh):
    return jax.shard_map(
        local,
        mesh=mesh,
        in_specs=(
            P(None, "sp", None, None),
            P(),
            P(),
            P("wa", None, None, None),
            P("wa", None, None),
            P("wa", None, None, None),
            P("wa", None, None),
            P(),
            P(),
            P(None, "wa"),
            P("wa"),
            P("wa", None),
            P(),
            P(None, "sp", None, None),
        ),
        out_specs=(
            P(None, "sp", None, None),
            P(None, "sp", None, None),
            P(),
            P(),
            P("wa", None, None, None),
            P("wa", None, None),
            P("wa", None, None, None),
            P("wa", None, None),
            P(),
            P(),
            P(None, "wa"),
            P("wa"),
            P("wa", None),
            P(),
        ),
        check_vma=False,
    )
```

```python
import functools
import math
import types

import jax
import jax.numpy as jnp
import numpy as np
from jax import lax
from jax.experimental import pallas as pl
from jax.experimental.pallas import tpu as pltpu
from jax.sharding import PartitionSpec as P

threshold = 0.01
narrow = jnp.bfloat16
wide = jnp.float32
MESH = pl.DeviceIdType.MESH
halves = 2


def round_up(value, step):
    return -(-value // step) * step


def phase_angles(rows, columns, period):
    product = rows[:, None] * columns[None, :] % period
    return (np.float32(2.0 * math.pi / period) * product.astype(np.float32)).astype(np.float32)


def plan(n_sp, n_wa, fields, rows_here, width, channels, blocks, block, hidden):
    z = types.SimpleNamespace(
        n_sp=n_sp, n_wa=n_wa, n_y=n_wa // 2, width=width, channels=channels, hidden=hidden,
        blocks=blocks, block=block, fields=fields, planes=rows_here,
    )
    z.period = rows_here * n_sp
    z.modes = width // 2 + 1
    z.each = -(-z.modes // (n_sp * n_wa))
    z.plane = fields * width
    z.pitch = round_up(z.plane, 64)
    z.chunk = z.pitch // 2
    z.chunks = 2 * rows_here
    z.part = z.chunk // 2
    z.lanes = channels // halves
    z.slot = round_up(2 * rows_here * fields * z.each, 8)
    z.group = round_up(2 * n_sp * fields * z.each, 16)
    z.count = z.period * fields * z.each
    z.half_blocks = blocks // halves
    z.own_blocks = blocks // n_wa
    z.pack = round_up(4 * block + 16, 16 * n_sp // math.gcd(16 * n_sp, z.own_blocks))
    z.pack_share = z.own_blocks * z.pack // n_sp
    z.small = max(channels, hidden)
    z.plane_slot = round_up(halves * 2 * fields * z.each, 8)
    z.loaded = (
        "w1", "b1", "w2", "b2", "gain1", "shift1", "long_rows", "slot_rows", "gs", "lat", "lat_cols",
        "slot_cols", "long_out", "gain2", "shift2", "fc1", "fc1_bias", "fc2", "fc2_bias",
    )
    return z


def longitude_tables(z):
    angles = phase_angles(np.arange(z.width), np.arange(z.modes), z.width)
    scale = np.float32(1.0 / math.sqrt(z.width))
    padded = z.each * z.n_sp * z.n_wa
    table = np.zeros((2, padded, z.width), np.float32)
    table[0, : z.modes] = (np.cos(angles) * scale).T
    table[1, : z.modes] = (-np.sin(angles) * scale).T
    k = np.arange(padded)
    weights = np.where((k == 0) | (2 * k == z.width), 1.0, 2.0).astype(np.float32)
    both = np.stack([table, table * weights[None, :, None]])
    both = both.reshape(2, 2, z.n_wa, z.n_sp, z.each, z.width).transpose(0, 2, 1, 3, 4, 5)
    rows = np.zeros((2, z.n_wa, 2, z.n_sp, z.fields, z.each, z.width, z.fields), np.float32)
    for f in range(z.fields):
        rows[:, :, :, :, f, :, :, f] = both
    padded = np.zeros((2, z.n_wa, z.group, z.pitch), np.float32)
    used = 2 * z.n_sp * z.fields * z.each
    padded[:, :, :used, : z.plane] = rows.reshape(2, z.n_wa, used, z.plane)
    out = padded.reshape(2, z.n_wa * z.group, z.pitch).transpose(0, 2, 1)
    return padded.astype(narrow), np.ascontiguousarray(out).astype(narrow)


def slot_index(z):
    table = np.zeros((z.n_sp, z.slot, z.planes, z.group), np.float32)
    for d in range(z.n_sp):
        for c in range(2):
            for h in range(z.planes):
                for f in range(z.fields):
                    for j in range(z.each):
                        r = ((c * z.planes + h) * z.fields + f) * z.each + j
                        table[d, r, h, ((c * z.n_sp + d) * z.fields + f) * z.each + j] = 1.0
    return table.reshape(z.n_sp * z.slot, z.planes * z.group).astype(narrow)


def latitude_table(z):
    angles = phase_angles(np.arange(z.period), np.arange(z.period), z.period)
    scale = np.float32(1.0 / math.sqrt(z.period))
    inner = z.fields * z.each
    cosine = (np.cos(angles) * scale).reshape(z.period, z.n_sp, z.planes)
    sine = (np.sin(angles) * scale).reshape(z.period, z.n_sp, z.planes)
    table = np.zeros((2, z.period, inner, z.n_sp, 2, z.planes, inner), np.float32)
    for i in range(inner):
        table[0, :, i, :, 0, :, i] = cosine
        table[0, :, i, :, 1, :, i] = sine
        table[1, :, i, :, 1, :, i] = cosine
        table[1, :, i, :, 0, :, i] = -sine
    padded = np.zeros((2 * z.count, z.n_sp, z.slot), np.float32)
    padded[:, :, : 2 * z.planes * inner] = table.reshape(2 * z.count, z.n_sp, -1)
    return padded.reshape(2 * z.count, z.n_sp * z.slot).astype(narrow)


def plane_tables(z, index, lat):
    used = 2 * z.fields * z.each
    per = z.planes * used
    shape = (z.n_sp, z.slot, z.planes, z.group)
    moved = np.zeros((halves, z.n_sp, z.plane_slot, z.group), narrow)
    turned = np.zeros((halves, 2 * z.count, z.n_sp, z.planes, z.plane_slot), narrow)
    kept = index.reshape(shape)[:, :per, 0].reshape(z.n_sp, 2, z.planes, -1, z.group)[:, :, 0]
    source = lat.reshape(-1, z.n_sp, z.slot)[:, :, :per].reshape(-1, z.n_sp, 2, z.planes, used // 2)
    source = source.transpose(0, 1, 3, 2, 4).reshape(-1, z.n_sp, z.planes, used)
    for half in range(halves):
        rows = slice(half * used, (half + 1) * used)
        moved[half, :, rows] = kept.reshape(z.n_sp, used, z.group)
        turned[half, ..., rows] = source
    return moved.reshape(halves, -1, z.group), turned.reshape(halves, 2 * z.count, -1)


def dot(left, right):
    return jnp.dot(left, right, preferred_element_type=wide)


def dot_right_transposed(left, right):
    return lax.dot_general(left, right, (((1,), (1,)), ((), ())), preferred_element_type=wide)


def dot_left_transposed(left, right):
    return lax.dot_general(left, right, (((0,), (0,)), ((), ())), preferred_element_type=wide)


def gelu_with_slope(v):
    scale = np.float32(math.sqrt(2.0 / math.pi))
    square = v * v
    bent = jnp.tanh(scale * v * (1.0 + 0.044715 * square))
    above = 0.5 + 0.5 * bent
    slope = above + 0.5 * v * (1.0 - bent * bent) * (scale * (1.0 + (3 * 0.044715) * square))
    return v * above, slope


cuts = 3
EARLY = 4
SWAPPED = (0,)
SCHEDULE = {'c0': (0,), 'q4': (2, 5, 0), 'n4': (2, 5, 0), 'm2': (2, 0), 'g1': (5, 0), 'o2': (0,), 'n1': (1,), 'q5': (1, 3), 'm0': (1, 4), 'v': (5, 1, 3, 4), 's0': (1, 4), 'g2': (1,), 'p': (1,), 'c2': (2,), 'q2': (2,), 'g0': (2, 3), 'o1': (2, 5, 4), 'm1': (3,), 'o0': (3,), 'o3': (3,), 'l4': (3,), 'm4': (4,), 'f0': (4,), 'c5': (5,)}


def chunk_rows(z, c):
    return min(z.chunk, z.plane - (c % 2) * z.chunk)


def row_parts(z, c, step=48):
    rows = chunk_rows(z, c)
    return [(start, min(step, rows - start)) for start in range(0, rows, step)]


def place(e):
    z = e.z
    sp, wa = lax.axis_index("sp"), lax.axis_index("wa")
    e.sp, e.wa = sp, wa
    e.core, e.y = lax.rem(wa, 2), lax.div(wa, 2)
    e.sibling = (sp, wa + 1 - 2 * e.core)
    e.sp_peers = [(lax.rem(sp + i, z.n_sp), wa) for i in range(1, z.n_sp)]
    e.y_peers = [(sp, lax.rem(wa + 2 * j, z.n_wa)) for j in range(1, z.n_y)]
    e.wa_peers = [(sp, lax.rem(wa + j, z.n_wa)) for j in range(1, z.n_wa)]


def greet(e):
    barrier = pltpu.get_barrier_semaphore()
    for peer in e.sp_peers + e.wa_peers:
        pl.semaphore_signal(barrier, inc=1, device_id=peer, device_id_type=MESH)


def greeted(e):
    barrier = pltpu.get_barrier_semaphore()
    pl.semaphore_wait(barrier, len(e.sp_peers) + len(e.wa_peers))


class Copy:
    def __init__(self, copy):
        self.copy, self.received, self.sent = copy, False, False

    def wait_recv(self):
        if not self.received:
            self.copy.wait_recv()
        self.received = True

    def wait_send(self):
        if not self.sent:
            self.copy.wait_send()
        self.sent = True


class Arrival:
    def __init__(self, e, source, target, send, recv, peer):
        self.copy = pltpu.make_async_remote_copy(
            src_ref=source, dst_ref=target, send_sem=send, recv_sem=recv,
            device_id=peer, device_id_type=MESH,
        )
        self.copy.start()
        self.received = False
        e.copies.append(self)

    def wait_recv(self):
        if not self.received:
            self.copy.wait_recv()
        self.received = True

    def wait_send(self):
        pass


class Group:
    def __init__(self, e, sent, landed, send, recv):
        self.ends = {"recv": (landed, recv), "send": (sent, send)}
        e.copies.append(self)

    def wait(self, end):
        if end in self.ends:
            ref, sem = self.ends.pop(end)
            pltpu.make_async_copy(ref, ref, sem).wait()

    def wait_recv(self):
        self.wait("recv")

    def wait_send(self):
        self.wait("send")


def start_remote(source, target, send, recv, peer):
    pltpu.make_async_remote_copy(
        src_ref=source, dst_ref=target, send_sem=send, recv_sem=recv,
        device_id=peer, device_id_type=MESH,
    ).start()


def remote(e, source, target, send, recv, peer):
    copy = pltpu.make_async_remote_copy(
        src_ref=source, dst_ref=target, send_sem=send, recv_sem=recv,
        device_id=peer, device_id_type=MESH,
    )
    copy.start()
    e.copies.append(Copy(copy))
    return e.copies[-1]


def arrive(copies):
    for copy in copies:
        copy.wait_recv()


def finish(copies):
    for copy in copies:
        copy.wait_send()


def line(ref):
    return ref[...].reshape(1, -1)


def local_copy(e, source, target, sem):
    copy = pltpu.make_async_copy(source, target, sem)
    copy.start()
    return copy


def mean(values):
    return jnp.mean(values, -1, keepdims=True)


def total(values):
    return jnp.sum(values, 0, keepdims=True)


def lane_slice(e, half):
    return pl.ds(half * e.z.lanes, e.z.lanes)


def clear_padding(e, buffer):
    z = e.z
    start = chunk_rows(z, 1) // 16 * 16
    for c in range(1, z.chunks, 2):
        if start < z.chunk:
            buffer[c, start:] = jnp.zeros_like(buffer[c, start:])


def field_rows(e, source, c, start, size):
    z = e.z
    first = ((c % 2) * z.chunk + start) // z.fields
    return source[c // 2, first : first + size // z.fields].reshape(size, z.channels)


def others(e):
    return pl.ds(0, e.z.n_sp - 1)


def send_plane(e, tag, p, together):
    z = e.z
    slots, landed = getattr(e, "slots_" + tag), getattr(e, "landed_" + tag)
    at = 0 if together else p
    send, recv = getattr(e, "send_" + tag).at[at], getattr(e, "recv_" + tag).at[at]
    for peer in e.sp_peers:
        start_remote(slots.at[peer[0], p], landed.at[e.sp, p], send, recv, peer)
    landed[e.sp, p] = slots[e.sp, p]
    rest = others(e)
    if not together:
        return Group(e, slots.at[rest, p], landed.at[rest, p], send, recv)
    if p + 1 < z.planes:
        return None
    return Group(e, slots.at[rest], landed.at[rest], send, recv)


def columns_to_slots(e, table, tag, p):
    z = e.z
    source = e.xn[2 * p : 2 * p + 2].reshape(z.pitch, z.channels)
    columns = dot(table, source).astype(narrow)
    moved = dot(e.slot_rows[0], columns[:, : z.lanes]) + dot(e.slot_rows[1], columns[:, z.lanes :])
    moved = moved.astype(narrow)
    slots = getattr(e, "slots_" + tag)
    for d in range(z.n_sp):
        slots[d, p] = moved[d * z.plane_slot : (d + 1) * z.plane_slot]
    return send_plane(e, tag, p, True)


def mode_rows(e, landed):
    z = e.z
    rows = landed[...].astype(wide)
    return rows.reshape(z.n_sp * z.planes * z.plane_slot, z.lanes).astype(narrow)


def modes_from_slots(e, rows, table):
    z = e.z
    real = dot(table[: z.count], rows)
    imag = dot(table[z.count :], rows)
    return jnp.concatenate([real, imag], 1)


def modes_to_slots(e, values, tag):
    z = e.z
    moved = jnp.zeros((z.n_sp * z.planes * z.plane_slot, z.lanes), wide)
    for half, value in enumerate(values):
        stacked = jnp.concatenate([value[:, : z.lanes], value[:, z.lanes :]], 0)
        moved = moved + dot(e.lat_cols[half], stacked)
    moved = moved.astype(narrow)
    slots = getattr(e, "slots_" + tag)
    for d in range(z.n_sp):
        for p in range(z.planes):
            at = (d * z.planes + p) * z.plane_slot
            slots[d, p] = moved[at : at + z.plane_slot]
    return [send_plane(e, tag, p, False) for p in range(z.planes)]


class Gather:
    def __init__(self, e, gathered, tag):
        self.e, self.gathered = e, gathered
        self.sems = [
            getattr(e, name + tag) for name in ("send_y", "recv_y", "send_core", "recv_core")
        ]
        self.y, self.core = {}, {}
        send_y, _, send_core, _ = self.sems
        if e.y_peers:
            e.sends.append((gathered.at[:, pl.ds(0, e.z.n_y - 1)], send_y.at[0, 0]))
        e.sends.append((gathered.at[:, pl.ds(0, e.z.n_y)], send_core.at[0, 0]))

    def start(self, group, landed, p):
        e, z = self.e, self.e.z
        send_y, recv_y, send_core, recv_core = self.sems
        group.wait_recv()
        rows = landed[:, p].astype(wide).reshape(z.n_sp * z.plane_slot, z.lanes).astype(narrow)
        for half in range(halves):
            ordered = dot(e.slot_cols[half], rows).astype(narrow)
            self.gathered[p, e.wa, :, lane_slice(e, half)] = ordered
        own = self.gathered.at[p, e.wa]
        self.y[p] = [
            Arrival(e, own, own, send_y.at[0, 0], recv_y.at[p, j], peer)
            for j, peer in enumerate(e.y_peers)
        ]
        self.core[p] = [
            Arrival(e, own, own, send_core.at[0, 0], recv_core.at[p, 0], e.sibling)
        ]

    def forward(self, p):
        e, z = self.e, self.e.z
        send_y, recv_y, send_core, recv_core = self.sems
        for j, copy in enumerate(self.y[p]):
            copy.wait_recv()
            slab = self.gathered.at[p, lax.rem(e.wa + z.n_wa - 2 * (j + 1), z.n_wa)]
            sems = send_core.at[0, 0], recv_core.at[p, j + 1]
            self.core[p].append(Arrival(e, slab, slab, *sems, e.sibling))

    def rows(self, table, p):
        z = self.e.z
        arrive(self.core[p])
        return dot(table, self.gathered[p].reshape(z.n_wa * z.group, z.channels))


def pack_weights(e):
    z = e.z
    for i in range(z.own_blocks):
        at = e.wa * z.own_blocks + i
        e.packed[at, : 2 * z.block] = e.w1[i]
        e.packed[at, 2 * z.block : 4 * z.block] = e.w2[i]
        line = lax.broadcasted_iota(jnp.int32, (16, z.block), 0)
        bias = jnp.zeros((16, z.block), wide)
        for k in range(2):
            bias = jnp.where(line == k, e.b1[i, k : k + 1].astype(wide), bias)
            bias = jnp.where(line == 2 + k, e.b2[i, k : k + 1].astype(wide), bias)
        e.packed[at, 4 * z.block : 4 * z.block + 16] = bias.astype(narrow)


def own_weights(e, wa):
    z = e.z
    return e.packed.at[pl.ds(wa * z.own_blocks, z.own_blocks)]


def send_weights(e):
    own = own_weights(e, e.wa)
    peers = [e.sibling] + e.y_peers
    return [
        remote(e, own, own, e.send_w.at[j], e.recv_w.at[j], peer) for j, peer in enumerate(peers)
    ]


def forward_weights(e, copies):
    z = e.z
    arrive(copies[1:])
    more = []
    for j in range(1, z.n_y):
        slab = own_weights(e, lax.rem(e.wa + z.n_wa - 2 * j, z.n_wa))
        at = z.n_y + j - 1
        more.append(remote(e, slab, slab, e.send_w.at[at], e.recv_w.at[at], e.sibling))
    return copies + more


def spread(z, index):
    row = lax.broadcasted_iota(jnp.int32, (z.block, z.lanes), 0)
    lane = lax.broadcasted_iota(jnp.int32, (z.block, z.lanes), 1)
    return jnp.where(lane == row + index * z.block, 1.0, 0.0).astype(narrow)


def build_weights(e):
    z = e.z
    n, lanes = z.block, z.lanes
    for half in range(halves):
        bias = jnp.zeros((16, lanes), wide)
        for i in range(z.half_blocks):
            source = e.packed[half * z.half_blocks + i, : 4 * n + 16]
            placed = dot(source, spread(z, i))
            bias = bias + placed[4 * n :]
            for k, target in ((0, e.big1), (1, e.big2)):
                real = placed[2 * k * n : (2 * k + 1) * n]
                imag = placed[(2 * k + 1) * n : (2 * k + 2) * n]
                up, down = pl.ds(i * n, n), pl.ds(lanes + i * n, n)
                target[half, up, :lanes] = real.astype(narrow)
                target[half, up, lanes:] = imag.astype(narrow)
                target[half, down, :lanes] = (-imag).astype(narrow)
                target[half, down, lanes:] = real.astype(narrow)
        e.bias[half] = bias


def modes_forward(e, rows, half):
    z = e.z
    spec = modes_from_slots(e, rows, e.lat[half]).astype(narrow)
    e.spec[half] = spec
    bias = e.bias[half]
    bias1 = jnp.concatenate([bias[0:1], bias[1:2]], 1)
    bias2 = jnp.concatenate([bias[2:3], bias[3:4]], 1)
    hid, slope = gelu_with_slope(dot(spec, e.big1[half]) + bias1)
    e.slope1[half] = slope
    hid = hid.astype(narrow)
    e.hid[half] = hid
    two = dot(hid, e.big2[half]) + bias2
    bent = jnp.tanh(two * (1.0 / threshold))
    e.slope2[half] = bent * bent
    return (two - threshold * bent).astype(narrow)


def modes_backward(e, rows, half):
    z = e.z
    grad_two = (modes_from_slots(e, rows, e.lat[half]) * e.slope2[half]).astype(narrow)
    e.grad_two[half] = grad_two
    grad_hid = dot_right_transposed(grad_two, e.big2[half])
    grad_one = (grad_hid * e.slope1[half]).astype(narrow)
    e.grad_one[half] = grad_one
    return dot_right_transposed(grad_one, e.big1[half]).astype(narrow)


def outer_parts(z, left, right):
    lanes = z.lanes
    product = dot_left_transposed(left, right)
    real = product[:lanes, :lanes] + product[lanes:, lanes:]
    imag = product[:lanes, lanes:] - product[lanes:, :lanes]
    return real.astype(narrow), imag.astype(narrow)


def spectral_grads(e, half):
    z = e.z
    n, lanes = z.block, z.lanes
    real1, imag1 = outer_parts(z, e.spec[half], e.grad_one[half])
    real2, imag2 = outer_parts(z, e.hid[half], e.grad_two[half])
    bias1 = jnp.sum(e.grad_one[half].astype(wide), 0, keepdims=True)
    bias2 = jnp.sum(e.grad_two[half].astype(wide), 0, keepdims=True)
    line = lax.broadcasted_iota(jnp.int32, (16, lanes), 0)
    bias = jnp.zeros((16, lanes), wide)
    for k, row in enumerate((bias1[:, :lanes], bias1[:, lanes:], bias2[:, :lanes], bias2[:, lanes:])):
        bias = jnp.where(line == k, row, bias)
    bias = bias.astype(narrow)
    for i in range(z.half_blocks):
        at = half * z.half_blocks + i
        owner = at // z.own_blocks
        target = e.grad_pack.at[owner // 2, owner % 2, at % z.own_blocks]
        parts = [value[i * n : (i + 1) * n] for value in (real1, imag1, real2, imag2)]
        stacked = jnp.concatenate(parts + [bias], 0)
        target[: 4 * n + 16] = dot_right_transposed(stacked, spread(z, i)).astype(narrow)
        if z.pack > 4 * n + 16:
            target[4 * n + 16 :] = jnp.zeros((z.pack - 4 * n - 16, n), narrow)


class WaSum:
    def __init__(self, e, name, partial):
        self.e, self.partial = e, partial
        for part in ("recv_core", "slots_y", "done"):
            setattr(self, part, getattr(e, name + "_" + part))
        self.sems = {
            part: getattr(e, name + "_" + part)
            for part in ("ss_core", "rs_core", "ss_y", "rs_y", "ss_done", "rs_done")
        }
        self.core, self.y, self.last = {}, {}, {}
        if e.y_peers:
            e.sends.append((self.slots_y.at[:, pl.ds(0, e.z.n_y - 1)], self.sems["ss_y"].at[0]))

    def own(self):
        part = self.e.z.part
        return pl.ds(pl.multiple_of(self.e.core * part, 16), part)

    def other(self):
        part = self.e.z.part
        return pl.ds(pl.multiple_of((1 - self.e.core) * part, 16), part)

    def start(self, c, values):
        e, s = self.e, self.sems
        self.partial[c] = values.astype(narrow)
        self.core[c] = remote(
            e,
            self.partial.at[c, self.other()], self.recv_core.at[c],
            s["ss_core"].at[c], s["rs_core"].at[c], e.sibling,
        )

    def middle(self, c):
        e, s = self.e, self.sems
        self.core[c].wait_recv()
        both = self.partial[c, self.own()].astype(wide) + self.recv_core[c].astype(wide)
        self.slots_y[c, e.y] = both.astype(narrow)
        slot = self.slots_y.at[c, e.y]
        self.y[c] = [
            Arrival(e, slot, slot, s["ss_y"].at[0], s["rs_y"].at[c, j], peer)
            for j, peer in enumerate(e.y_peers)
        ]

    def end(self, c):
        e, s = self.e, self.sems
        arrive(self.y[c])
        value = self.slots_y[c, 0].astype(wide)
        for k in range(1, e.z.n_y):
            value = value + self.slots_y[c, k].astype(wide)
        self.done[c, self.own()] = value.astype(narrow)
        rows = self.done.at[c, self.own()]
        self.last[c] = remote(e, rows, rows, s["ss_done"].at[c], s["rs_done"].at[c], e.sibling)

    def value(self, c):
        self.last[c].wait_recv()


def wa_sum_scratch(s, z, name):
    s.vmem(name + "_recv_core", (z.chunks, z.part, z.channels))
    s.vmem(name + "_slots_y", (z.chunks, z.n_y, z.part, z.channels))
    s.vmem(name + "_done", (z.chunks, z.chunk, z.channels))
    for part in ("ss_core", "rs_core", "ss_done", "rs_done"):
        s.dma(name + "_" + part, (z.chunks,))
    s.dma(name + "_ss_y", (1,))
    s.dma(name + "_rs_y", (z.chunks, max(z.n_y - 1, 1)))


def cube_grouped(rows, n_sp):
    levels = cube_levels(rows, n_sp)
    sent = 2 * sum(size for _, _, size in levels)
    return all(halve for _, halve, _ in levels) and sent <= cuts * rows


def cube_levels(rows, n_sp, swap=False):
    bits = [2**k for k in range(n_sp.bit_length() - 1)]
    if swap:
        bits[:2] = bits[1::-1]
    levels = []
    for bit in bits:
        halve = rows % 32 == 0
        rows = rows // 2 if halve else rows
        levels.append((bit, halve, rows))
    return levels


class CubeSum:
    def __init__(self, e, block, landed, out, send, recv, chunk):
        self.e, self.block, self.landed, self.out = e, block, landed, out
        self.send, self.recv, self.chunk = send, recv, chunk
        self.rows = block.shape[0]
        self.levels = cube_levels(self.rows, e.z.n_sp, chunk in SWAPPED)
        self.start, self.size = 0, self.rows
        self.step, self.copies, self.spans = 0, [], []
        self.sent = 2 * sum(size for _, _, size in self.levels)
        self.whole = e.total1 if chunk < cuts else e.total2
        self.grouped = cube_grouped(self.rows, e.z.n_sp)
        if self.grouped:
            ref = self.whole.at[pl.ds(0, self.sent)]
            e.sends.append((ref, send.at[chunk, 0]))
        self.steps = self.begin()

    def peer(self, bit):
        e = self.e
        mine = lax.rem(lax.div(e.sp, bit), 2)
        return mine, (e.sp + bit - 2 * bit * mine, e.wa)

    def rows_at(self, start, size):
        return pl.ds(pl.multiple_of(start, 16), size)

    def post(self, source, target, peer):
        k = self.step
        self.step += 1
        recv = self.recv.at[self.chunk, k]
        if self.grouped:
            copy = Arrival(self.e, source, target, self.send.at[self.chunk, 0], recv, peer)
        else:
            copy = remote(self.e, source, target, self.send.at[self.chunk, k], recv, peer)
        self.copies.append(copy)
        return copy

    def begin(self):
        offset = 0
        for bit, halve, size in self.levels:
            mine, peer = self.peer(bit)
            self.spans.append((bit, halve, self.start, self.size))
            if halve:
                keep = self.start + mine * size
                give = self.start + (1 - mine) * size
            else:
                keep = give = self.start
            target = self.landed.at[offset : offset + size]
            copy = self.post(self.block.at[self.rows_at(give, size)], target, peer)
            yield
            copy.wait_recv()
            own = self.rows_at(keep, size)
            value = self.block[own].astype(wide) + target[...].astype(wide)
            if not halve:
                copy.wait_send()
            self.block[own] = value.astype(narrow)
            self.start, self.size = keep, size
            offset += size
        own = self.rows_at(self.start, self.size)
        self.out[own] = self.block[own]
        for bit, halve, start, size in reversed(self.spans):
            if halve:
                mine, peer = self.peer(bit)
                rows = self.out.at[self.rows_at(self.start, self.size)]
                copy = self.post(rows, rows, peer)
                yield
                copy.wait_recv()
            self.start, self.size = start, size

    def advance(self):
        return next(self.steps, None)


def cube_landed_rows(rows, n_sp):
    return sum(size for _, _, size in cube_levels(rows, n_sp))


def exchange_small(e, own, landed, send, recv):
    landed[e.sp] = own
    return spread_slot(e, landed, send, recv)


def spread_slot(e, landed, send, recv):
    slot = landed.at[e.sp]
    for peer in e.sp_peers:
        start_remote(slot, slot, send.at[0], recv.at[0], peer)
    rest = others(e)
    return Group(e, landed.at[rest], landed.at[rest], send.at[0], recv.at[0])


def sum_small(e, landed, group):
    group.wait_recv()
    value = landed[0]
    for k in range(1, e.z.n_sp):
        value = value + landed[k]
    return value


def place_rows(rows, width):
    line = lax.broadcasted_iota(jnp.int32, (8, width), 0)
    result = jnp.zeros((8, width), wide)
    for k, row in rows:
        if row.shape[1] < width:
            row = jnp.concatenate([row, jnp.zeros((1, width - row.shape[1]), wide)], 1)
        result = jnp.where(line == k, row, result)
    return result


def spec_sum_start(e):
    z = e.z
    return [
        remote(
            e,
            e.grad_pack.at[:, 1 - e.core], e.pack_core, e.ss_pack.at[0], e.rs_pack.at[0], e.sibling
        )
    ]


def spec_sum_middle(e, copies):
    z = e.z
    arrive(copies)
    for k in range(z.n_y):
        both = e.grad_pack[k, e.core].astype(wide) + e.pack_core[k].astype(wide)
        e.pack_send[k] = both.astype(narrow)
    new = [
        remote(
            e,
            e.pack_send.at[lax.rem(e.y + j + 1, z.n_y)], e.pack_y.at[e.y],
            e.ss_pack.at[1 + j], e.rs_pack.at[1 + j], peer,
        )
        for j, peer in enumerate(e.y_peers)
    ]
    e.pack_y[e.y] = e.pack_send[e.y]
    return new


def spec_sum_scatter(e, copies):
    z = e.z
    arrive(copies)
    value = e.pack_y[0].astype(wide)
    for k in range(1, z.n_y):
        value = value + e.pack_y[k].astype(wide)
    e.pack_sum[...] = value.reshape(z.n_sp, z.pack_share, z.block).astype(narrow)
    e.pack_landed[e.sp] = e.pack_sum[e.sp]
    for peer in e.sp_peers:
        start_remote(
            e.pack_sum.at[peer[0]], e.pack_landed.at[e.sp], e.ss_share.at[0], e.rs_share.at[0], peer
        )
    rest = others(e)
    return [
        Group(e, e.pack_sum.at[rest], e.pack_landed.at[rest], e.ss_share.at[0], e.rs_share.at[0])
    ]


def spec_sum_gather(e, copies):
    z = e.z
    arrive(copies)
    value = e.pack_landed[0].astype(wide)
    for k in range(1, z.n_sp):
        value = value + e.pack_landed[k].astype(wide)
    e.pack_out[e.sp] = value.astype(narrow)
    return [spread_slot(e, e.pack_out, e.ss_whole, e.rs_whole)]


def first_norm(e, c):
    gain, shift = line(e.gain1), line(e.shift1)
    for start, size in row_parts(e.z, c):
        values = field_rows(e, e.xs, c, start, size).astype(wide)
        center = mean(values)
        centred = values - center
        inv_std = lax.rsqrt(mean(centred * centred) + 1e-05)
        rows = pl.ds(start, size)
        e.xn[c, rows] = (centred * inv_std * gain + shift).astype(narrow)
        e.stats[c, rows, 0:1] = center
        e.stats[c, rows, 1:2] = inv_std


def second_norm(e, c):
    gain, shift = line(e.gain2), line(e.shift2)
    for start, size in row_parts(e.z, c):
        rows = pl.ds(start, size)
        values = e.mixed[c, rows]
        center = mean(values)
        centred = values - center
        inv_std = lax.rsqrt(mean(centred * centred) + 1e-05)
        e.xn2[c, rows] = (centred * inv_std * gain + shift).astype(narrow)
        e.stats[c, rows, 2:3] = center
        e.stats[c, rows, 3:4] = inv_std


def second_norm_backward(e, c, gain_grad, shift_grad):
    gain = line(e.gain2)
    for start, size in row_parts(e.z, c):
        rows = pl.ds(start, size)
        grad = e.grads_done[c, rows].astype(wide)
        inv_std = e.stats[c, rows, 3:4]
        hat = (e.mixed[c, rows] - e.stats[c, rows, 2:3]) * inv_std
        gain_grad = gain_grad + total(grad * hat)
        shift_grad = shift_grad + total(grad)
        scaled = grad * gain
        back = inv_std * (scaled - mean(scaled) - hat * mean(scaled * hat))
        e.xn[c, rows] = (e.gp[c, rows].astype(wide) + back).astype(narrow)
    return gain_grad, shift_grad


def first_norm_sums(e, c, gain_grad, shift_grad):
    for start, size in row_parts(e.z, c):
        rows = pl.ds(start, size)
        grad = e.xn2[c, rows].astype(wide)
        values = field_rows(e, e.xs, c, start, size).astype(wide)
        hat = (values - e.stats[c, rows, 0:1]) * e.stats[c, rows, 1:2]
        gain_grad = gain_grad + total(grad * hat)
        shift_grad = shift_grad + total(grad)
    return gain_grad, shift_grad


def first_norm_backward(e, c):
    gain = line(e.gain1)
    for start, size in row_parts(e.z, c):
        rows = pl.ds(start, size)
        grad = e.xn2[c, rows].astype(wide)
        inv_std = e.stats[c, rows, 1:2]
        values = field_rows(e, e.xs, c, start, size).astype(wide)
        hat = (values - e.stats[c, rows, 0:1]) * inv_std
        scaled = grad * gain
        back = inv_std * (scaled - mean(scaled) - hat * mean(scaled * hat))
        e.xn[c, rows] = (e.xn[c, rows].astype(wide) + back).astype(narrow)


def whole_body(e):
    z = e.z
    chunks = range(z.chunks)
    x_loads = [
        local_copy(e, e.hbm_x.at[p], e.xs.at[p], e.load_x.at[p]) for p in range(z.planes)
    ]
    loads = {}
    for index, name in enumerate(z.loaded):
        source = getattr(e, "hbm_" + name)
        if name == "long_rows":
            source = source.at[:, e.wa]
        elif name == "gs":
            source = source.at[pl.ds(0, 1)]
        loads[name] = local_copy(e, source, getattr(e, name), e.load.at[index])

    def need(*names):
        for name in names:
            loads.pop(name).wait()

    greet(e)
    clear_padding(e, e.xn)
    clear_padding(e, e.xn2)
    clear_padding(e, e.gp)
    need("w1", "b1", "w2", "b2")
    pack_weights(e)
    need("gain1", "shift1", "long_rows", "slot_rows")
    table = e.long_rows[0]
    for p in range(z.planes):
        x_loads[p].wait()
        first_norm(e, 2 * p)
        first_norm(e, 2 * p + 1)
        if p == 0:
            greeted(e)
            weights = send_weights(e)
        first = columns_to_slots(e, table, "a", p)

    need("gs")
    bias2_grad = jnp.zeros((1, z.channels), wide)
    for c in chunks:
        for start, size in row_parts(z, c):
            values = field_rows(e, e.gs, c % 2, start, size)
            e.gp[c, start : start + size] = values
            bias2_grad = bias2_grad + total(values.astype(wide))
        if c % 2 == 1 and c // 2 + 1 < z.planes:
            source = e.hbm_gs.at[pl.ds(c // 2 + 1, 1)]
            local_copy(e, source, e.gs, e.load.at[z.loaded.index("gs")]).wait()
    need("fc2")
    for p in range(z.planes):
        rows = e.gp[2 * p : 2 * p + 2].reshape(z.pitch, z.channels)
        grad_act = dot_right_transposed(rows, e.fc2[...]).astype(narrow)
        e.gh[2 * p : 2 * p + 2] = grad_act.reshape(2, z.chunk, z.hidden)
    weights = forward_weights(e, weights)
    arrive(weights)
    build_weights(e)
    need("lat", "lat_cols")
    first.wait_recv()
    rows = mode_rows(e, e.landed_a)
    second = modes_to_slots(e, [modes_forward(e, rows, half) for half in range(halves)], "b")
    need("slot_cols", "long_out", "gain2", "shift2", "fc1", "fc1_bias", "fc2_bias")
    gather = Gather(e, e.gathered, "")
    gather.start(second[0], e.landed_b, 0)
    gather.start(second[1], e.landed_b, 1)
    gather.forward(0)
    for p in range(2, z.planes):
        gather.start(second[p], e.landed_b, p)
    finish(second)

    grads = WaSum(e, "grads", e.xn)
    bias1 = line(e.fc1_bias).astype(wide)
    bias1_grad = jnp.zeros((1, z.hidden), wide)
    for p in range(z.planes):
        filtered = gather.rows(e.long_out[1], p).astype(narrow).astype(wide)
        pair = (2 * p, 2 * p + 1)
        for c in pair:
            size = chunk_rows(z, c)
            at = (c % 2) * z.chunk
            values = field_rows(e, e.xs, c, 0, size).astype(wide)
            e.mixed[c, pl.ds(0, size)] = values + filtered[at : at + size]
            second_norm(e, c)
        if p >= 1:
            grads.middle(2 * p - 2)
            grads.middle(2 * p - 1)
        both = slice(2 * p, 2 * p + 2)
        rows = e.xn2[both].reshape(z.pitch, z.channels)
        hidden, slope = gelu_with_slope(dot(rows, e.fc1[...]) + bias1)
        e.act[both] = hidden.astype(narrow).reshape(2, z.chunk, z.hidden)
        grad_hidden = e.gh[both].reshape(z.pitch, z.hidden).astype(wide) * slope
        grad_hidden = grad_hidden.astype(narrow)
        e.gh[both] = grad_hidden.reshape(2, z.chunk, z.hidden)
        if p + 1 < z.planes:
            gather.forward(p + 1)
        part = dot_right_transposed(grad_hidden, e.fc1[...])
        for c in pair:
            grads.start(c, part[(c % 2) * z.chunk : (c % 2 + 1) * z.chunk])
        bias1_grad = bias1_grad + total(grad_hidden.astype(wide))
    all_rows = z.chunks * z.chunk
    sources = (
        (e.xn2, e.gh, e.sum1, e.landed1, e.total1, z.channels),
        (e.act, e.gp, e.sum2, e.landed2, e.total2, z.hidden),
    )
    cubes = []

    def tick(name):
        for index in SCHEDULE.get(name, ()):
            cubes[index].advance()

    for index, (left, right, block, landed, out, rows) in enumerate(sources):
        size = rows // cuts
        for k in range(cuts):
            part = left[:, :, k * size : (k + 1) * size].reshape(all_rows, size)
            value = dot_left_transposed(part, right[...].reshape(all_rows, right.shape[-1]))
            block[k] = value.astype(narrow)
            cube = CubeSum(
                e, block.at[k], landed.at[k], out.at[pl.ds(k * size, size)],
                e.send_cube, e.recv_cube, cuts * index + k,
            )
            cubes.append(cube)
            if len(cubes) == 1:
                grads.middle(z.chunks - 2)
                grads.middle(z.chunks - 1)
            tick("c%d" % (cuts * index + k))
    gain2_grad = jnp.zeros((1, z.channels), wide)
    shift2_grad = jnp.zeros((1, z.channels), wide)
    table = e.long_rows[1]
    branch = WaSum(e, "branch", e.xn2)
    for c in range(z.chunks + 1):
        if c < z.chunks:
            tick("q%d" % c)
            grads.end(c)
        if c >= 1:
            last = c - 1
            grads.value(last)
            finish([grads.core[last]])
            gain2_grad, shift2_grad = second_norm_backward(e, last, gain2_grad, shift2_grad)
            if last % 2 == 1:
                third = columns_to_slots(e, table, "c", last // 2)
                rows = e.act[last - 1 : last + 1].reshape(z.pitch, z.hidden)
                part = dot(rows, e.fc2[...])
                branch.start(last - 1, part[: z.chunk])
                branch.start(last, part[z.chunk :])
            tick("n%d" % last)

    rows = [(0, bias1_grad), (1, bias2_grad), (2, gain2_grad), (3, shift2_grad)]
    small_one = exchange_small(
        e, place_rows(rows, z.small), e.small_one, e.send_one, e.recv_one
    )
    early, late = chunks[:EARLY], chunks[EARLY:]
    for c in early:
        branch.middle(c)
        tick("m%d" % c)
    third.wait_recv()
    tick("v")
    rows = mode_rows(e, e.landed_c)
    fourth = modes_to_slots(e, [modes_backward(e, rows, half) for half in range(halves)], "d")
    tick("w0")
    for half in range(halves):
        spectral_grads(e, half)
        tick("s%d" % half)
    packs = [spec_sum_start(e)]
    writes = []
    bias = e.fc2_bias[...].reshape(1, -1).astype(wide)

    def write_output(c):
        branch.value(c)
        finish([branch.last[c]])
        for start, size in row_parts(z, c):
            rows = pl.ds(start, size)
            value = e.mixed[c, rows] + (e.branch_done[c, rows].astype(wide) + bias)
            e.branch_done[c, rows] = value.astype(narrow)
        local_copy(e, e.branch_done.at[c], e.hbm_output.at[c], e.write_sems.at[0])

    packs.append(spec_sum_middle(e, packs[-1]))
    gather = Gather(e, e.gathered2, "2")
    for p in range(z.planes):
        gather.start(fourth[p], e.landed_d, p)
        if p + 1 == z.planes:
            packs.append(spec_sum_scatter(e, packs[-1]))
        tick("g%d" % p)
    for c in late:
        branch.middle(c)
        tick("m%d" % c)
    for c in early:
        branch.end(c)
    for c in early:
        write_output(c)
        tick("o%d" % c)
    finish(branch.core.values())
    packs.append(spec_sum_gather(e, packs[-1]))
    gain1_grad = jnp.zeros((1, z.channels), wide)
    shift1_grad = jnp.zeros((1, z.channels), wide)
    for p in range(z.planes):
        gather.forward(p)
        grad = gather.rows(e.long_out[0], p).astype(narrow)
        e.xn2[2 * p : 2 * p + 2] = grad.reshape(2, z.chunk, z.channels)
        for c in (2 * p, 2 * p + 1):
            gain1_grad, shift1_grad = first_norm_sums(e, c, gain1_grad, shift1_grad)
        if p + 1 == z.planes:
            small_two = exchange_small(
                e, place_rows([(0, gain1_grad), (1, shift1_grad)], z.small),
                e.small_two, e.send_two, e.recv_two,
            )
        for c in (2 * p, 2 * p + 1):
            first_norm_backward(e, c)
            local_copy(e, e.xn.at[c], e.hbm_fields_grad.at[c], e.write_sems.at[1])
        tick("f%d" % p)
    for c in late:
        branch.end(c)
    for c in late:
        write_output(c)
        tick("l%d" % c)
    tick("p")
    arrive(packs[-1])
    writes.append(local_copy(e, e.pack_out, e.hbm_pack, e.store.at[0]))
    e.small_out[0] = sum_small(e, e.small_one, small_one)
    e.small_out[1] = sum_small(e, e.small_two, small_two)
    writes.append(local_copy(e, e.small_out, e.hbm_small, e.store.at[1]))
    for _ in range(max(len(cube.levels) for cube in cubes) * 2):
        for cube in cubes:
            cube.advance()
    for index, cube in enumerate(cubes):
        cube.advance()
        target = e.hbm_fc1_grad if index < cuts else e.hbm_fc2_grad
        rows = cube.rows
        target = target.at[pl.ds((index % cuts) * rows, rows)]
        writes.append(local_copy(e, cube.out, target, e.store.at[2 + index]))
    arrive(e.copies)
    finish(e.copies)
    e.sends += [(e.branch_done, e.write_sems.at[0]), (e.xn, e.write_sems.at[1])]
    for ref, sem in e.sends:
        pltpu.make_async_copy(ref, ref, sem).wait()
    for write in writes:
        write.wait()


class Names:
    def __init__(self):
        self.names, self.shapes = [], []

    def add(self, name, shape):
        self.names.append(name)
        self.shapes.append(shape)

    def vmem(self, name, shape, dtype=narrow):
        self.add(name, pltpu.VMEM(shape, dtype))

    def dma(self, name, shape):
        self.add(name, pltpu.SemaphoreType.DMA(shape))


def scratch_of(z):
    s = Names()
    fields = (z.planes, z.width, z.fields, z.channels)
    rows = (z.chunks, z.chunk, z.channels)
    hidden = (z.chunks, z.chunk, z.hidden)
    s.vmem("xs", fields)
    lat_rows = z.n_sp * z.planes * z.plane_slot
    n = z.block
    for name, shape, dtype in (
        ("w1", (z.own_blocks, 2 * n, n), narrow), ("b1", (z.own_blocks, 2, n), narrow),
        ("w2", (z.own_blocks, 2 * n, n), narrow), ("b2", (z.own_blocks, 2, n), narrow),
        ("gain1", (z.channels,), wide), ("shift1", (z.channels,), wide),
        ("gain2", (z.channels,), wide), ("shift2", (z.channels,), wide),
        ("fc1", (z.channels, z.hidden), narrow), ("fc1_bias", (z.hidden,), narrow),
        ("fc2", (z.hidden, z.channels), narrow), ("fc2_bias", (z.channels,), narrow),
        ("gs", (1,) + fields[1:], narrow), ("long_rows", (2, z.group, z.pitch), narrow),
        ("slot_rows", (halves, z.n_sp * z.plane_slot, z.group), narrow),
        ("slot_cols", (halves, z.group, z.n_sp * z.plane_slot), narrow),
        ("lat", (halves, 2 * z.count, lat_rows), narrow),
        ("lat_cols", (halves, lat_rows, 2 * z.count), narrow),
        ("long_out", (2, z.pitch, z.n_wa * z.group), narrow),
    ):
        s.vmem(name, shape, dtype)
    s.dma("load_x", (z.planes,))
    s.dma("load", (len(z.loaded),))
    s.dma("store", (2 + 2 * cuts,))
    s.dma("write_sems", (2,))
    for name in ("xn", "gp", "xn2"):
        s.vmem(name, rows)
    s.vmem("act", hidden)
    s.vmem("gh", hidden)
    s.vmem("mixed", rows, wide)
    s.vmem("stats", (z.chunks, z.chunk, 4), wide)
    for name in ("slots_a", "slots_b", "slots_c", "slots_d", "landed_a", "landed_b", "landed_c", "landed_d"):
        s.vmem(name, (z.n_sp, z.planes, z.plane_slot, z.lanes))
    for tag in "abcd":
        s.dma("send_" + tag, (z.planes,))
        s.dma("recv_" + tag, (z.planes,))
    for tag in ("", "2"):
        s.vmem("gathered" + tag, (z.planes, z.n_wa, z.group, z.channels))
        s.dma("send_y" + tag, (1, 1))
        s.dma("send_core" + tag, (1, 1))
        s.dma("recv_y" + tag, (z.planes, max(z.n_y - 1, 1)))
        s.dma("recv_core" + tag, (z.planes, z.n_y))
    s.vmem("packed", (z.blocks, z.pack, z.block))
    s.vmem("bias", (halves, 16, z.lanes), wide)
    s.dma("send_w", (2 * z.n_y - 1,))
    s.dma("recv_w", (2 * z.n_y - 1,))
    both = (halves, z.count, 2 * z.lanes)
    for name in ("spec", "hid", "grad_one", "grad_two"):
        s.vmem(name, both)
    s.vmem("slope1", both, wide)
    s.vmem("slope2", both, wide)
    for name in ("big1", "big2"):
        s.vmem(name, (halves, 2 * z.lanes, 2 * z.lanes))
    s.vmem("grad_pack", (z.n_y, 2, z.own_blocks, z.pack, z.block))
    for name in ("pack_core", "pack_send", "pack_y"):
        s.vmem(name, (z.n_y, z.own_blocks, z.pack, z.block))
    s.vmem("pack_out", (z.n_sp, z.pack_share, z.block))
    s.vmem("small_out", (2, 8, z.small), wide)
    s.vmem("pack_sum", (z.n_sp, z.pack_share, z.block))
    s.vmem("pack_landed", (z.n_sp, z.pack_share, z.block))
    for name in ("ss_pack", "rs_pack"):
        s.dma(name, (z.n_y,))
    for name in ("ss_share", "rs_share", "ss_whole", "rs_whole"):
        s.dma(name, (1,))
    wa_sum_scratch(s, z, "grads")
    wa_sum_scratch(s, z, "branch")
    for tag, rows, lanes in (("1", z.channels, z.hidden), ("2", z.hidden, z.channels)):
        s.vmem("sum" + tag, (cuts, rows // cuts, lanes))
        s.vmem("total" + tag, (rows, lanes))
        s.vmem("landed" + tag, (cuts, cube_landed_rows(rows // cuts, z.n_sp), lanes))
    steps = 2 * len(cube_levels(z.channels, z.n_sp))
    grouped = all(cube_grouped(rows // cuts, z.n_sp) for rows in (z.channels, z.hidden))
    s.dma("send_cube", (2 * cuts, 1 if grouped else steps))
    s.dma("recv_cube", (2 * cuts, steps))
    for tag in ("one", "two"):
        s.vmem("small_" + tag, (z.n_sp, 8, z.small), wide)
        s.dma("send_" + tag, (1,))
        s.dma("recv_" + tag, (1,))
    return s


def call_kernel(body, z, inputs, outputs, scratch, collective):
    names = [name for name, _ in inputs] + [name for name, _, _ in outputs]

    def kernel(*refs):
        e = types.SimpleNamespace(z=z)
        for name, ref in zip(names + scratch.names, refs):
            setattr(e, name, ref)
        e.copies, e.sends = [], []
        place(e)
        body(e)

    def spec(name):
        return pl.BlockSpec(memory_space=pl.ANY if name.startswith("hbm_") else pltpu.VMEM)

    return pl.pallas_call(
        kernel,
        out_shape=[jax.ShapeDtypeStruct(shape, dtype) for _, shape, dtype in outputs],
        in_specs=[spec(name) for name, _ in inputs],
        out_specs=[spec(name) for name, _, _ in outputs],
        scratch_shapes=scratch.shapes,
        compiler_params=pltpu.CompilerParams(
            collective_id=collective,
            has_side_effects=collective is not None,
            vmem_limit_bytes=61 * 1024 * 1024,
        ),
    )(*[value for _, value in inputs])


def finish_body(e):
    z = e.z
    loads, writes = [], []
    pairs = [
        (source.at[c], target.at[c])
        for source, target in ((e.hbm_output, e.rows_output), (e.hbm_fields, e.rows_fields))
        for c in range(z.chunks)
    ]
    pairs += [
        (e.hbm_fc1, e.rows_fc1), (e.hbm_fc2, e.rows_fc2), (e.hbm_pack, e.pack), (e.hbm_small, e.small)
    ]
    for index, (source, target) in enumerate(pairs):
        loads.append(local_copy(e, source, target, e.load.at[index]))

    def write(source, target):
        writes.append(local_copy(e, source, target, e.store.at[len(writes)]))

    for index, (rows, wide_rows, target) in enumerate(
        (
            (e.rows_output, e.wide_output, e.hbm_output_out),
            (e.rows_fields, e.wide_fields, e.hbm_fields_out),
        )
    ):
        for c in range(z.chunks):
            loads[index * z.chunks + c].wait()
            for start, size in row_parts(z, c, 96):
                values = rows[c, start : start + size].astype(wide)
                first = ((c % 2) * z.chunk + start) // z.fields
                wide_rows[c // 2, first : first + size // z.fields] = values.reshape(
                    size // z.fields, z.fields, z.channels
                )
            if c % 2 == 1:
                write(wide_rows.at[c // 2], target.at[c // 2])
    for index, (rows, wide_rows, target) in enumerate(
        ((e.rows_fc1, e.wide_fc1, e.hbm_fc1_out), (e.rows_fc2, e.wide_fc2, e.hbm_fc2_out))
    ):
        loads[2 * z.chunks + index].wait()
        wide_rows[...] = rows[...].astype(wide)
        write(wide_rows, target)
    for load in loads[2 * z.chunks + 2 :]:
        load.wait()
    n = z.block
    e.w1[...] = e.pack[:, : 2 * n].astype(wide)
    e.w2[...] = e.pack[:, 2 * n : 4 * n].astype(wide)
    bias = e.pack[:, 4 * n : 4 * n + 16].astype(wide)
    e.b1[...] = bias[:, 0:2]
    e.b2[...] = bias[:, 2:4]
    small = e.small[...]
    e.gain1[...] = small[1, 0, : z.channels]
    e.shift1[...] = small[1, 1, : z.channels]
    e.gain2[...] = small[0, 2, : z.channels]
    e.shift2[...] = small[0, 3, : z.channels]
    e.fc1_bias[...] = small[0, 0, : z.hidden]
    e.fc2_bias[...] = small[0, 1, : z.channels]
    for name in z.small_names:
        write(getattr(e, name), getattr(e, "hbm_out_" + name))
    for copy in writes:
        copy.wait()


def finish_call(z, output, fields_grad, fc1, fc2, pack, small):
    channels, hidden, n = z.channels, z.hidden, z.block
    inputs = [
        ("hbm_output", output), ("hbm_fields", fields_grad), ("hbm_fc1", fc1), ("hbm_fc2", fc2),
        ("hbm_pack", pack.reshape(z.own_blocks, z.pack, n)), ("hbm_small", small),
    ]
    fields = (z.planes, z.width, z.fields, channels)
    smalls = {
        "gain1": (channels,), "shift1": (channels,),
        "w1": (z.own_blocks, 2 * n, n), "b1": (z.own_blocks, 2, n),
        "w2": (z.own_blocks, 2 * n, n), "b2": (z.own_blocks, 2, n),
        "gain2": (channels,), "shift2": (channels,),
        "fc1_bias": (hidden,), "fc2_bias": (channels,),
    }
    z.small_names = tuple(smalls)
    outputs = [("hbm_output_out", fields, wide), ("hbm_fields_out", fields, wide)]
    outputs += [("hbm_out_" + name, shape, wide) for name, shape in smalls.items()]
    outputs += [
        ("hbm_fc1_out", (channels, hidden), wide), ("hbm_fc2_out", (hidden, channels), wide),
    ]
    s = Names()
    s.vmem("rows_output", output.shape)
    s.vmem("rows_fields", fields_grad.shape)
    s.vmem("rows_fc1", fc1.shape)
    s.vmem("rows_fc2", fc2.shape)
    s.vmem("pack", (z.own_blocks, z.pack, n))
    s.vmem("small", small.shape, wide)
    s.vmem("wide_output", fields, wide)
    s.vmem("wide_fields", fields, wide)
    s.vmem("wide_fc1", fc1.shape, wide)
    s.vmem("wide_fc2", fc2.shape, wide)
    for name, shape in smalls.items():
        s.vmem(name, shape, wide)
    s.dma("load", (2 * z.chunks + 4,))
    s.dma("store", (2 * z.planes + 2 + len(smalls),))
    results = call_kernel(finish_body, z, inputs, outputs, s, None)
    named = dict(zip(smalls, results[2:-2]))
    return results[0], results[1], results[-2], results[-1], named


def local(
    fields_in,
    norm1_gain,
    norm1_shift,
    spec_w1,
    spec_b1,
    spec_w2,
    spec_b2,
    norm2_gain,
    norm2_shift,
    fc1_weight,
    fc1_bias,
    fc2_weight,
    fc2_bias,
    out_grad,
):
    fields, rows_here, width, channels = fields_in.shape
    n_sp, n_wa = lax.axis_size("sp"), lax.axis_size("wa")
    block, hidden = spec_w1.shape[2], fc1_weight.shape[1]
    z = plan(
        n_sp, n_wa, fields, rows_here, width, channels, channels // block, block, hidden
    )
    long_rows, long_out = longitude_tables(z)
    index, lat = plane_tables(z, slot_index(z), latitude_table(z))
    tables = [
        jnp.asarray(np.ascontiguousarray(table))
        for table in (
            long_rows, long_out, index, index.transpose(0, 2, 1), lat, lat.transpose(0, 2, 1),
        )
    ]
    own, n = z.own_blocks, block
    turned = lambda value: jnp.transpose(value, (1, 2, 0, 3))
    inputs = [
        ("hbm_x", turned(fields_in)), ("hbm_gs", turned(out_grad)),
        ("hbm_fc1", fc1_weight), ("hbm_fc2", fc2_weight),
        ("hbm_gain1", norm1_gain), ("hbm_shift1", norm1_shift),
        ("hbm_gain2", norm2_gain), ("hbm_shift2", norm2_shift),
        ("hbm_fc1_bias", fc1_bias), ("hbm_fc2_bias", fc2_bias),
        ("hbm_w1", spec_w1.reshape(own, 2 * n, n)), ("hbm_b1", spec_b1),
        ("hbm_w2", spec_w2.reshape(own, 2 * n, n)), ("hbm_b2", spec_b2),
    ]
    names = ("long_rows", "long_out", "slot_rows", "slot_cols", "lat", "lat_cols")
    inputs += [("hbm_" + name, table) for name, table in zip(names, tables)]
    flat = (z.chunks, z.chunk, channels)
    outputs = [
        ("hbm_output", flat, narrow), ("hbm_fields_grad", flat, narrow),
        ("hbm_fc1_grad", (channels, hidden), narrow), ("hbm_fc2_grad", (hidden, channels), narrow),
        ("hbm_pack", (z.n_sp, z.pack_share, n), narrow), ("hbm_small", (2, 8, z.small), wide),
    ]
    output, fields_grad, fc1, fc2, named = finish_call(
        z, *call_kernel(whole_body, z, inputs, outputs, scratch_of(z), 0)
    )
    back = lambda value: jnp.transpose(value, (2, 0, 1, 3))
    shaped = lambda value: value.reshape(own, 2, n, n)
    return (
        back(output), back(fields_grad), named["gain1"], named["shift1"],
        shaped(named["w1"]), named["b1"], shaped(named["w2"]), named["b2"],
        named["gain2"], named["shift2"], fc1, named["fc1_bias"], fc2, named["fc2_bias"],
    )


def solution(mesh):
    return jax.shard_map(
        local,
        mesh=mesh,
        in_specs=(
            P(None, "sp", None, None),
            P(),
            P(),
            P("wa", None, None, None),
            P("wa", None, None),
            P("wa", None, None, None),
            P("wa", None, None),
            P(),
            P(),
            P(None, "wa"),
            P("wa"),
            P("wa", None),
            P(),
            P(None, "sp", None, None),
        ),
        out_specs=(
            P(None, "sp", None, None),
            P(None, "sp", None, None),
            P(),
            P(),
            P("wa", None, None, None),
            P("wa", None, None),
            P("wa", None, None, None),
            P("wa", None, None),
            P(),
            P(),
            P(None, "wa"),
            P("wa"),
            P("wa", None),
            P(),
        ),
        check_vma=False,
    )
```
